32 devices in a mesh: dp: 16 (over z, y, x), mp: 2 (over core).
Axes of the slice: x: 2, y: 2, z: 4, core: 2. Of those that a mesh axis runs over, the one named last changes fastest.
Arguments:
- input_codes: int32 [2, 16, 800], P(None, 'dp'), may hold values from 0 to 4095
- target_codes: int32 [2, 16, 800], P(None, 'dp'), may hold values from 0 to 4095
- item_lengths: int32 [2, 16, 8], P(None, 'dp'), may hold values from 0 to 680, as said below
- item_labels: int32 [2, 16, 8], P(None, 'dp'), may hold values from 0 to 999
- code_table: float32 [4096, 1024], P('dp'), may hold values from -6 to 6
- class_table: float32 [1000, 1024], P(None, 'dp'), may hold values from -6 to 6
- adaln_weight: float32 [1024, 6144], P('dp'), may hold values from -0.1875 to 0.1875
- qkv_weight: float32 [3, 1024, 1024], P(None, 'dp', 'mp'), may hold values from -0.1875 to 0.1875
- proj_weight: float32 [1024, 1024], P('mp', 'dp'), may hold values from -1 to 1
- expand_weight: float32 [1024, 4096], P('dp', 'mp'), may hold values from -0.1875 to 0.1875
- contract_weight: float32 [4096, 1024], P('mp', 'dp'), may hold values from -0.09375 to 0.09375
- head_weight: float32 [1024, 4096], P('dp', 'mp')
- code_moment: float32 [4096, 1024], P('dp'), may hold values from -3.7252903e-09 to 3.7252903e-09
- class_moment: float32 [1000, 1024], P(None, 'dp'), may hold values from -1.1920929e-07 to 1.1920929e-07
- adaln_moment: float32 [1024, 6144], P('dp'), may hold values from -1.1920929e-07 to 1.1920929e-07
- qkv_moment: float32 [3, 1024, 1024], P(None, 'dp', 'mp'), may hold values from -1.1920929e-07 to 1.1920929e-07
- proj_moment: float32 [1024, 1024], P('mp', 'dp'), may hold values from -1.1920929e-07 to 1.1920929e-07
- expand_moment: float32 [1024, 4096], P('dp', 'mp'), may hold values from -1.1920929e-07 to 1.1920929e-07
- contract_moment: float32 [4096, 1024], P('mp', 'dp'), may hold values from -1.1920929e-07 to 1.1920929e-07
- head_moment: float32 [1024, 4096], P('dp', 'mp'), may hold values from -1.1920929e-07 to 1.1920929e-07
- code_square: float32 [4096, 1024], P('dp'), may hold values from 1.4672444e-18 to 5.8689776e-18
- class_square: float32 [1000, 1024], P(None, 'dp'), may hold values from 1.859513e-15 to 7.423911e-15
- adaln_square: float32 [1024, 6144], P('dp'), may hold values from 1.859513e-15 to 7.423911e-15
- qkv_square: float32 [3, 1024, 1024], P(None, 'dp', 'mp'), may hold values from 1.859513e-15 to 7.423911e-15
- proj_square: float32 [1024, 1024], P('mp', 'dp'), may hold values from 1.859513e-15 to 7.423911e-15
- expand_square: float32 [1024, 4096], P('dp', 'mp'), may hold values from 1.859513e-15 to 7.423911e-15
- contract_square: float32 [4096, 1024], P('mp', 'dp'), may hold values from 1.859513e-15 to 7.423911e-15
- head_square: float32 [1024, 4096], P('dp', 'mp'), may hold values from 1.859513e-15 to 7.423911e-15
Outputs:
- code_first: float32 [4096, 1024], P('dp')
- class_first: float32 [1000, 1024], P(None, 'dp')
- adaln_first: float32 [1024, 6144], P('dp')
- qkv_first: float32 [3, 1024, 1024], P(None, 'dp', 'mp')
- proj_first: float32 [1024, 1024], P('mp', 'dp')
- expand_first: float32 [1024, 4096], P('dp', 'mp')
- contract_first: float32 [4096, 1024], P('mp', 'dp')
- head_first: float32 [1024, 4096], P('dp', 'mp')
- code_second: float32 [4096, 1024], P('dp')
- class_second: float32 [1000, 1024], P(None, 'dp')
- adaln_second: float32 [1024, 6144], P('dp')
- qkv_second: float32 [3, 1024, 1024], P(None, 'dp', 'mp')
- proj_second: float32 [1024, 1024], P('mp', 'dp')
- expand_second: float32 [1024, 4096], P('dp', 'mp')
- contract_second: float32 [4096, 1024], P('mp', 'dp')
- head_second: float32 [1024, 4096], P('dp', 'mp')
- code_new: float32 [4096, 1024], P('dp')
- class_new: float32 [1000, 1024], P(None, 'dp')
- adaln_new: float32 [1024, 6144], P('dp')
- qkv_new: float32 [3, 1024, 1024], P(None, 'dp', 'mp')
- proj_new: float32 [1024, 1024], P('mp', 'dp')
- expand_new: float32 [1024, 4096], P('dp', 'mp')
- contract_new: float32 [4096, 1024], P('mp', 'dp')
- head_new: float32 [1024, 4096], P('dp', 'mp')
- loss: float32 [], replicated
- scale_counts: float32 [10], replicated
- grad_norm: float32 [], replicated
The draws below stay inside these ranges and needn't reach their ends.
Inputs may be any that keep to these rules, and one draw needn't show every extreme that they name: `item_lengths`: every entry is 0 or one of 1, 5, 14, 30, 55, 91, 155, 255, 424, 680 (an item ends at a scale of the pyramid); in a row the nonzero entries come first and sum to at most 800.
All inputs are finite; a program needn't handle non-finite values.
Results may differ from the reference program's by a relative error of at most 0.012.
The reference program's roundings to bfloat16 on the way count: a program that leaves them out, or rounds other values in their place, can miss the bound.
Values may be sent and summed in bfloat16 or wider, within the bound.
No kernel may reach another device: no remote copies, remote signals or barrier semaphores. Data moves between devices by JAX's collectives and lax.ppermute only.
A program may use at most 576 MiB of HBM per device.

```python
import math
import jax
import jax.numpy as jnp
from jax import lax

D = 1024
HEADS = 16
HEAD_WIDTH = 64
FF = 4096
CODES = 4096
CLASSES = 1000
LEN = 800
ITEMS = 8
NSCALES = 10
MICRO = 2
STEP = 10
ROWS_ALL = 16
PARAMS = 28286976


def draw_item_lengths(key, part):
    pyramid_sizes = jnp.array([1, 5, 14, 30, 55, 91, 155, 255, 424, 680], dtype=jnp.int32)
    places = jnp.arange(ROWS_ALL, dtype=jnp.int32)
    budget = (LEN + 2 * LEN * places // max(ROWS_ALL - 1, 1)) // 3
    budget = jnp.broadcast_to(budget[None, :], (MICRO, ROWS_ALL)).astype(jnp.int32)
    levels = jax.random.randint(key, (ITEMS, MICRO, ROWS_ALL), 1, 11, dtype=jnp.int32)
    levels = levels.at[0].set(10)
    level_ids = jnp.arange(1, 11, dtype=jnp.int32)

    def place(remaining, chosen):
        allowed = (level_ids <= chosen[..., None]) & (pyramid_sizes <= remaining[..., None])
        length = jnp.max(jnp.where(allowed, pyramid_sizes, 0), axis=-1).astype(jnp.int32)
        return (remaining - length, length)
    _, lengths = lax.scan(place, budget, levels)
    return jnp.transpose(lengths, (1, 2, 0))


def draw_head_weight(key, part):
    columns = jnp.arange(CODES, dtype=jnp.float32) / (CODES - 1)
    base = jax.random.normal(key, (D, CODES), jnp.float32)
    growth = 1.0 + 2.0 * columns
    return base * growth[None, :] / math.sqrt(D)


def set_ends(entries, key, low, largest):
    shape = entries.shape
    spot = [jax.random.randint(jax.random.fold_in(key, axis), (), 0, shape[axis]) for axis in range(len(shape))]
    entries = entries.at[tuple(spot)].set(low)
    longest = shape.index(max(shape))
    spot[longest] = (spot[longest] + 1) % shape[longest]
    return entries.at[tuple(spot)].set(largest)


def block_scale(own_key, shape, shards, smallest, largest):
    def one(axis_at, shards_of):
        draws = jax.random.uniform(jax.random.fold_in(jax.random.fold_in(own_key, 6), axis_at), (shards_of,), jnp.float32, smallest / len(shards), largest / len(shards))
        return jnp.repeat(jnp.exp(draws), shape[axis_at] // shards_of).reshape((-1,) + (1,) * (len(shape) - axis_at - 1))

    factor_of = one(*shards[0])
    for cut in shards[1:]:
        factor_of = factor_of * one(*cut)
    return factor_of


def noise(rng, extent, spread, most, shards=(), held_as=jnp.bfloat16):
    drawn = jax.random.normal(rng, extent, jnp.float32) * spread
    if len(shards) > 0:
        drawn = block_scale(rng, extent, shards, -0.22, 0.18) * drawn
    return jnp.clip(drawn, min=-most, max=most).astype(held_as)


def setup_inputs(seed: int = 0) -> dict:
    key_list = jax.random.split(jax.random.key(seed), 29)
    return {
        "input_codes": set_ends(jax.random.randint(key_list[0], (MICRO, ROWS_ALL, LEN), 0, CODES), jax.random.fold_in(key_list[0], 1), 0, CODES - 1).astype(jnp.int32),
        "target_codes": set_ends(jax.random.randint(key_list[1], (MICRO, ROWS_ALL, LEN), 0, CODES), jax.random.fold_in(key_list[1], 1), 0, CODES - 1).astype(jnp.int32),
        "item_lengths": draw_item_lengths(jax.random.fold_in(key_list[28], 71), 0),
        "item_labels": set_ends(jax.random.randint(key_list[3], (MICRO, ROWS_ALL, ITEMS), 0, CLASSES), jax.random.fold_in(key_list[3], 1), 0, CLASSES - 1).astype(jnp.int32),
        "code_table": noise(key_list[4], (CODES, D), 1.0, 6.0, ((0, 16),), jnp.float32),
        "class_table": noise(key_list[5], (CLASSES, D), 1.0, 6.0, ((1, 16),), jnp.float32),
        "adaln_weight": noise(key_list[6], (D, 6 * D), D ** -0.5, 0.1875, ((0, 16),), jnp.float32),
        "qkv_weight": noise(key_list[7], (3, D, D), D ** -0.5, 0.1875, ((1, 16), (2, 2)), jnp.float32),
        "proj_weight": noise(key_list[8], (D, D), (D // 32) ** -0.5, 1.0, ((0, 2), (1, 16)), jnp.float32),
        "expand_weight": noise(key_list[9], (D, FF), D ** -0.5, 0.1875, ((0, 16), (1, 2)), jnp.float32),
        "contract_weight": noise(key_list[10], (FF, D), FF ** -0.5, 0.09375, ((0, 2), (1, 16)), jnp.float32),
        "head_weight": draw_head_weight(jax.random.fold_in(key_list[28], 71), 0),
        "code_moment": noise(key_list[12], (CODES, D), (0.0002 / (PARAMS * CODES) ** 0.5), 3.725290298461914e-09, ((0, 16),), jnp.float32),
        "class_moment": noise(key_list[13], (CLASSES, D), (0.000111 / PARAMS ** 0.5), 1.1920928955078125e-07, ((1, 16),), jnp.float32),
        "adaln_moment": noise(key_list[14], (D, 6 * D), (0.000111 / PARAMS ** 0.5), 1.1920928955078125e-07, ((0, 16),), jnp.float32),
        "qkv_moment": noise(key_list[15], (3, D, D), (0.000111 / PARAMS ** 0.5), 1.1920928955078125e-07, ((1, 16), (2, 2)), jnp.float32),
        "proj_moment": noise(key_list[16], (D, D), (0.000111 / PARAMS ** 0.5), 1.1920928955078125e-07, ((0, 2), (1, 16)), jnp.float32),
        "expand_moment": noise(key_list[17], (D, FF), (0.000111 / PARAMS ** 0.5), 1.1920928955078125e-07, ((0, 16), (1, 2)), jnp.float32),
        "contract_moment": noise(key_list[18], (FF, D), (0.000111 / PARAMS ** 0.5), 1.1920928955078125e-07, ((0, 2), (1, 16)), jnp.float32),
        "head_moment": noise(key_list[19], (D, CODES), (0.000111 / PARAMS ** 0.5), 1.1920928955078125e-07, ((0, 16), (1, 2)), jnp.float32),
        "code_square": jnp.clip(jnp.exp(math.log(5.868977554190821e-18) - 1.3862944 * jax.random.uniform(key_list[20], (CODES, D), jnp.float32) ** block_scale(key_list[20], (CODES, D), ((0, 16),), -0.2, 0.2)), 1.4672443885477053e-18, 5.868977554190821e-18),
        "class_square": jnp.clip(jnp.exp(math.log(7.423910898735672e-15) - 1.38439135 * jax.random.uniform(key_list[21], (CLASSES, D), jnp.float32) ** block_scale(key_list[21], (CLASSES, D), ((1, 16),), -0.2, 0.2)), 1.8595130284475205e-15, 7.423910898735672e-15),
        "adaln_square": jnp.clip(jnp.exp(math.log(7.423910898735672e-15) - 1.38439135 * jax.random.uniform(key_list[22], (D, 6 * D), jnp.float32) ** block_scale(key_list[22], (D, 6 * D), ((0, 16),), -0.2, 0.2)), 1.8595130284475205e-15, 7.423910898735672e-15),
        "qkv_square": jnp.clip(jnp.exp(math.log(7.423910898735672e-15) - 1.38439135 * jax.random.uniform(key_list[23], (3, D, D), jnp.float32) ** block_scale(key_list[23], (3, D, D), ((1, 16), (2, 2)), -0.2, 0.2)), 1.8595130284475205e-15, 7.423910898735672e-15),
        "proj_square": jnp.clip(jnp.exp(math.log(7.423910898735672e-15) - 1.38439135 * jax.random.uniform(key_list[24], (D, D), jnp.float32) ** block_scale(key_list[24], (D, D), ((0, 2), (1, 16)), -0.2, 0.2)), 1.8595130284475205e-15, 7.423910898735672e-15),
        "expand_square": jnp.clip(jnp.exp(math.log(7.423910898735672e-15) - 1.38439135 * jax.random.uniform(key_list[25], (D, FF), jnp.float32) ** block_scale(key_list[25], (D, FF), ((0, 16), (1, 2)), -0.2, 0.2)), 1.8595130284475205e-15, 7.423910898735672e-15),
        "contract_square": jnp.clip(jnp.exp(math.log(7.423910898735672e-15) - 1.38439135 * jax.random.uniform(key_list[26], (FF, D), jnp.float32) ** block_scale(key_list[26], (FF, D), ((0, 2), (1, 16)), -0.2, 0.2)), 1.8595130284475205e-15, 7.423910898735672e-15),
        "head_square": jnp.clip(jnp.exp(math.log(7.423910898735672e-15) - 1.38439135 * jax.random.uniform(key_list[27], (D, CODES), jnp.float32) ** block_scale(key_list[27], (D, CODES), ((0, 16), (1, 2)), -0.2, 0.2)), 1.8595130284475205e-15, 7.423910898735672e-15),
    }


FULL_PRECISION = lax.Precision.HIGHEST
EPSILON = 1e-06
SOFTMAX_WARMTH = 12.0
CLIP_NORM = 0.001
BETA_ONE = 0.9
BETA_TWO = 0.95
DECAY = 0.05
ADAM_EPSILON = 1e-08
PYRAMID = (1, 5, 14, 30, 55, 91, 155, 255, 424)

@jax.custom_vjp
def low(v):
    return lax.optimization_barrier(v.astype(jnp.bfloat16)).astype(jnp.float32)

@jax.custom_vjp
def lowered_backward(v):
    return v

def low_keep(v):
    return (low(v), None)

def low_pass(kept, grad):
    return (grad,)

def back_keep(v):
    return (v, None)

def back_low(kept, grad):
    return (low(grad),)
low.defvjp(low_keep, low_pass)
lowered_backward.defvjp(back_keep, back_low)

def layout(lengths):
    lengths = lengths.astype(jnp.int32)
    ends = jnp.cumsum(lengths).astype(jnp.int32)
    places = jnp.arange(LEN, dtype=jnp.int32)
    passed = places[:, None] >= ends[None, :]
    segment = lax.optimization_barrier(jnp.sum(passed.astype(jnp.int32), axis=1)).astype(jnp.int32)
    start = lax.optimization_barrier(jnp.sum(jnp.where(passed, lengths[None, :], 0), axis=1)).astype(jnp.int32)
    offset = places - start
    bounds = jnp.array(PYRAMID, dtype=jnp.int32)
    scale_id = lax.optimization_barrier(jnp.sum((offset[:, None] >= bounds[None, :]).astype(jnp.int32), axis=1)).astype(jnp.int32)
    usable = places < ends[-1]
    return (segment, scale_id, usable)

def norm_rows(values):
    centered = values - lax.optimization_barrier(jnp.mean(values, axis=-1, keepdims=True))
    return centered * lax.rsqrt(lax.optimization_barrier(jnp.mean(centered * centered, axis=-1, keepdims=True)) + EPSILON)

def unit_heads(values):
    return values * lax.rsqrt(lax.optimization_barrier(jnp.mean(values * values, axis=-1, keepdims=True)) + EPSILON)

def matmul(left, right):
    return jnp.dot(left, right, precision=FULL_PRECISION)

def split_heads(values):
    return values.reshape(LEN, HEADS, HEAD_WIDTH)

def row_loss(weights, code_ids, target_ids, lengths, labels, inv_counts):
    code_table, class_table, adaln_weight, qkv_weight, proj_weight, expand_weight, contract_weight, head_weight = weights
    segment, scale_id, usable = layout(lengths)
    tokens = low(jnp.take(code_table, code_ids, axis=0))
    class_vec = low(jax.nn.silu(low(jnp.take(class_table, labels, axis=0))))
    modulation = lowered_backward(matmul(class_vec, low(adaln_weight)))
    modulation = jnp.concatenate([modulation, jnp.zeros((1, 6 * D), jnp.float32)], axis=0)
    per_token = jnp.take(modulation, segment, axis=0)
    gate_attn, gate_mlp, scale_attn, scale_mlp, shift_attn, shift_mlp = jnp.split(per_token, 6, axis=1)
    normed_attn = low(norm_rows(tokens) * (1.0 + scale_attn) + shift_attn)
    queries = split_heads(lowered_backward(matmul(normed_attn, low(qkv_weight[0]))))
    keys_raw = split_heads(lowered_backward(matmul(normed_attn, low(qkv_weight[1]))))
    value_b = split_heads(low(lowered_backward(matmul(normed_attn, low(qkv_weight[2])))))
    query_normed = low(unit_heads(queries))
    key_normed = low(unit_heads(keys_raw))
    attention_scores = lowered_backward(jnp.einsum('ygp,ugp->gyu', query_normed, key_normed, precision=FULL_PRECISION) * (SOFTMAX_WARMTH / HEAD_WIDTH))
    allowed = (segment[:, None] == segment[None, :]) & (scale_id[None, :] <= scale_id[:, None])
    attention_scores = jnp.where(allowed[None], attention_scores, -1e+30)
    attention = low(jax.nn.softmax(attention_scores, axis=-1))
    attended = jnp.einsum('hqk,khd->qhd', attention, value_b, precision=FULL_PRECISION).reshape(LEN, D)
    attended = low(lowered_backward(attended))
    attn_out = lowered_backward(matmul(attended, low(proj_weight)))
    middle = tokens + gate_attn * attn_out
    normed_mlp = low(norm_rows(middle) * (1.0 + scale_mlp) + shift_mlp)
    hidden_pre = lowered_backward(matmul(normed_mlp, low(expand_weight)))
    active = low(jax.nn.gelu(hidden_pre, approximate=True))
    mlp_out = lowered_backward(matmul(active, low(contract_weight)))
    residual = middle + gate_mlp * mlp_out
    normed_head = low(norm_rows(residual))
    logits = lowered_backward(matmul(normed_head, low(head_weight)))
    log_total = jax.nn.logsumexp(logits, axis=-1)
    target = jnp.take_along_axis(logits, target_ids[:, None], axis=1)[:, 0]
    token_weight = jnp.where(usable, jnp.take(inv_counts, scale_id), 0.0)
    return jnp.sum((log_total - target) * token_weight)

def step_rates():
    return (2.5, 2.5, 2.5 / math.sqrt(D), 2.5 / math.sqrt(D), 2.5 / math.sqrt(D // 32), 2.5 / math.sqrt(D), 2.5 / math.sqrt(FF), 5.0 / math.sqrt(D))

def adamw_update(weight, grad, moment, square, rate):
    first = BETA_ONE * moment + (1.0 - BETA_ONE) * grad
    second = BETA_TWO * square + (1.0 - BETA_TWO) * grad * grad
    corrected = first / (1.0 - BETA_ONE ** STEP) / (jnp.sqrt(second / (1.0 - BETA_TWO ** STEP)) + ADAM_EPSILON)
    return (first, second, weight - rate * (corrected + DECAY * weight))

def reference(input_codes, target_codes, item_lengths, item_labels, code_table, class_table, adaln_weight, qkv_weight, proj_weight, expand_weight, contract_weight, head_weight, code_moment, class_moment, adaln_moment, qkv_moment, proj_moment, expand_moment, contract_moment, head_moment, code_square, class_square, adaln_square, qkv_square, proj_square, expand_square, contract_square, head_square):
    weights = (code_table, class_table, adaln_weight, qkv_weight, proj_weight, expand_weight, contract_weight, head_weight)
    moments = (code_moment, class_moment, adaln_moment, qkv_moment, proj_moment, expand_moment, contract_moment, head_moment)
    squares = (code_square, class_square, adaln_square, qkv_square, proj_square, expand_square, contract_square, head_square)
    code_ids = input_codes.reshape(-1, LEN)
    target_ids = target_codes.reshape(-1, LEN)
    lengths = item_lengths.reshape(-1, ITEMS)
    labels = item_labels.reshape(-1, ITEMS)
    segment, scale_id, usable = jax.vmap(layout)(lengths)
    picked = (scale_id[..., None] == jnp.arange(NSCALES, dtype=jnp.int32)) & usable[..., None]
    scale_counts = lax.optimization_barrier(jnp.sum(picked.astype(jnp.float32), axis=(0, 1)))
    inv_counts = 1.0 / (NSCALES * jnp.maximum(scale_counts, 1.0))
    checked = jax.checkpoint(row_loss)

    def total(params):

        def step(carry, row):
            return (carry + checked(params, row[0], row[1], row[2], row[3], inv_counts), None)
        summed, _ = lax.scan(step, jnp.zeros((), jnp.float32), (code_ids, target_ids, lengths, labels))
        return summed
    loss, pullback = jax.vjp(total, weights)
    grads = pullback(jnp.ones((), jnp.float32))[0]
    squared = jnp.zeros((), jnp.float32)
    for grad in grads:
        squared = squared + jnp.sum(grad * grad)
    grad_norm = jnp.sqrt(squared)
    clip = jnp.minimum(1.0, CLIP_NORM / (grad_norm + 1e-06))
    firsts, seconds, updated = ([], [], [])
    for weight, grad, moment, square, rate in zip(weights, grads, moments, squares, step_rates()):
        first, second, fresh = adamw_update(weight, grad * clip, moment, square, rate)
        firsts.append(first)
        seconds.append(second)
        updated.append(fresh)
    return (firsts[0], firsts[1], firsts[2], firsts[3], firsts[4], firsts[5], firsts[6], firsts[7], seconds[0], seconds[1], seconds[2], seconds[3], seconds[4], seconds[5], seconds[6], seconds[7], updated[0], updated[1], updated[2], updated[3], updated[4], updated[5], updated[6], updated[7], loss, scale_counts, grad_norm)
```

```python
import math

import jax
import jax.numpy as jnp
from jax import lax
from jax.experimental import pallas as pl
from jax.experimental.pallas import tpu as pltpu
from jax.sharding import PartitionSpec as P

D = 1024
HEAD_WIDTH = 64
FF = 4096
CLASSES = 1000
LEN = 800
ITEMS = 8
NSCALES = 10
MICRO = 2
STEP = 10


EPSILON = 1e-06
SOFTMAX_WARMTH = 12.0
CLIP_NORM = 0.001
BETA_ONE = 0.9
BETA_TWO = 0.95
DECAY = 0.05
ADAM_EPSILON = 1e-08
PYRAMID = (1, 5, 14, 30, 55, 91, 155, 255, 424)

SCORE_SCALE = SOFTMAX_WARMTH / HEAD_WIDTH
VMEM_LIMIT = 60 * 2**20

bf16 = jnp.bfloat16
f32 = jnp.float32
barrier = lax.optimization_barrier


def swap(values, bits):
    n = lax.axis_size("dp")
    return lax.ppermute(values, "dp", [(i, i ^ bits) for i in range(n)])


def swap_core(values):
    return lax.ppermute(values, "mp", [(0, 1), (1, 0)])


def quarter():
    return lax.axis_size("dp") // 4


def run_tick(stages):
    outs = []
    for kind, value in stages:
        if kind == "z":
            outs.append([swap(value, 4 * j) for j in range(1, quarter())])
        elif kind == "zs":
            outs.append([swap(value[j], 4 * j) for j in range(1, quarter())])
        elif kind == "xy":
            outs.append([swap(value[0], 1), swap(value[1], 2)])
        else:
            outs.append(swap_core(value))
    return outs


class Gather:
    def __init__(self, block, core=True):
        self.block = block
        self.step = 0
        self.core = core

    def done(self):
        return self.step == (4 if self.core else 3)

    def request(self):
        if self.step == 0:
            return ("z", self.block)
        if self.step == 1:
            return ("xy", (self.group, self.group))
        if self.step == 2:
            half = self.group.shape[0] // 2
            return ("xy", (self.from_y[:half], self.from_x[half:]))
        return ("mp", self.own)

    def accept(self, got):
        if self.step == 0:
            self.group = jnp.concatenate([self.block] + got)
        elif self.step == 1:
            self.from_x, self.from_y = got
        elif self.step == 2:
            self.own = jnp.concatenate([self.group, self.from_x, self.from_y] + got)
        else:
            self.peer = got
        self.step += 1


class Scatter:
    def __init__(self, own, peer=None, dtype=bf16):
        n = lax.axis_size("dp")
        self.dtype = dtype
        shape = (4, n // 4, own.shape[0] // n) + own.shape[1:]
        self.own = own.reshape(shape)
        self.peer = None if peer is None else peer.reshape(shape)
        self.step = 0 if peer is not None else 1
        self.total = self.own.astype(f32) if peer is None else None

    def done(self):
        return self.step == 4

    def request(self):
        half = self.own.shape[1] // 2
        if self.step == 0:
            return ("mp", self.peer)
        if self.step == 1:
            s = self.total
            return ("xy", (s[3, :half].astype(self.dtype), s[3, half:].astype(self.dtype)))
        if self.step == 2:
            s = self.total
            rest = s[1][:half], s[1][half:] + self.diag[1].astype(f32)
            rest_y = s[2][:half] + self.diag[0].astype(f32), s[2][half:]
            return (
                "xy",
                (
                    jnp.concatenate(rest).astype(self.dtype),
                    jnp.concatenate(rest_y).astype(self.dtype),
                ),
            )
        return ("zs", [self.column[j].astype(self.dtype) for j in range(quarter())])

    def accept(self, got):
        if self.step == 0:
            self.total = self.own.astype(f32) + got.astype(f32)
        elif self.step == 1:
            self.diag = got
        elif self.step == 2:
            self.column = self.total[0] + got[0].astype(f32) + got[1].astype(f32)
        else:
            out = self.column[0]
            for part in got:
                out = out + part.astype(f32)
            self.result = out
        self.step += 1


class Engine:
    def __init__(self):
        self.jobs = []
        self.last = ()

    def add(self, job):
        self.jobs.append(job)

    def tick(self, live=()):
        jobs = [job for job in self.jobs if not job.done()]
        requests = [job.request() for job in jobs]
        kinds = [kind for kind, _ in requests]
        values = [value for _, value in requests]
        values, live, _ = barrier((values, live, self.last))
        outs = barrier(run_tick(list(zip(kinds, values))))
        self.last = outs
        for job, out in zip(jobs, outs):
            job.accept(out)
        return live


def small_gather(values):
    group = jnp.stack([values] + [swap(values, 4 * j) for j in range(1, quarter())])
    return jnp.concatenate([group] + [swap(group, g) for g in (1, 2, 3)])


def total_over_all(values):
    n = lax.axis_size("dp")
    bits = 1
    while bits < n:
        values = values + swap(values, bits)
        bits *= 2
    return values + swap_core(values)


def place_of(index):
    apart = jnp.bitwise_xor(index, lax.axis_index("dp"))
    return (apart & 3) * quarter() + (apart >> 2)


def layout(lengths):
    ends = jnp.cumsum(lengths)
    places = jnp.arange(LEN, dtype=jnp.int32)
    passed = places[:, None] >= ends[None, :]
    segment = jnp.sum(passed.astype(jnp.int32), axis=1)
    start = jnp.sum(jnp.where(passed, lengths[None, :], 0), axis=1)
    offset = places - start
    bounds = jnp.array(PYRAMID, dtype=jnp.int32)
    scale_id = jnp.sum((offset[:, None] >= bounds[None, :]).astype(jnp.int32), axis=1)
    usable = places < ends[-1]
    return (segment, scale_id, usable)


def norm_rows(values):
    centered = values - jnp.mean(values, axis=-1, keepdims=True)
    return centered * lax.rsqrt(jnp.mean(centered * centered, axis=-1, keepdims=True) + EPSILON)


def unit_heads(values):
    return values * lax.rsqrt(jnp.mean(values * values, axis=-1, keepdims=True) + EPSILON)


def modulate(values, scale_part, shift_part):
    return norm_rows(values) * (1.0 + scale_part) + shift_part


def gelu_tanh(values):
    return jax.nn.gelu(values, approximate=True)


def matmul(left, right):
    return jnp.dot(left, right, preferred_element_type=f32)


def matmul_tn(left, right):
    return lax.dot_general(left, right, (((0,), (0,)), ((), ())), preferred_element_type=f32)


def matmul_nt(left, right):
    return lax.dot_general(left, right, (((1,), (1,)), ((), ())), preferred_element_type=f32)


def exact_tn(left, right):
    return lax.dot_general(
        left,
        right,
        (((0,), (0,)), ((), ())),
        precision=lax.Precision.HIGHEST,
        preferred_element_type=f32,
    )


def unit_pair(values):
    factor = lax.rsqrt(jnp.mean(values * values, axis=-1, keepdims=True) + EPSILON)
    return factor, (values * factor).astype(bf16)


def unit_back(values, factor, grad):
    inner = jnp.mean(grad * values, axis=-1, keepdims=True)
    return (factor * (grad - values * (factor * factor * inner))).astype(bf16)


def attend_kernel(q_ref, k_ref, v_ref, bias_ref, out_ref):
    outs = []
    for head in range(2):
        cut = slice(head * HEAD_WIDTH, (head + 1) * HEAD_WIDTH)
        _, query_n = unit_pair(q_ref[:, cut])
        _, key_n = unit_pair(k_ref[:, cut])
        raised = jnp.exp(matmul_nt(query_n, key_n) * SCORE_SCALE + bias_ref[...])
        share = 1.0 / jnp.sum(raised, axis=-1, keepdims=True)
        outs.append(matmul((raised * share).astype(bf16), v_ref[:, cut].astype(bf16)).astype(bf16))
    out_ref[...] = jnp.concatenate(outs, axis=1)


def attend_back_kernel(q_ref, k_ref, v_ref, g_ref, bias_ref, out_ref):
    pair, pairs = pl.program_id(0), pl.num_programs(0)
    results = [[], [], []]
    for head in range(2):
        cut = slice(head * HEAD_WIDTH, (head + 1) * HEAD_WIDTH)
        query, key = q_ref[:, cut], k_ref[:, cut]
        query_f, query_n = unit_pair(query)
        key_f, key_n = unit_pair(key)
        value_b, grad_out = v_ref[:, cut].astype(bf16), g_ref[:, cut]
        grad_q, grad_k, grad_v = [], 0.0, 0.0
        for low, high in ((0, 384), (384, LEN)):
            raised = jnp.exp(matmul_nt(key_n, query_n[low:high]) * SCORE_SCALE + bias_ref[:, low:high])
            attention = raised * (1.0 / jnp.sum(raised, axis=0, keepdims=True))
            grad_probs = matmul_nt(value_b, grad_out[low:high])
            row_dot = jnp.sum(attention * grad_probs, axis=0, keepdims=True)
            grad_scores = (attention * (grad_probs - row_dot)).astype(bf16)
            grad_v = grad_v + matmul(attention.astype(bf16), grad_out[low:high])
            grad_k = grad_k + matmul(grad_scores, query_n[low:high])
            grad_q.append(matmul_tn(key_n, grad_scores).T)
        grad_q = jnp.concatenate(grad_q, axis=0) * SCORE_SCALE
        results[0].append(unit_back(query, query_f, grad_q))
        results[1].append(unit_back(key, key_f, grad_k * SCORE_SCALE))
        results[2].append(grad_v.astype(bf16))
    for i in range(3):
        start = pl.multiple_of((i * pairs + pair) * 2 * HEAD_WIDTH, 2 * HEAD_WIDTH)
        out_ref[:, pl.ds(start, 2 * HEAD_WIDTH)] = jnp.concatenate(results[i], axis=1)


def pair_specs(pairs):
    def third(i):
        return pl.BlockSpec((LEN, 2 * HEAD_WIDTH), lambda pair: (0, i * pairs + pair))

    return [third(0), third(1), third(2)], pl.BlockSpec((LEN, LEN), lambda pair: (0, 0))


def attend(raw, bias):
    width = raw.shape[1] // 3
    thirds, bias_spec = pair_specs(width // (2 * HEAD_WIDTH))
    return pl.pallas_call(
        attend_kernel,
        grid=(width // (2 * HEAD_WIDTH),),
        in_specs=thirds + [bias_spec],
        out_specs=thirds[0],
        out_shape=jax.ShapeDtypeStruct((LEN, width), bf16),
        compiler_params=pltpu.CompilerParams(vmem_limit_bytes=VMEM_LIMIT),
        cost_estimate=pl.CostEstimate(
            flops=4 * LEN * LEN * width,
            transcendentals=LEN * LEN * width // HEAD_WIDTH,
            bytes_accessed=16 * LEN * width,
        ),
    )(raw, raw, raw, bias)


def attend_back(raw, grad_out, bias_t):
    width = raw.shape[1] // 3
    thirds, bias_spec = pair_specs(width // (2 * HEAD_WIDTH))
    return pl.pallas_call(
        attend_back_kernel,
        grid=(width // (2 * HEAD_WIDTH),),
        in_specs=thirds + [thirds[0], bias_spec],
        out_specs=pl.BlockSpec((LEN, 3 * width), lambda pair: (0, 0)),
        out_shape=jax.ShapeDtypeStruct((LEN, 3 * width), bf16),
        compiler_params=pltpu.CompilerParams(vmem_limit_bytes=VMEM_LIMIT),
        cost_estimate=pl.CostEstimate(
            flops=10 * LEN * LEN * width,
            transcendentals=LEN * LEN * width // HEAD_WIDTH,
            bytes_accessed=20 * LEN * width,
        ),
    )(raw, raw, raw, grad_out, bias_t)


def step_rates():
    return (
        2.5,
        2.5,
        2.5 / math.sqrt(D),
        2.5 / math.sqrt(D),
        2.5 / math.sqrt(D // 32),
        2.5 / math.sqrt(D),
        2.5 / math.sqrt(FF),
        5.0 / math.sqrt(D),
    )


def adamw_update(weight, grad, moment, square, rate):
    first = BETA_ONE * moment + (1.0 - BETA_ONE) * grad
    second = BETA_TWO * square + (1.0 - BETA_TWO) * grad * grad
    corrected = (
        first / (1.0 - BETA_ONE**STEP) / (jnp.sqrt(second / (1.0 - BETA_TWO**STEP)) + ADAM_EPSILON)
    )
    return (first, second, weight - rate * (corrected + DECAY * weight))


def on_device(
    input_codes,
    target_codes,
    item_lengths,
    item_labels,
    code_table,
    class_table,
    adaln_weight,
    qkv_weight,
    proj_weight,
    expand_weight,
    contract_weight,
    head_weight,
    code_moment,
    class_moment,
    adaln_moment,
    qkv_moment,
    proj_moment,
    expand_moment,
    contract_moment,
    head_moment,
    code_square,
    class_square,
    adaln_square,
    qkv_square,
    proj_square,
    expand_square,
    contract_square,
    head_square,
):
    masters = (
        code_table,
        class_table,
        adaln_weight,
        qkv_weight,
        proj_weight.T,
        expand_weight,
        contract_weight.T,
        head_weight,
    )
    moments = (
        code_moment,
        class_moment,
        adaln_moment,
        qkv_moment,
        proj_moment.T,
        expand_moment,
        contract_moment.T,
        head_moment,
    )
    squares = (
        code_square,
        class_square,
        adaln_square,
        qkv_square,
        proj_square.T,
        expand_square,
        contract_square.T,
        head_square,
    )
    n = lax.axis_size("dp")
    core = lax.axis_index("mp")
    rows = code_table.shape[0]
    half_rows = rows // 2
    width = proj_weight.shape[0]
    wide = expand_weight.shape[1]
    codes_local = head_weight.shape[1]

    def mine(values):
        return lax.dynamic_index_in_dim(values, core, 0, keepdims=False)

    code_block = lax.dynamic_slice_in_dim(code_table, core * half_rows, half_rows, 0).astype(bf16)
    attn_block = jnp.concatenate(
        [qkv_weight[0], qkv_weight[1], qkv_weight[2], proj_weight.T], axis=1
    ).astype(bf16)
    jobs = [
        Gather(block)
        for block in (
            code_block,
            attn_block,
            expand_weight.astype(bf16),
            contract_weight.T.astype(bf16),
            head_weight.astype(bf16),
        )
    ]
    numbers = small_gather(jnp.concatenate([item_lengths[:, 0], item_labels[:, 0]], axis=1))
    engine = Engine()
    engine.add(jobs[0])
    engine.tick()
    labels_own = mine(jnp.swapaxes(numbers[:, :, ITEMS:], 0, 1)).reshape(-1)
    labels_peer = mine(jnp.swapaxes(numbers[:, ::-1, ITEMS:], 0, 1)).reshape(-1)
    class_low = class_table.astype(bf16)
    adaln_low = adaln_weight.astype(bf16)

    def class_part(labels):
        picked = (labels[:, None] == jnp.arange(CLASSES, dtype=jnp.int32)[None, :]).astype(bf16)
        class_rows = matmul(picked, class_low)
        return picked, class_rows, jax.nn.silu(class_rows).astype(bf16)

    picked_own, class_rows_own, class_vec_own = class_part(labels_own)
    picked_peer, class_rows_peer, class_vec_peer = class_part(labels_peer)
    mod_job = Scatter(matmul(class_vec_own, adaln_low), None, f32)
    engine.add(mod_job)
    for job in jobs[1:4]:
        engine.add(job)
        engine.tick()

    lengths = mine(item_lengths)[0]
    code_ids = mine(input_codes)[0]
    target_ids = mine(target_codes)[0]
    segment, scale_id, usable = layout(lengths)
    bounds = jnp.array((0,) + PYRAMID, dtype=jnp.int32)
    sizes = jnp.array(PYRAMID + (LEN,), dtype=jnp.int32) - bounds
    all_lengths = numbers[:, :, :ITEMS].reshape(-1)
    scale_counts = jnp.sum(
        jnp.clip(all_lengths[:, None] - bounds[None, :], 0, sizes[None, :]), axis=0
    ).astype(f32)
    inv_counts = 1.0 / (NSCALES * jnp.maximum(scale_counts, 1.0))
    scale_hot = scale_id[:, None] == jnp.arange(NSCALES, dtype=jnp.int32)[None, :]
    token_weight = jnp.where(
        usable, jnp.sum(jnp.where(scale_hot, inv_counts[None, :], 0.0), axis=1), 0.0
    )

    block_width = D // n
    block_ids = jnp.arange(n, dtype=jnp.int32)
    block_place = place_of(block_ids)
    feature_place = (block_place[:, None] * block_width + jnp.arange(block_width)[None, :]).reshape(-1)
    turn = (feature_place[:, None] == jnp.arange(D, dtype=jnp.int32)[None, :]).astype(bf16)
    relative_block = ((jnp.arange(n) % quarter()) * 4 + jnp.arange(n) // quarter()) ^ lax.axis_index("dp")

    same = segment[:, None] == segment[None, :]
    bias = jnp.where(same & (scale_id[None, :] <= scale_id[:, None]), 0.0, -1e30)
    bias_t = jnp.where(same & (scale_id[:, None] <= scale_id[None, :]), 0.0, -1e30)
    within = code_ids % rows
    other = (within // half_rows != core).astype(jnp.int32)
    code_rows = other * (n * half_rows) + place_of(code_ids // rows) * half_rows + within % half_rows

    engine.add(jobs[4])
    table, mod, turn, code_rows = engine.tick(
        ((jobs[0].own, jobs[0].peer), mod_job.result, turn, code_rows)
    )
    tokens = matmul(jnp.take(jnp.concatenate(table), code_rows, axis=0), turn)
    mod = mod.reshape(ITEMS * 6, n, block_width)
    mod = jnp.take(mod, relative_block, axis=1).reshape(ITEMS, 6 * D)
    padded = jnp.concatenate([mod, jnp.zeros((1, 6 * D), f32)], axis=0)
    per_token = jnp.take(padded, segment, axis=0)
    gate_attn, gate_mlp, scale_attn, scale_mlp, shift_attn, shift_mlp = jnp.split(
        per_token, 6, axis=1
    )
    normed_attn = modulate(tokens, scale_attn, shift_attn).astype(bf16)
    normed_attn, bias = engine.tick((normed_attn, bias))
    attn_w = (jobs[1].own, jobs[1].peer)
    raw = [matmul(normed_attn, w[:, : 3 * width]) for w in attn_w]
    attended = [attend(r, bias) for r in raw]
    attended, normed_attn = engine.tick((attended, normed_attn))
    attn_out = sum(matmul_nt(a, w[:, 3 * width :]) for a, w in zip(attended, attn_w))
    middle = tokens + gate_attn * attn_out
    normed_mlp = modulate(middle, scale_mlp, shift_mlp).astype(bf16)
    expand_w = (jobs[2].own, jobs[2].peer)
    hidden_pre = [matmul(normed_mlp, w) for w in expand_w]
    active = [gelu_tanh(h).astype(bf16) for h in hidden_pre]
    active, middle = engine.tick((active, middle))
    contract_w = (jobs[3].own, jobs[3].peer)
    mlp_out = matmul_nt(active[0], contract_w[0]) + matmul_nt(active[1], contract_w[1])
    residual = middle + gate_mlp * mlp_out
    normed_head = norm_rows(residual).astype(bf16)
    head_w = (jobs[4].own, jobs[4].peer)
    logits = [matmul(normed_head, w) for w in head_w]
    shifted = [
        target_ids - core * codes_local,
        target_ids - (1 - core) * codes_local,
    ]
    is_target = [
        jnp.arange(codes_local, dtype=jnp.int32)[None, :] == s[:, None] for s in shifted
    ]
    target_logit = sum(jnp.sum(jnp.where(t, x, 0.0), axis=1) for t, x in zip(is_target, logits))
    row_max = jnp.maximum(jnp.max(logits[0], axis=1), jnp.max(logits[1], axis=1))
    exp_total = sum(jnp.sum(jnp.exp(x - row_max[:, None]), axis=1) for x in logits)
    log_total = row_max + jnp.log(exp_total)
    loss_local = jnp.sum((log_total - target_logit) * token_weight)

    grad_logits = [
        ((jnp.exp(x - log_total[:, None]) - t.astype(f32)) * token_weight[:, None]).astype(bf16)
        for x, t in zip(logits, is_target)
    ]

    def scatter_job(left, rights):
        return Scatter(*[matmul_tn(left, right).astype(bf16) for right in rights])

    head_job = scatter_job(normed_head, grad_logits)
    engine.add(head_job)
    grad_logits, active = engine.tick((grad_logits, active))
    grad_normed_head = matmul_nt(grad_logits[0], head_w[0]) + matmul_nt(grad_logits[1], head_w[1])
    _, norm_back = jax.vjp(norm_rows, residual)
    grad_residual = norm_back(grad_normed_head)[0]
    grad_mlp_out = (gate_mlp * grad_residual).astype(bf16)
    grad_gate_mlp = grad_residual * mlp_out
    contract_job = scatter_job(grad_mlp_out, active)
    engine.add(contract_job)
    grad_mlp_out, hidden_pre, grad_residual = engine.tick((grad_mlp_out, hidden_pre, grad_residual))
    grad_pre = []
    for h, w in zip(hidden_pre, contract_w):
        _, gelu_back = jax.vjp(gelu_tanh, h)
        grad_pre.append(gelu_back(matmul(grad_mlp_out, w))[0].astype(bf16))
    expand_job = scatter_job(normed_mlp, grad_pre)
    engine.add(expand_job)
    grad_pre, grad_residual = engine.tick((grad_pre, grad_residual))
    grad_normed_mlp = matmul_nt(grad_pre[0], expand_w[0]) + matmul_nt(grad_pre[1], expand_w[1])
    _, mlp_norm_back = jax.vjp(modulate, middle, scale_mlp, shift_mlp)
    grad_middle_part, grad_scale_mlp, grad_shift_mlp = mlp_norm_back(grad_normed_mlp)
    grad_middle = grad_residual + grad_middle_part
    grad_attn_out = (gate_attn * grad_middle).astype(bf16)
    grad_gate_attn = grad_middle * attn_out
    grad_proj = [matmul_tn(grad_attn_out, a).astype(bf16) for a in attended]
    grad_attended = [matmul(grad_attn_out, w[:, 3 * width :]).astype(bf16) for w in attn_w]
    grad_attended, raw, bias_t, grad_proj = engine.tick((grad_attended, raw, bias_t, grad_proj))
    grad_own = attend_back(raw[0], grad_attended[0], bias_t)
    grad_own, grad_attended, normed_attn = engine.tick((grad_own, grad_attended, normed_attn))
    grad_peer = attend_back(raw[1], grad_attended[1], bias_t)
    grad_raw = (grad_own, grad_peer)
    attn_job = Scatter(
        *[
            jnp.concatenate([matmul_tn(normed_attn, g).astype(bf16), p], axis=1)
            for g, p in zip(grad_raw, grad_proj)
        ]
    )
    engine.add(attn_job)
    grad_raw, grad_middle, turn = engine.tick((grad_raw, grad_middle, turn))
    grad_normed_attn = sum(matmul_nt(g, w[:, : 3 * width]) for g, w in zip(grad_raw, attn_w))
    _, attn_norm_back = jax.vjp(modulate, tokens, scale_attn, shift_attn)
    grad_tokens_part, grad_scale_attn, grad_shift_attn = attn_norm_back(grad_normed_attn)
    grad_tokens = grad_middle + grad_tokens_part
    grad_flat = matmul_nt(grad_tokens.astype(bf16), turn).astype(bf16)
    code_hot = (
        code_rows[:, None] == jnp.arange(2 * n * half_rows, dtype=jnp.int32)[None, :]
    ).astype(bf16)
    grad_code = matmul_tn(code_hot, grad_flat).astype(bf16)
    code_job = Scatter(grad_code[: n * half_rows], grad_code[n * half_rows :])
    engine.add(code_job)
    grad_scale_attn, grad_shift_attn = engine.tick((grad_scale_attn, grad_shift_attn))
    grad_per_token = jnp.concatenate(
        [
            grad_gate_attn,
            grad_gate_mlp,
            grad_scale_attn,
            grad_scale_mlp,
            grad_shift_attn,
            grad_shift_mlp,
        ],
        axis=1,
    )
    segment_hot = (segment[:, None] == jnp.arange(ITEMS, dtype=jnp.int32)[None, :]).astype(f32)
    grad_items = exact_tn(segment_hot, grad_per_token)
    grad_modulation = jnp.take(
        grad_items.reshape(ITEMS * 6, n, block_width), block_place, axis=1
    ).reshape(ITEMS, 6 * D).astype(bf16)
    item_job = Gather(grad_modulation)
    engine.add(item_job)
    for _ in range(4):
        engine.tick()
    adaln_grad = matmul_tn(class_vec_own, item_job.own) + matmul_tn(class_vec_peer, item_job.peer)

    def class_grad_part(picked, class_rows, items):
        grad_class_vec = matmul_nt(items, adaln_low)
        _, silu_back = jax.vjp(jax.nn.silu, class_rows)
        return exact_tn(picked.astype(f32), silu_back(grad_class_vec)[0])

    class_grad = class_grad_part(picked_own, class_rows_own, item_job.own) + class_grad_part(
        picked_peer, class_rows_peer, item_job.peer
    )
    code_half = code_job.result
    code_other = swap_core(code_half)
    code_grad = jnp.where(
        core == 0,
        jnp.concatenate([code_half, code_other]),
        jnp.concatenate([code_other, code_half]),
    )
    attn_grad = attn_job.result
    qkv_grad = jnp.stack([attn_grad[:, i * width : (i + 1) * width] for i in range(3)])
    gradients = (
        code_grad,
        class_grad,
        adaln_grad,
        qkv_grad,
        attn_grad[:, 3 * width :],
        expand_job.result,
        contract_job.result,
        head_job.result,
    )
    shared_sq = jnp.sum(class_grad * class_grad) + jnp.sum(adaln_grad * adaln_grad)
    own_sq = jnp.sum(code_half * code_half) + jnp.sum(attn_grad * attn_grad)
    for grad in gradients[5:]:
        own_sq = own_sq + jnp.sum(grad * grad)
    totals = total_over_all(
        jnp.concatenate([(own_sq + 0.5 * shared_sq).reshape(1), loss_local.reshape(1)])
    )
    squared, loss = totals[0], totals[1]
    grad_norm = jnp.sqrt(squared)
    clip = jnp.minimum(1.0, CLIP_NORM / (grad_norm + 1e-06))
    firsts, seconds, updated = ([], [], [])
    for place, (weight, grad, moment, square, rate) in enumerate(
        zip(masters, gradients, moments, squares, step_rates())
    ):
        for kept, value in zip(
            (firsts, seconds, updated), adamw_update(weight, grad * clip, moment, square, rate)
        ):
            kept.append(value.T if place in (4, 6) else value)
    return (*firsts, *seconds, *updated, loss, scale_counts, grad_norm)


def solution(mesh):
    token_spec = P(None, "dp", None)
    weight_specs = (
        P("dp", None),
        P(None, "dp"),
        P("dp", None),
        P(None, "dp", "mp"),
        P("mp", "dp"),
        P("dp", "mp"),
        P("mp", "dp"),
        P("dp", "mp"),
    )
    return jax.shard_map(
        on_device,
        mesh=mesh,
        in_specs=(token_spec,) * 4 + weight_specs * 3,
        out_specs=weight_specs * 3 + (P(), P(), P()),
        check_vma=False,
    )
```

```python
import math

import jax
import jax.numpy as jnp
from jax import lax
from jax.experimental import pallas as pl
from jax.experimental.pallas import tpu as pltpu
from jax.sharding import PartitionSpec as P

D = 1024
HEAD_WIDTH = 64
FF = 4096
CLASSES = 1000
LEN = 800
ITEMS = 8
NSCALES = 10
MICRO = 2
STEP = 10


EPSILON = 1e-06
SOFTMAX_WARMTH = 12.0
CLIP_NORM = 0.001
BETA_ONE = 0.9
BETA_TWO = 0.95
DECAY = 0.05
ADAM_EPSILON = 1e-08
PYRAMID = (1, 5, 14, 30, 55, 91, 155, 255, 424)

SCORE_SCALE = SOFTMAX_WARMTH / HEAD_WIDTH
GELU_C = math.sqrt(2.0 / math.pi)
PAIR = 2 * HEAD_WIDTH
BLOCK = 512
ATTEND_FLOPS = LEN * PAIR * (8 * D + 4 * LEN)
VMEM_LIMIT = 60 * 2**20

bf16 = jnp.bfloat16
f32 = jnp.float32
barrier = lax.optimization_barrier


def swap(values, bits):
    n = lax.axis_size("dp")
    return lax.ppermute(values, "dp", [(i, i ^ bits) for i in range(n)])


def swap_core(values):
    return lax.ppermute(values, "mp", [(0, 1), (1, 0)])


def quarter():
    return lax.axis_size("dp") // 4


def columns_of_chips():
    n = lax.axis_size("dp")
    return [[xy + 4 * z for z in range(n // 4)] for xy in range(4)]


def over_z(values):
    return lax.all_to_all(values, "dp", 0, 0, tiled=True, axis_index_groups=columns_of_chips())


def sum_z(values):
    return lax.psum_scatter(values, "dp", scatter_dimension=0, axis_index_groups=columns_of_chips())


def join_kernel(*refs):
    parts, out = refs[:-1], refs[-1]
    at = 0
    for part in parts:
        rows = part.shape[0]
        out[at : at + rows, :] = part[...]
        at += rows


def join(parts):
    rows = sum(part.shape[0] for part in parts)
    total = parts[0].shape[1]
    return pl.pallas_call(
        join_kernel,
        grid=(total // BLOCK,),
        in_specs=[pl.BlockSpec((part.shape[0], BLOCK), lambda i: (0, i)) for part in parts],
        out_specs=pl.BlockSpec((rows, BLOCK), lambda i: (0, i)),
        out_shape=jax.ShapeDtypeStruct((rows, total), parts[0].dtype),
    )(*parts)


class Gather:
    def __init__(self, block):
        self.block = block
        self.step = 0

    def request(self):
        if self.step == 0:
            return jnp.broadcast_to(self.block[None], (quarter(),) + self.block.shape)
        if self.step == 1:
            return self.group
        if self.step == 2:
            half = self.group.shape[0] // 2
            return (self.from_y[:half], self.from_x[half:])
        return self.own

    def send(self, values):
        self.step += 1
        if self.step == 1:
            return over_z(values)
        if self.step == 2:
            return swap(values, 1), swap(values, 2)
        if self.step == 3:
            return swap(values[0], 1), swap(values[1], 2)
        return swap_core(values)

    def accept(self, out):
        if self.step == 1:
            self.group = out.reshape((-1,) + self.block.shape[1:])
        elif self.step == 2:
            self.from_x, self.from_y = out
        elif self.step == 3:
            self.own = join([self.group, self.from_x, self.from_y, *out])
        else:
            self.peer = out


class Exchange:
    def __init__(self, block, behind=False):
        self.block = block
        self.behind = behind
        self.step = 0

    def request(self):
        n = lax.axis_size("dp")
        if self.step == 1:
            return self.own
        return self.block if self.behind else jnp.broadcast_to(self.block[None], (n,) + self.block.shape)

    def send(self, values):
        self.step += 1
        if self.step == 2:
            return swap_core(values)
        if self.behind:
            self.own = lax.all_gather(values, "dp", axis=0, tiled=True)
            return None
        return lax.all_to_all(values, "dp", 0, 0, tiled=True)

    def accept(self, out):
        if self.step == 2:
            self.peer = out
        elif not self.behind:
            self.own = out.reshape(-1, out.shape[-1])


class Scatter:
    def __init__(self, peer, own=None, behind=False, wide=False, dtype=bf16):
        self.wide = wide
        self.dtype = dtype
        self.peer = peer
        self.own = own
        self.behind = behind
        self.step = 0 if peer is not None else 1

    def group(self, g, part=slice(None)):
        n = lax.axis_size("dp")
        shape = (4, n // 4, self.own.shape[0] // n) + self.own.shape[1:]
        total = self.own.reshape(shape)[g, part].astype(f32)
        if self.peer is not None:
            total = total + self.other.reshape(shape)[g, part].astype(f32)
        return total

    def request(self):
        if self.step == 0:
            return self.peer
        half = quarter() // 2
        low, high = slice(0, half), slice(half, None)
        if self.step == 1:
            values = (self.group(3, low), self.group(3, high))
        elif self.step == 2:
            values = (
                jnp.concatenate([self.group(1, low), self.group(1, high) + self.diagonal[1].astype(f32)]),
                jnp.concatenate([self.group(2, low) + self.diagonal[0].astype(f32), self.group(2, high)]),
            )
        else:
            values = self.group(0) + self.sides[0].astype(f32) + self.sides[1].astype(f32)
            if self.behind and self.wide:
                return values
        return jax.tree.map(lambda value: value.astype(self.dtype), values)

    def send(self, values):
        self.step += 1
        if self.step == 1:
            return swap_core(values)
        if self.step < 4:
            return swap(values[0], 1), swap(values[1], 2)
        if self.behind:
            self.total = sum_z(values).astype(f32)
            return None
        return over_z(values)

    def accept(self, out):
        if self.step == 1:
            self.other = out
        elif self.step == 2:
            self.diagonal = out
        elif self.step == 3:
            self.sides = out
        elif not self.behind:
            self.total = jnp.sum(out.astype(f32), axis=0)

    def result(self):
        return self.total


class Ticks:
    def __init__(self):
        self.last = []

    def wait(self, live=()):
        outs, live = barrier(([out for _, out in self.last], live))
        for (job, _), out in zip(self.last, outs):
            if out is not None:
                job.accept(out)
        self.last = []
        return live

    def __call__(self, jobs, live=()):
        values, live = barrier(([job.request() for job in jobs], live))
        self.last = [(job, job.send(value)) for job, value in zip(jobs, values)]
        return live


def small_gather(values):
    group = jnp.stack([values] + [swap(values, 4 * j) for j in range(1, quarter())])
    group = jnp.concatenate([group] + [swap(group, g) for g in (1, 2, 3)])
    apart = jnp.bitwise_xor(jnp.arange(4 * quarter(), dtype=jnp.int32), lax.axis_index("dp"))
    return jnp.take(group, (apart & 3) * quarter() + (apart >> 2), axis=0)


def total_over_all(values):
    count = lax.axis_size("dp") * lax.axis_size("mp")
    parts = jnp.broadcast_to(values[None], (count,) + values.shape)
    return jnp.sum(lax.all_to_all(parts, ("dp", "mp"), 0, 0, tiled=True), axis=0)


def place_of(index):
    apart = jnp.bitwise_xor(index, lax.axis_index("dp")) & 3
    return apart * quarter() + (index >> 2)


def layout(lengths):
    ends = jnp.cumsum(lengths)
    places = jnp.arange(LEN, dtype=jnp.int32)
    passed = places[:, None] >= ends[None, :]
    segment = jnp.sum(passed.astype(jnp.int32), axis=1)
    start = jnp.sum(jnp.where(passed, lengths[None, :], 0), axis=1)
    offset = places - start
    bounds = jnp.array(PYRAMID, dtype=jnp.int32)
    scale_id = jnp.sum((offset[:, None] >= bounds[None, :]).astype(jnp.int32), axis=1)
    usable = places < ends[-1]
    return (segment, scale_id, usable)


def matmul(left, right):
    return jnp.dot(left, right, preferred_element_type=f32)


def matmul_tn(left, right):
    return lax.dot_general(left, right, (((0,), (0,)), ((), ())), preferred_element_type=f32)


def matmul_nt(left, right):
    return lax.dot_general(left, right, (((1,), (1,)), ((), ())), preferred_element_type=f32)


def exact_tn(left, right):
    return lax.dot_general(
        left,
        right,
        (((0,), (0,)), ((), ())),
        precision=lax.Precision.HIGHEST,
        preferred_element_type=f32,
    )


def unit_pair(values):
    factor = lax.rsqrt(jnp.mean(values * values, axis=-1, keepdims=True) + EPSILON)
    return factor, (values * factor).astype(bf16)


def unit_back(values, factor, grad):
    inner = jnp.mean(grad * values, axis=-1, keepdims=True)
    return (factor * (grad - values * (factor * factor * inner))).astype(bf16)


def normed(values):
    centered = values - jnp.mean(values, axis=-1, keepdims=True)
    factor = lax.rsqrt(jnp.mean(centered * centered, axis=-1, keepdims=True) + EPSILON)
    return centered * factor, factor


def normed_back(hat, factor, grad):
    inner = jnp.mean(grad * hat, axis=-1, keepdims=True)
    return factor * (grad - jnp.mean(grad, axis=-1, keepdims=True) - hat * inner)


def spread(hot, part):
    high = part.astype(bf16).astype(f32)
    mid = (part - high).astype(bf16).astype(f32)
    low = part - high - mid
    return matmul(hot, jnp.concatenate([high, mid, low], axis=0).astype(bf16))


def item_sum(hot_t, values):
    high = values.astype(bf16)
    low = (values - high.astype(f32)).astype(bf16)
    return matmul(hot_t, high) + matmul(hot_t, low)


def flip(values):
    return values.astype(f32).T.astype(bf16)


def gelu_parts(values):
    inner = GELU_C * (values + 0.044715 * values * values * values)
    cdf = 0.5 * (1.0 + jnp.tanh(inner))
    return cdf, values * cdf


def gelu_slope(values, cdf):
    return cdf + values * (2.0 * cdf * (1.0 - cdf)) * (GELU_C * (1.0 + 0.134145 * values * values))


def whole(*shape):
    return pl.BlockSpec(shape, lambda *_: (0,) * len(shape), pipeline_mode=pl.Buffered(1))


def columns(rows, width):
    return pl.BlockSpec((rows, width), lambda i: (0, i))


def sds(shape, dtype):
    return jax.ShapeDtypeStruct(shape, dtype)


def kernel_call(body, grid, in_specs, out_specs, out_shape, flops, scratch=()):
    return pl.pallas_call(
        body,
        grid=grid,
        in_specs=in_specs,
        out_specs=out_specs,
        out_shape=out_shape,
        scratch_shapes=list(scratch),
        compiler_params=pltpu.CompilerParams(vmem_limit_bytes=VMEM_LIMIT),
        cost_estimate=pl.CostEstimate(flops=flops, transcendentals=0, bytes_accessed=2**24),
    )


def add_up(ref, part, start=None):
    first = pl.program_id(0) == 0

    @pl.when(first)
    def _():
        ref[...] = part if start is None else start[...] + part

    @pl.when(jnp.logical_not(first))
    def _():
        ref[...] += part


def at_end(fn):
    pl.when(pl.program_id(0) == pl.num_programs(0) - 1)(fn)


def embed_kernel(code_ref, own_ref, peer_ref, turn_ref, hot_ref, mod_ref, tok_ref, na_ref, na_t_ref, acc):
    step, steps = pl.program_id(0), pl.num_programs(0)
    rows = own_ref.shape[0]
    lane = lax.broadcasted_iota(jnp.int32, (LEN, rows), 1) + step * rows
    hot_own = (lane == code_ref[...]).astype(bf16)
    hot_peer = (lane + steps * rows == code_ref[...]).astype(bf16)
    add_up(acc, matmul(hot_own, own_ref[...]) + matmul(hot_peer, peer_ref[...]))

    @at_end
    def _():
        tokens = matmul(acc[...].astype(bf16), turn_ref[...])
        tok_ref[...] = tokens.astype(bf16)
        hat, _ = normed(tokens)
        out = hat * (1.0 + spread(hot_ref[...], mod_ref[:, :D])) + spread(hot_ref[...], mod_ref[:, D:])
        na_ref[...] = out.astype(bf16)
        na_t_ref[...] = flip(out)


def embed(code_rows, own, peer, turn, hot, mod):
    rows = own.shape[0]
    block = rows // 4
    rows_spec = pl.BlockSpec((block, D), lambda i: (i, 0))
    return kernel_call(
        embed_kernel,
        (4,),
        [whole(LEN, 1), rows_spec, rows_spec, whole(D, D), whole(LEN, 24), whole(ITEMS, 2 * D)],
        [whole(LEN, D), whole(LEN, D), whole(D, LEN)],
        [sds((LEN, D), bf16), sds((LEN, D), bf16), sds((D, LEN), bf16)],
        4 * LEN * rows * D,
        [pltpu.VMEM((LEN, D), f32)],
    )(code_rows, own, peer, turn, hot, mod)


def attend_pair(na_ref, w_ref, bias_ref):
    raw = matmul(na_ref[...], w_ref[:, : 3 * PAIR])
    outs = []
    for head in range(2):
        cut = [slice(i * PAIR + head * HEAD_WIDTH, i * PAIR + (head + 1) * HEAD_WIDTH) for i in range(3)]
        _, query_n = unit_pair(raw[:, cut[0]])
        _, key_n = unit_pair(raw[:, cut[1]])
        raised = jnp.exp(matmul_nt(query_n, key_n) * SCORE_SCALE + bias_ref[...])
        share = 1.0 / jnp.sum(raised, axis=-1, keepdims=True)
        outs.append(matmul((raised * share).astype(bf16), raw[:, cut[2]].astype(bf16)).astype(bf16))
    return jnp.concatenate(outs, axis=1)


def attend_first_kernel(na_ref, w_ref, bias_ref, out_ref, acc_ref):
    out = attend_pair(na_ref, w_ref, bias_ref)
    out_ref[...] = out
    add_up(acc_ref, matmul_nt(out, w_ref[:, 3 * PAIR :]))


def attend_last_kernel(
    na_ref, w_ref, bias_ref, part_ref, tok_ref, hot_ref, mod_ref, out_ref, acc_ref, mid_ref, nm_ref, nm_t_ref
):
    out = attend_pair(na_ref, w_ref, bias_ref)
    out_ref[...] = out
    add_up(acc_ref, matmul_nt(out, w_ref[:, 3 * PAIR :]), part_ref)

    @at_end
    def _():
        middle = tok_ref[...].astype(f32) + spread(hot_ref[...], mod_ref[:, :D]) * acc_ref[...]
        mid_ref[...] = middle
        hat, _ = normed(middle)
        out = hat * (1.0 + spread(hot_ref[...], mod_ref[:, D : 2 * D])) + spread(
            hot_ref[...], mod_ref[:, 2 * D :]
        )
        nm_ref[...] = out.astype(bf16)
        nm_t_ref[...] = flip(out)


def attend_first(na, w, bias):
    steps = w.shape[1] // (4 * PAIR)
    return kernel_call(
        attend_first_kernel,
        (steps,),
        [whole(LEN, D), columns(D, 4 * PAIR), whole(LEN, LEN)],
        [columns(LEN, PAIR), whole(LEN, D)],
        [sds((LEN, steps * PAIR), bf16), sds((LEN, D), f32)],
        steps * ATTEND_FLOPS,
    )(na, w, bias)


def attend_last(na, w, bias, part, tokens, hot, mod):
    steps = w.shape[1] // (4 * PAIR)
    return kernel_call(
        attend_last_kernel,
        (steps,),
        [
            whole(LEN, D),
            columns(D, 4 * PAIR),
            whole(LEN, LEN),
            whole(LEN, D),
            whole(LEN, D),
            whole(LEN, 24),
            whole(ITEMS, 3 * D),
        ],
        [columns(LEN, PAIR), whole(LEN, D), whole(LEN, D), whole(LEN, D), whole(D, LEN)],
        [
            sds((LEN, steps * PAIR), bf16),
            sds((LEN, D), f32),
            sds((LEN, D), f32),
            sds((LEN, D), bf16),
            sds((D, LEN), bf16),
        ],
        steps * ATTEND_FLOPS,
    )(na, w, bias, part, tokens, hot, mod)


def attend_pair_back(na_ref, na_t_ref, go_ref, go_t_ref, o_ref, w_ref, bias_ref, dw_ref):
    raw = matmul(na_ref[...], w_ref[:, : 3 * PAIR])
    grad_att = matmul(go_ref[...], w_ref[:, 3 * PAIR :]).astype(bf16)
    results = [[], [], []]
    for head in range(2):
        cut = [slice(i * PAIR + head * HEAD_WIDTH, i * PAIR + (head + 1) * HEAD_WIDTH) for i in range(3)]
        query, key = raw[:, cut[0]], raw[:, cut[1]]
        query_f, query_n = unit_pair(query)
        key_f, key_n = unit_pair(key)
        value_b = raw[:, cut[2]].astype(bf16)
        grad_out = grad_att[:, head * HEAD_WIDTH : (head + 1) * HEAD_WIDTH]
        grad_q, grad_k, grad_v = [], 0.0, 0.0
        for low, high in ((0, 384), (384, LEN)):
            raised = jnp.exp(matmul_nt(key_n, query_n[low:high]) * SCORE_SCALE + bias_ref[:, low:high])
            attention = raised * (1.0 / jnp.sum(raised, axis=0, keepdims=True))
            grad_probs = matmul_nt(value_b, grad_out[low:high])
            row_dot = jnp.sum(attention * grad_probs, axis=0, keepdims=True)
            grad_scores = (attention * (grad_probs - row_dot)).astype(bf16)
            grad_v = grad_v + matmul(attention.astype(bf16), grad_out[low:high])
            grad_k = grad_k + matmul(grad_scores, query_n[low:high])
            grad_q.append(matmul_tn(key_n, grad_scores).T)
        grad_q = jnp.concatenate(grad_q, axis=0) * SCORE_SCALE
        results[0].append(unit_back(query, query_f, grad_q))
        results[1].append(unit_back(key, key_f, grad_k * SCORE_SCALE))
        results[2].append(grad_v.astype(bf16))
    grad_raw = jnp.concatenate([part for pair in results for part in pair], axis=1)
    dw_ref[:, : 3 * PAIR] = matmul(na_t_ref[...], grad_raw).astype(bf16)
    dw_ref[:, 3 * PAIR :] = matmul(go_t_ref[...], o_ref[...]).astype(bf16)
    return matmul_nt(grad_raw, w_ref[:, : 3 * PAIR])


def attend_back_first_kernel(na_ref, na_t_ref, go_ref, go_t_ref, o_ref, w_ref, bias_ref, dw_ref, acc_ref):
    add_up(acc_ref, attend_pair_back(na_ref, na_t_ref, go_ref, go_t_ref, o_ref, w_ref, bias_ref, dw_ref))


def attend_back_last_kernel(
    na_ref, na_t_ref, go_ref, go_t_ref, o_ref, w_ref, bias_ref,
    part_ref, tok_ref, gm_ref, hot_ref, hot_t_ref, mod_ref,
    dw_ref, gt_ref, items_ref, acc_ref,
):
    part = attend_pair_back(na_ref, na_t_ref, go_ref, go_t_ref, o_ref, w_ref, bias_ref, dw_ref)
    add_up(acc_ref, part, part_ref)

    @at_end
    def _():
        grad = acc_ref[...]
        hat, factor = normed(tok_ref[...].astype(f32))
        items_ref[:, :D] = item_sum(hot_t_ref[...], grad * hat)
        items_ref[:, D:] = item_sum(hot_t_ref[...], grad)
        inner = normed_back(hat, factor, grad * (1.0 + spread(hot_ref[...], mod_ref[...])))
        gt_ref[...] = (gm_ref[...] + inner).astype(bf16)


def attend_back_specs():
    return [
        whole(LEN, D),
        whole(D, LEN),
        whole(LEN, D),
        whole(D, LEN),
        columns(LEN, PAIR),
        columns(D, 4 * PAIR),
        whole(LEN, LEN),
    ]


def attend_back_first(na, na_t, go, go_t, out, w, bias_t):
    steps = w.shape[1] // (4 * PAIR)
    return kernel_call(
        attend_back_first_kernel,
        (steps,),
        attend_back_specs(),
        [columns(D, 4 * PAIR), whole(LEN, D)],
        [sds(w.shape, bf16), sds((LEN, D), f32)],
        3 * steps * ATTEND_FLOPS,
    )(na, na_t, go, go_t, out, w, bias_t)


def attend_back_last(na, na_t, go, go_t, out, w, bias_t, part, tokens, grad_middle, hot, hot_t, mod):
    steps = w.shape[1] // (4 * PAIR)
    return kernel_call(
        attend_back_last_kernel,
        (steps,),
        attend_back_specs()
        + [
            whole(LEN, D),
            whole(LEN, D),
            whole(LEN, D),
            whole(LEN, 24),
            whole(2 * ITEMS, LEN),
            whole(ITEMS, D),
        ],
        [columns(D, 4 * PAIR), whole(LEN, D), whole(2 * ITEMS, 2 * D)],
        [sds(w.shape, bf16), sds((LEN, D), bf16), sds((2 * ITEMS, 2 * D), f32)],
        3 * steps * ATTEND_FLOPS,
        [pltpu.VMEM((LEN, D), f32)],
    )(na, na_t, go, go_t, out, w, bias_t, part, tokens, grad_middle, hot, hot_t, mod)


def mlp_part(nm_ref, w_refs, h_refs):
    total = 0.0
    for w_ref, h_ref in zip(w_refs, h_refs):
        hidden = matmul(nm_ref[...], w_ref[:, :BLOCK])
        h_ref[...] = hidden
        _, active = gelu_parts(hidden)
        total = total + matmul_nt(active.astype(bf16), w_ref[:, BLOCK:])
    return total


def mlp_first_kernel(nm_ref, w0_ref, w1_ref, h0_ref, h1_ref, acc_ref):
    add_up(acc_ref, mlp_part(nm_ref, (w0_ref, w1_ref), (h0_ref, h1_ref)))


def mlp_last_kernel(
    nm_ref, w0_ref, w1_ref, part_ref, mid_ref, hot_ref, mod_ref, h0_ref, h1_ref, acc_ref, res_ref, nh_ref, nh_t_ref
):
    add_up(acc_ref, mlp_part(nm_ref, (w0_ref, w1_ref), (h0_ref, h1_ref)), part_ref)

    @at_end
    def _():
        residual = mid_ref[...] + spread(hot_ref[...], mod_ref[...]) * acc_ref[...]
        res_ref[...] = residual
        hat, _ = normed(residual)
        nh_ref[...] = hat.astype(bf16)
        nh_t_ref[...] = flip(hat)


def mlp_first(nm, ws):
    steps = ws[0].shape[1] // (2 * BLOCK)
    hidden = sds((LEN, steps * BLOCK), f32)
    *hiddens, acc = kernel_call(
        mlp_first_kernel,
        (steps,),
        [whole(LEN, D)] + [columns(D, 2 * BLOCK)] * 2,
        [columns(LEN, BLOCK)] * 2 + [whole(LEN, D)],
        [hidden, hidden, sds((LEN, D), f32)],
        8 * steps * LEN * D * BLOCK,
    )(nm, *ws)
    return hiddens, acc


def mlp_last(nm, ws, part, middle, hot, mod):
    steps = ws[0].shape[1] // (2 * BLOCK)
    hidden = sds((LEN, steps * BLOCK), f32)
    h0, h1, *rest = kernel_call(
        mlp_last_kernel,
        (steps,),
        [whole(LEN, D)]
        + [columns(D, 2 * BLOCK)] * 2
        + [whole(LEN, D), whole(LEN, D), whole(LEN, 24), whole(ITEMS, D)],
        [columns(LEN, BLOCK)] * 2 + [whole(LEN, D), whole(LEN, D), whole(LEN, D), whole(D, LEN)],
        [
            hidden,
            hidden,
            sds((LEN, D), f32),
            sds((LEN, D), f32),
            sds((LEN, D), bf16),
            sds((D, LEN), bf16),
        ],
        8 * steps * LEN * D * BLOCK,
    )(nm, *ws, part, middle, hot, mod)
    return [h0, h1], *rest


def mlp_part_back(nm_t_ref, g_ref, g_t_ref, h_refs, w_refs, dw_ref):
    total = 0.0
    for i, (h_ref, w_ref) in enumerate(zip(h_refs, w_refs)):
        hidden = h_ref[...]
        cdf, active = gelu_parts(hidden)
        at = 2 * i * BLOCK
        dw_ref[:, at + BLOCK : at + 2 * BLOCK] = matmul(g_t_ref[...], active.astype(bf16)).astype(bf16)
        grad_pre = (gelu_slope(hidden, cdf) * matmul(g_ref[...], w_ref[:, BLOCK:])).astype(bf16)
        dw_ref[:, at : at + BLOCK] = matmul(nm_t_ref[...], grad_pre).astype(bf16)
        total = total + matmul_nt(grad_pre, w_ref[:, :BLOCK])
    return total


def mlp_back_first_kernel(nm_t_ref, g_ref, g_t_ref, h0_ref, h1_ref, w0_ref, w1_ref, dw_ref, acc_ref):
    add_up(acc_ref, mlp_part_back(nm_t_ref, g_ref, g_t_ref, (h0_ref, h1_ref), (w0_ref, w1_ref), dw_ref))


def mlp_back_last_kernel(
    nm_t_ref, g_ref, g_t_ref, h0_ref, h1_ref, w0_ref, w1_ref,
    part_ref, mid_ref, gr_ref, out_ref, hot_ref, hot_t_ref, mod_ref,
    dw_ref, gm_ref, go_ref, go_t_ref, items_ref, acc_ref,
):
    part = mlp_part_back(nm_t_ref, g_ref, g_t_ref, (h0_ref, h1_ref), (w0_ref, w1_ref), dw_ref)
    add_up(acc_ref, part, part_ref)

    @at_end
    def _():
        grad = acc_ref[...]
        hat, factor = normed(mid_ref[...])
        items_ref[:, D : 2 * D] = item_sum(hot_t_ref[...], grad * hat)
        items_ref[:, 2 * D :] = item_sum(hot_t_ref[...], grad)
        grad_middle = gr_ref[...] + normed_back(
            hat, factor, grad * (1.0 + spread(hot_ref[...], mod_ref[:, D:]))
        )
        gm_ref[...] = grad_middle
        items_ref[:, :D] = item_sum(hot_t_ref[...], grad_middle * out_ref[...])
        grad_out = spread(hot_ref[...], mod_ref[:, :D]) * grad_middle
        go_ref[...] = grad_out.astype(bf16)
        go_t_ref[...] = flip(grad_out)


def mlp_back_specs():
    return (
        [whole(D, LEN), whole(LEN, D), whole(D, LEN)]
        + [columns(LEN, BLOCK)] * 2
        + [columns(D, 2 * BLOCK)] * 2
    )


def mlp_back_first(nm_t, g, g_t, hiddens, ws):
    steps = ws[0].shape[1] // (2 * BLOCK)
    return kernel_call(
        mlp_back_first_kernel,
        (steps,),
        mlp_back_specs(),
        [columns(D, 4 * BLOCK), whole(LEN, D)],
        [sds((D, 4 * steps * BLOCK), bf16), sds((LEN, D), f32)],
        16 * steps * LEN * D * BLOCK,
    )(nm_t, g, g_t, *hiddens, *ws)


def mlp_back_last(nm_t, g, g_t, hiddens, ws, part, middle, grad_res, attn_out, hot, hot_t, mod):
    steps = ws[0].shape[1] // (2 * BLOCK)
    return kernel_call(
        mlp_back_last_kernel,
        (steps,),
        mlp_back_specs()
        + [whole(LEN, D)] * 4
        + [whole(LEN, 24), whole(2 * ITEMS, LEN), whole(ITEMS, 2 * D)],
        [
            columns(D, 4 * BLOCK),
            whole(LEN, D),
            whole(LEN, D),
            whole(D, LEN),
            whole(2 * ITEMS, 3 * D),
        ],
        [
            sds((D, 4 * steps * BLOCK), bf16),
            sds((LEN, D), f32),
            sds((LEN, D), bf16),
            sds((D, LEN), bf16),
            sds((2 * ITEMS, 3 * D), f32),
        ],
        16 * steps * LEN * D * BLOCK,
        [pltpu.VMEM((LEN, D), f32)],
    )(nm_t, g, g_t, *hiddens, *ws, part, middle, grad_res, attn_out, hot, hot_t, mod)


def head_kernel(
    nh_ref, nh_t_ref, own_ref, peer_ref, target_ref, weight_ref, res_ref, mlp_ref, hot_ref, hot_t_ref, mod_ref,
    dw_own_ref, dw_peer_ref, loss_ref, gr_ref, gmo_ref, gmo_t_ref, items_ref,
    logits, most, total, chosen, acc,
):
    step = pl.program_id(0)
    half = pl.num_programs(0) // 2
    block = own_ref.shape[1]
    lane = lax.broadcasted_iota(jnp.int32, (LEN, block), 1)

    @pl.when(step == 0)
    def _():
        most[...] = jnp.full((LEN, 1), -1e30, f32)
        total[...] = jnp.zeros((LEN, 1), f32)
        chosen[...] = jnp.zeros((LEN, 1), f32)

    for which, w_ref, dw_ref in ((0, own_ref, dw_own_ref), (1, peer_ref, dw_peer_ref)):

        @pl.when(step < half)
        def _():
            place = step + which * half
            values = matmul(nh_ref[...], w_ref[...])
            logits[place] = values
            most_new = jnp.maximum(most[...], jnp.max(values, axis=1, keepdims=True))
            total[...] = total[...] * jnp.exp(most[...] - most_new) + jnp.sum(
                jnp.exp(values - most_new), axis=1, keepdims=True
            )
            most[...] = most_new
            is_target = lane + place * block == target_ref[...]
            chosen[...] += jnp.sum(jnp.where(is_target, values, 0.0), axis=1, keepdims=True)

    @pl.when(step == half - 1)
    def _():
        most[...] = most[...] + jnp.log(total[...])
        loss = jnp.sum(weight_ref[...] * (most[...] - chosen[...]), axis=0, keepdims=True)
        loss_ref[...] = jnp.broadcast_to(loss, (8, 128))

    for which, w_ref, dw_ref in ((0, own_ref, dw_own_ref), (1, peer_ref, dw_peer_ref)):

        @pl.when(step >= half)
        def _():
            place = step - half + which * half
            is_target = lane + place * block == target_ref[...]
            grad = (jnp.exp(logits[place] - most[...]) - is_target.astype(f32)) * weight_ref[...]
            grad = grad.astype(bf16)
            dw_ref[...] = matmul(nh_t_ref[...], grad).astype(bf16)
            part = matmul_nt(grad, w_ref[...])

            @pl.when(jnp.logical_and(step == half, which == 0))
            def _():
                acc[...] = part

            @pl.when(jnp.logical_not(jnp.logical_and(step == half, which == 0)))
            def _():
                acc[...] += part

    @at_end
    def _():
        hat, factor = normed(res_ref[...])
        grad_res = normed_back(hat, factor, acc[...])
        gr_ref[...] = grad_res
        items_ref[...] = item_sum(hot_t_ref[...], grad_res * mlp_ref[...])
        grad_mlp = spread(hot_ref[...], mod_ref[...]) * grad_res
        gmo_ref[...] = grad_mlp.astype(bf16)
        gmo_t_ref[...] = flip(grad_mlp)


def head(nh, nh_t, own, peer, target, weight, residual, mlp_out, hot, hot_t, mod):
    half = own.shape[1] // BLOCK
    w_spec = pl.BlockSpec((D, BLOCK), lambda i: (0, i % half))
    dw_spec = pl.BlockSpec((D, BLOCK), lambda i: (0, jnp.maximum(i - half, 0)))
    return kernel_call(
        head_kernel,
        (2 * half,),
        [
            whole(LEN, D),
            whole(D, LEN),
            w_spec,
            w_spec,
            whole(LEN, 1),
            whole(LEN, 1),
            whole(LEN, D),
            whole(LEN, D),
            whole(LEN, 24),
            whole(2 * ITEMS, LEN),
            whole(ITEMS, D),
        ],
        [
            dw_spec,
            dw_spec,
            whole(8, 128),
            whole(LEN, D),
            whole(LEN, D),
            whole(D, LEN),
            whole(2 * ITEMS, D),
        ],
        [
            sds(own.shape, bf16),
            sds(own.shape, bf16),
            sds((8, 128), f32),
            sds((LEN, D), f32),
            sds((LEN, D), bf16),
            sds((D, LEN), bf16),
            sds((2 * ITEMS, D), f32),
        ],
        12 * half * LEN * D * BLOCK,
        [
            pltpu.VMEM((2 * half, LEN, BLOCK), f32),
            pltpu.VMEM((LEN, 1), f32),
            pltpu.VMEM((LEN, 1), f32),
            pltpu.VMEM((LEN, 1), f32),
            pltpu.VMEM((LEN, D), f32),
        ],
    )(nh, nh_t, own, peer, target, weight, residual, mlp_out, hot, hot_t, mod)


def code_first_kernel(code_ref, gt_ref, turn_ref, out_ref, flat_ref):
    step, steps = pl.program_id(0), pl.num_programs(0)
    rows = out_ref.shape[0]

    @pl.when(step == 0)
    def _():
        flat_ref[...] = matmul_nt(gt_ref[...], turn_ref[...]).astype(bf16)

    row = lax.broadcasted_iota(jnp.int32, (rows, LEN), 0) + (step + steps) * rows
    out_ref[...] = matmul((row == code_ref[...]).astype(bf16), flat_ref[...]).astype(bf16)


def code_last_kernel(code_ref, flat_ref, out_ref):
    rows = out_ref.shape[0]
    row = lax.broadcasted_iota(jnp.int32, (rows, LEN), 0) + pl.program_id(0) * rows
    out_ref[...] = matmul((row == code_ref[...]).astype(bf16), flat_ref[...]).astype(bf16)


def code_back_first(code_rows, grad_tokens, turn, rows):
    spec = pl.BlockSpec((rows // 4, D), lambda i: (i, 0))
    out, flat = kernel_call(
        code_first_kernel,
        (4,),
        [whole(1, LEN), whole(LEN, D), whole(D, D)],
        [spec, whole(LEN, D)],
        [sds((rows, D), bf16), sds((LEN, D), bf16)],
        2 * LEN * rows * D,
    )(code_rows, grad_tokens, turn)
    return code_rows, flat, out


def code_back_last(code_rows, flat, rows):
    spec = pl.BlockSpec((rows // 4, D), lambda i: (i, 0))
    return kernel_call(
        code_last_kernel,
        (4,),
        [whole(1, LEN), whole(LEN, D)],
        spec,
        sds((rows, D), bf16),
        2 * LEN * rows * D,
    )(code_rows, flat)


def step_rates():
    return (
        2.5,
        2.5,
        2.5 / math.sqrt(D),
        2.5 / math.sqrt(D),
        2.5 / math.sqrt(D // 32),
        2.5 / math.sqrt(D),
        2.5 / math.sqrt(FF),
        5.0 / math.sqrt(D),
    )


def adamw_update(weight, grad, moment, square, rate):
    first = BETA_ONE * moment + (1.0 - BETA_ONE) * grad
    second = BETA_TWO * square + (1.0 - BETA_TWO) * grad * grad
    corrected = (
        first / (1.0 - BETA_ONE**STEP) / (jnp.sqrt(second / (1.0 - BETA_TWO**STEP)) + ADAM_EPSILON)
    )
    return (first, second, weight - rate * (corrected + DECAY * weight))


def on_device(
    input_codes,
    target_codes,
    item_lengths,
    item_labels,
    code_table,
    class_table,
    adaln_weight,
    qkv_weight,
    proj_weight,
    expand_weight,
    contract_weight,
    head_weight,
    code_moment,
    class_moment,
    adaln_moment,
    qkv_moment,
    proj_moment,
    expand_moment,
    contract_moment,
    head_moment,
    code_square,
    class_square,
    adaln_square,
    qkv_square,
    proj_square,
    expand_square,
    contract_square,
    head_square,
):
    masters = (
        code_table,
        class_table,
        adaln_weight,
        qkv_weight,
        proj_weight.T,
        expand_weight,
        contract_weight.T,
        head_weight,
    )
    moments = (
        code_moment,
        class_moment,
        adaln_moment,
        qkv_moment,
        proj_moment.T,
        expand_moment,
        contract_moment.T,
        head_moment,
    )
    squares = (
        code_square,
        class_square,
        adaln_square,
        qkv_square,
        proj_square.T,
        expand_square,
        contract_square.T,
        head_square,
    )
    n = lax.axis_size("dp")
    core = lax.axis_index("mp")
    rows = code_table.shape[0]
    half_rows = rows // 2
    width = proj_weight.shape[0]
    wide = expand_weight.shape[1]
    codes_local = head_weight.shape[1]

    def mine(values):
        return lax.dynamic_index_in_dim(values, core, 0, keepdims=False)

    pairs = width // PAIR
    code_block = lax.dynamic_slice_in_dim(code_table, core * half_rows, half_rows, 0).astype(bf16)
    attn_block = jnp.stack([qkv_weight[0], qkv_weight[1], qkv_weight[2], proj_weight.T], axis=1)
    attn_block = attn_block.reshape(-1, 4, pairs, PAIR).swapaxes(1, 2).reshape(-1, 4 * width)
    blocks = wide // BLOCK
    mlp_blocks = jnp.stack(
        [expand_weight.reshape(-1, blocks, BLOCK), contract_weight.T.reshape(-1, blocks, BLOCK)], axis=2
    ).astype(bf16)
    code_w, attn_w, mlp_a, mlp_b, head_w = [
        Gather(block)
        for block in (
            code_block,
            attn_block.astype(bf16),
            mlp_blocks[:, 0::2].reshape(-1, wide),
            mlp_blocks[:, 1::2].reshape(-1, wide),
            head_weight.astype(bf16),
        )
    ]
    begin = Ticks()
    begin([code_w])
    numbers = small_gather(jnp.stack([item_lengths[:, 0], item_labels[:, 0]], axis=1))
    positions = jnp.arange(n, dtype=jnp.int32)
    block_at = ((lax.axis_index("dp") & 3) ^ (positions // quarter())) + 4 * (positions % quarter())
    block_place = place_of(positions)
    labels = numbers[:, :, 1]
    labels_own = jnp.where(core == 0, labels[:, 0], labels[:, 1])
    labels_peer = jnp.where(core == 0, labels[:, 1], labels[:, 0])
    class_low = class_table.astype(bf16)
    adaln_low = adaln_weight.astype(bf16)

    def class_part(item_labels):
        ids = jnp.arange(CLASSES, dtype=jnp.int32)
        picked = (item_labels.reshape(-1, 1) == ids[None, :]).astype(bf16)
        class_rows = matmul(picked, class_low)
        return picked, class_rows, jax.nn.silu(class_rows).astype(bf16)

    _, _, class_vec = class_part(labels_own[block_at])
    order = (2, 4, 0, 1, 3, 5)
    adaln_parts = jnp.concatenate([adaln_low[:, i * D : (i + 1) * D] for i in order], axis=1)

    mod_parts = matmul(class_vec, adaln_parts)

    mod_job = Scatter(None, mod_parts, dtype=f32)
    attn_w.block, mod_job.own = begin.wait((attn_w.block, mod_job.own))
    begin([code_w, attn_w, mod_job])
    mlp_a.block = begin.wait(mlp_a.block)
    begin([code_w, mlp_a, mod_job])
    begin.wait()
    begin([code_w, attn_w, mod_job])
    begin.wait()

    lengths = mine(item_lengths)[0]
    code_ids = mine(input_codes)[0]
    target_ids = mine(target_codes)[0]
    segment, scale_id, usable = layout(lengths)
    bounds = jnp.array((0,) + PYRAMID, dtype=jnp.int32)
    sizes = jnp.array(PYRAMID + (LEN,), dtype=jnp.int32) - bounds
    all_lengths = numbers[:, :, 0].reshape(-1)
    scale_counts = jnp.sum(
        jnp.clip(all_lengths[:, None] - bounds[None, :], 0, sizes[None, :]), axis=0
    ).astype(f32)
    inv_counts = 1.0 / (NSCALES * jnp.maximum(scale_counts, 1.0))
    scale_hot = scale_id[:, None] == jnp.arange(NSCALES, dtype=jnp.int32)[None, :]
    token_weight = jnp.where(
        usable, jnp.sum(jnp.where(scale_hot, inv_counts[None, :], 0.0), axis=1), 0.0
    )
    same = segment[:, None] == segment[None, :]
    bias = jnp.where(same & (scale_id[None, :] <= scale_id[:, None]), 0.0, -1e30)
    bias_t = jnp.where(same & (scale_id[:, None] <= scale_id[None, :]), 0.0, -1e30)
    hot = (segment[:, None] == jnp.arange(3 * ITEMS, dtype=jnp.int32)[None, :] % ITEMS).astype(bf16)
    item_rows = jnp.arange(2 * ITEMS, dtype=jnp.int32)
    hot_t = ((segment[None, :] == item_rows[:, None]) & (item_rows[:, None] < ITEMS)).astype(bf16)

    block_width = D // n
    feature_place = (block_place[:, None] * block_width + jnp.arange(block_width)[None, :]).reshape(-1)
    turn = (feature_place[:, None] == jnp.arange(D, dtype=jnp.int32)[None, :]).astype(bf16)
    within = code_ids % rows
    other = (within // half_rows != core).astype(jnp.int32)
    code_rows = other * (n * half_rows) + place_of(code_ids // rows) * half_rows + within % half_rows
    target = jnp.where(target_ids // codes_local == core, 0, codes_local) + target_ids % codes_local

    def placed(values):
        values = values.reshape(-1, n, block_width)
        return jnp.take(values, block_at, axis=1).reshape(ITEMS, -1)

    def beside(*parts):
        return jnp.concatenate(parts, axis=1)

    mods_embed = placed(mod_job.total[:, : 2 * D])
    scale_attn = mods_embed[:, :D]
    code_col = code_rows.reshape(LEN, 1)

    code_own, code_peer, code_col = begin(
        [attn_w, mlp_a, mlp_b], (code_w.own, code_w.peer, code_col)
    )
    tokens, na, na_t = begin.wait(embed(code_col, code_own, code_peer, turn, hot, mods_embed))
    na = begin([attn_w, mlp_a, mlp_b, head_w], na)
    att_own, part = begin.wait(attend_first(na, attn_w.own, bias))
    mods = placed(mod_job.total[:, 2 * D :])
    gate_attn, gate_mlp, scale_mlp, shift_mlp = jnp.split(mods, 4, axis=1)
    mods_attend = beside(gate_attn, scale_mlp, shift_mlp)
    mods_back = beside(gate_attn, scale_mlp)
    part = begin([mlp_a, mlp_b, head_w], part)
    att_peer, attn_out, middle, nm, nm_t = begin.wait(
        attend_last(na, attn_w.peer, bias, part, tokens, hot, mods_attend)
    )
    nm = begin([mlp_b, head_w], nm)
    mlp_own = (mlp_a.own, mlp_b.own)
    hidden_own, part = begin.wait(mlp_first(nm, mlp_own))
    mlp_peer = (mlp_a.peer, mlp_b.peer)
    part = begin([head_w], part)
    hidden_peer, mlp_out, residual, nh, nh_t = begin.wait(
        mlp_last(nm, mlp_peer, part, middle, hot, gate_mlp)
    )
    dhead_own, dhead_peer, loss_tile, grad_res, gmo, gmo_t, items_head = head(
        nh, nh_t, head_w.own, head_w.peer, target.reshape(LEN, 1), token_weight.reshape(LEN, 1),
        residual, mlp_out, hot, hot_t, gate_mlp,
    )
    loss_local = loss_tile[0, 0]

    def turned(parts):
        values = beside(*parts)
        values = jnp.take(values.reshape(-1, n, block_width), block_place, axis=1)
        return values.reshape(ITEMS, -1).astype(bf16)

    head_job = Scatter(dhead_peer, dhead_own, behind=True, wide=True)
    gmo = begin([head_job], gmo)
    dmlp_peer, part = begin.wait(mlp_back_first(nm_t, gmo, gmo_t, hidden_peer, mlp_peer))
    mlp_job = Scatter(dmlp_peer, behind=True)
    part = begin([head_job, mlp_job], part)
    mlp_job.own, grad_middle, gao, gao_t, items_mlp = begin.wait(
        mlp_back_last(
            nm_t, gmo, gmo_t, hidden_own, mlp_own, part, middle, grad_res, attn_out, hot, hot_t, mods_back
        )
    )
    item_job = Exchange(turned([items_mlp[:ITEMS, :D], items_head[:ITEMS], items_mlp[:ITEMS, D:]]), behind=True)
    gao = begin([head_job, mlp_job, item_job], gao)
    dattn_peer, part = begin.wait(attend_back_first(na, na_t, gao, gao_t, att_peer, attn_w.peer, bias_t))
    attn_job = Scatter(dattn_peer)
    part = begin([head_job, mlp_job, attn_job], part)
    attn_job.own, grad_tokens, items_attn = begin.wait(
        attend_back_last(
            na, na_t, gao, gao_t, att_own, attn_w.own, bias_t, part, tokens, grad_middle, hot, hot_t, scale_attn
        )
    )
    late_job = Exchange(turned([items_attn[:ITEMS]]))
    grad_tokens = begin([attn_job, late_job, mlp_job], grad_tokens)
    code_row, flat, dcode_peer = begin.wait(
        code_back_first(code_rows.reshape(1, LEN), grad_tokens, turn, n * half_rows)
    )
    code_job = Scatter(dcode_peer)
    flat = begin([code_job, attn_job], flat)
    code_job.own = begin.wait(code_back_last(code_row, flat, n * half_rows))
    begin([code_job, item_job, late_job])
    begin.wait()
    begin([code_job, attn_job])
    begin.wait()
    head_job.total, mlp_job.total = begin([code_job], (head_job.total, mlp_job.total))
    begin.wait()

    def factor_part(item_labels, grads):
        picked, class_rows, class_vec = class_part(item_labels)
        grad_class_vec = matmul_nt(grads, adaln_low)
        _, silu_back = jax.vjp(jax.nn.silu, class_rows)
        return matmul_tn(class_vec, grads), exact_tn(picked.astype(f32), silu_back(grad_class_vec)[0])

    def grad_rows(which):
        early, late = getattr(item_job, which), getattr(late_job, which)
        order = [early[:, : 2 * D], late[:, :D], early[:, 2 * D : 3 * D], late[:, D:], early[:, 3 * D :]]
        return beside(*order)

    adaln_a, class_a = factor_part(labels_own, grad_rows("own"))
    adaln_b, class_b = factor_part(labels_peer, grad_rows("peer"))
    adaln_grad = adaln_a + adaln_b
    class_grad = class_a + class_b
    code_half = code_job.result()
    code_other = swap_core(code_half)
    code_grad = jnp.where(
        core == 0,
        jnp.concatenate([code_half, code_other]),
        jnp.concatenate([code_other, code_half]),
    )
    attn_grad = attn_job.result()
    kinds = attn_grad.reshape(-1, pairs, 4, PAIR).transpose(2, 0, 1, 3).reshape(4, -1, width)
    mlp_kinds = mlp_job.result().reshape(-1, blocks, 2, BLOCK)
    gradients = (
        code_grad,
        class_grad,
        adaln_grad,
        kinds[:3],
        kinds[3],
        mlp_kinds[:, :, 0].reshape(-1, wide),
        mlp_kinds[:, :, 1].reshape(-1, wide),
        head_job.result(),
    )
    shared_sq = jnp.sum(class_grad * class_grad) + jnp.sum(adaln_grad * adaln_grad)
    own_sq = jnp.sum(code_half * code_half) + jnp.sum(attn_grad * attn_grad)
    for grad in gradients[5:]:
        own_sq = own_sq + jnp.sum(grad * grad)
    totals = total_over_all(
        jnp.concatenate([(own_sq + 0.5 * shared_sq).reshape(1), loss_local.reshape(1)])
    )
    squared, loss = totals[0], totals[1]
    grad_norm = jnp.sqrt(squared)
    clip = jnp.minimum(1.0, CLIP_NORM / (grad_norm + 1e-06))
    firsts, seconds, updated = ([], [], [])
    for place, (weight, grad, moment, square, rate) in enumerate(
        zip(masters, gradients, moments, squares, step_rates())
    ):
        for kept, value in zip(
            (firsts, seconds, updated), adamw_update(weight, grad * clip, moment, square, rate)
        ):
            kept.append(value.T if place in (4, 6) else value)
    return (*firsts, *seconds, *updated, loss, scale_counts, grad_norm)


def solution(mesh):
    token_spec = P(None, "dp", None)
    weight_specs = (
        P("dp", None),
        P(None, "dp"),
        P("dp", None),
        P(None, "dp", "mp"),
        P("mp", "dp"),
        P("dp", "mp"),
        P("mp", "dp"),
        P("dp", "mp"),
    )
    return jax.shard_map(
        on_device,
        mesh=mesh,
        in_specs=(token_spec,) * 4 + weight_specs * 3,
        out_specs=weight_specs * 3 + (P(), P(), P()),
        check_vma=False,
    )
```

```python
import math

import jax
import jax.numpy as jnp
from jax import lax
from jax.experimental import pallas as pl
from jax.experimental.pallas import tpu as pltpu
from jax.sharding import PartitionSpec as P

D = 1024
HEAD_WIDTH = 64
FF = 4096
CLASSES = 1000
LEN = 800
ITEMS = 8
NSCALES = 10
MICRO = 2
STEP = 10


EPSILON = 1e-06
SOFTMAX_WARMTH = 12.0
CLIP_NORM = 0.001
BETA_ONE = 0.9
BETA_TWO = 0.95
DECAY = 0.05
ADAM_EPSILON = 1e-08
PYRAMID = (1, 5, 14, 30, 55, 91, 155, 255, 424)

SCORE_SCALE = SOFTMAX_WARMTH / HEAD_WIDTH
SCORE_POWER = SCORE_SCALE * math.log2(math.e)
GELU_C = math.sqrt(2.0 / math.pi)
PAIR = 2 * HEAD_WIDTH
BLOCK = 512
JOIN_BLOCK = 1024
ATTEND_FLOPS = LEN * PAIR * (8 * D + 4 * LEN)
VMEM_LIMIT = 60 * 2**20

bf16 = jnp.bfloat16
f32 = jnp.float32
barrier = lax.optimization_barrier


def swap(values, bits):
    n = lax.axis_size("dp")
    return lax.ppermute(values, "dp", [(i, i ^ bits) for i in range(n)])


def swap_core(values):
    return lax.ppermute(values, "mp", [(0, 1), (1, 0)])


def quarter():
    return lax.axis_size("dp") // 4


def columns_of_chips():
    n = lax.axis_size("dp")
    return [[xy + 4 * z for z in range(n // 4)] for xy in range(4)]


def over_z(values):
    return lax.all_to_all(values, "dp", 0, 0, tiled=True, axis_index_groups=columns_of_chips())


def sum_z(values):
    return lax.psum_scatter(values, "dp", scatter_dimension=0, axis_index_groups=columns_of_chips())


def join_kernel(*refs):
    parts, out = refs[:-1], refs[-1]
    at = 0
    for part in parts:
        rows = part.shape[0]
        out[at : at + rows, :] = part[...]
        at += rows


def join(parts):
    rows = sum(part.shape[0] for part in parts)
    total = parts[0].shape[1]
    return pl.pallas_call(
        join_kernel,
        grid=(total // JOIN_BLOCK,),
        in_specs=[pl.BlockSpec((part.shape[0], JOIN_BLOCK), lambda i: (0, i)) for part in parts],
        out_specs=pl.BlockSpec((rows, JOIN_BLOCK), lambda i: (0, i)),
        out_shape=jax.ShapeDtypeStruct((rows, total), parts[0].dtype),
    )(*parts)


class Gather:
    def __init__(self, block, behind=False):
        self.block = block
        self.behind = behind
        self.step = 0

    def request(self):
        if self.step == 0 and self.behind:
            return self.block
        if self.step == 0:
            return jnp.broadcast_to(self.block[None], (quarter(),) + self.block.shape)
        if self.step == 1:
            return self.group
        if self.step == 2:
            half = self.group.shape[0] // 2
            return (self.from_y[:half], self.from_x[half:])
        return self.own

    def send(self, values):
        self.step += 1
        if self.step == 1 and self.behind:
            self.group = lax.all_gather(values, "dp", axis=0, tiled=True, axis_index_groups=columns_of_chips())
            return None
        if self.step == 1:
            return over_z(values)
        if self.step == 2:
            return swap(values, 1), swap(values, 2)
        if self.step == 3:
            return swap(values[0], 1), swap(values[1], 2)
        return swap_core(values)

    def accept(self, out):
        if out is None:
            return
        if self.step == 1:
            self.group = out.reshape((-1,) + self.block.shape[1:])
        elif self.step == 2:
            self.from_x, self.from_y = out
        elif self.step == 3:
            self.own = join([self.group, self.from_x, self.from_y, *out])
        else:
            self.peer = out


class Exchange:
    def __init__(self, block, behind=False):
        self.block = block
        self.behind = behind
        self.step = 0

    def request(self):
        n = lax.axis_size("dp")
        if self.step == 1:
            return self.own
        return self.block if self.behind else jnp.broadcast_to(self.block[None], (n,) + self.block.shape)

    def send(self, values):
        self.step += 1
        if self.step == 2:
            return swap_core(values)
        if self.behind:
            self.own = lax.all_gather(values, "dp", axis=0, tiled=True)
            return None
        return lax.all_to_all(values, "dp", 0, 0, tiled=True)

    def accept(self, out):
        if self.step == 2:
            self.peer = out
        elif not self.behind:
            self.own = out.reshape(-1, out.shape[-1])


class Scatter:
    def __init__(self, peer, own=None, behind=False, wide=False, dtype=bf16):
        self.wide = wide
        self.dtype = dtype
        self.peer = peer
        self.own = own
        self.behind = behind
        self.step = 0 if peer is not None else 1

    def group(self, g, part=slice(None)):
        n = lax.axis_size("dp")
        shape = (4, n // 4, self.own.shape[0] // n) + self.own.shape[1:]
        total = self.own.reshape(shape)[g, part].astype(f32)
        if self.peer is not None:
            total = total + self.other.reshape(shape)[g, part].astype(f32)
        return total

    def request(self):
        if self.step == 0:
            return self.peer
        half = quarter() // 2
        low, high = slice(0, half), slice(half, None)
        if self.step == 1:
            values = (self.group(3, low), self.group(3, high))
        elif self.step == 2:
            values = (
                jnp.concatenate([self.group(1, low), self.group(1, high) + self.diagonal[1].astype(f32)]),
                jnp.concatenate([self.group(2, low) + self.diagonal[0].astype(f32), self.group(2, high)]),
            )
        else:
            values = self.group(0) + self.sides[0].astype(f32) + self.sides[1].astype(f32)
            if self.behind and self.wide:
                return values
        return jax.tree.map(lambda value: value.astype(self.dtype), values)

    def send(self, values):
        self.step += 1
        if self.step == 1:
            return swap_core(values)
        if self.step < 4:
            return swap(values[0], 1), swap(values[1], 2)
        if self.behind:
            self.total = sum_z(values).astype(f32)
            return None
        return over_z(values)

    def accept(self, out):
        if self.step == 1:
            self.other = out
        elif self.step == 2:
            self.diagonal = out
        elif self.step == 3:
            self.sides = out
        elif not self.behind:
            self.total = jnp.sum(out.astype(f32), axis=0)

    def result(self):
        return self.total


class Ticks:
    def __init__(self):
        self.last = []

    def wait(self, live=()):
        outs, live = barrier(([out for _, out in self.last], live))
        for (job, _), out in zip(self.last, outs):
            if out is not None:
                job.accept(out)
        self.last = []
        return live

    def __call__(self, jobs, live=()):
        values, live = barrier(([job.request() for job in jobs], live))
        self.last = [(job, job.send(value)) for job, value in zip(jobs, values)]
        return live


def small_gather(values):
    group = jnp.stack([values] + [swap(values, 4 * j) for j in range(1, quarter())])
    group = jnp.concatenate([group] + [swap(group, g) for g in (1, 2, 3)])
    apart = jnp.bitwise_xor(jnp.arange(4 * quarter(), dtype=jnp.int32), lax.axis_index("dp"))
    return jnp.take(group, (apart & 3) * quarter() + (apart >> 2), axis=0)


def total_over_all(values):
    count = lax.axis_size("dp") * lax.axis_size("mp")
    parts = jnp.broadcast_to(values[None], (count,) + values.shape)
    return jnp.sum(lax.all_to_all(parts, ("dp", "mp"), 0, 0, tiled=True), axis=0)


def place_of(index):
    apart = jnp.bitwise_xor(index, lax.axis_index("dp")) & 3
    return apart * quarter() + (index >> 2)


def layout(lengths):
    ends = jnp.cumsum(lengths)
    places = jnp.arange(LEN, dtype=jnp.int32)
    passed = places[:, None] >= ends[None, :]
    segment = jnp.sum(passed.astype(jnp.int32), axis=1)
    start = jnp.sum(jnp.where(passed, lengths[None, :], 0), axis=1)
    offset = places - start
    bounds = jnp.array(PYRAMID, dtype=jnp.int32)
    scale_id = jnp.sum((offset[:, None] >= bounds[None, :]).astype(jnp.int32), axis=1)
    usable = places < ends[-1]
    return (segment, scale_id, usable)


def matmul(left, right):
    return jnp.dot(left, right, preferred_element_type=f32)


def matmul_tn(left, right):
    return lax.dot_general(left, right, (((0,), (0,)), ((), ())), preferred_element_type=f32)


def matmul_nt(left, right):
    return lax.dot_general(left, right, (((1,), (1,)), ((), ())), preferred_element_type=f32)


def exact_tn(left, right):
    return lax.dot_general(
        left,
        right,
        (((0,), (0,)), ((), ())),
        precision=lax.Precision.HIGHEST,
        preferred_element_type=f32,
    )


def unit_pair(values):
    factor = lax.rsqrt(jnp.mean(values * values, axis=-1, keepdims=True) + EPSILON)
    return factor, (values * factor).astype(bf16)


def unit_back(values, factor, grad):
    inner = jnp.mean(grad * values, axis=-1, keepdims=True)
    return (factor * (grad - values * (factor * factor * inner))).astype(bf16)


def normed(values):
    centered = values - jnp.mean(values, axis=-1, keepdims=True)
    factor = lax.rsqrt(jnp.mean(centered * centered, axis=-1, keepdims=True) + EPSILON)
    return centered * factor, factor


def normed_back(hat, factor, grad):
    inner = jnp.mean(grad * hat, axis=-1, keepdims=True)
    return factor * (grad - jnp.mean(grad, axis=-1, keepdims=True) - hat * inner)


def spread(hot, part):
    high = part.astype(bf16).astype(f32)
    mid = (part - high).astype(bf16).astype(f32)
    low = part - high - mid
    return matmul(hot, jnp.concatenate([high, mid, low], axis=0).astype(bf16))


def item_sum(hot_t, values):
    high = values.astype(bf16)
    low = (values - high.astype(f32)).astype(bf16)
    return matmul(hot_t, high) + matmul(hot_t, low)


def flip(values):
    return values.astype(f32).T.astype(bf16)


def gelu_parts(values):
    inner = GELU_C * (values + 0.044715 * values * values * values)
    cdf = 0.5 * (1.0 + jnp.tanh(inner))
    return cdf, values * cdf


def gelu_slope(values, cdf):
    return cdf + values * (2.0 * cdf * (1.0 - cdf)) * (GELU_C * (1.0 + 0.134145 * values * values))


def whole(*shape):
    return pl.BlockSpec(shape, lambda *_: (0,) * len(shape), pipeline_mode=pl.Buffered(1))


def columns(rows, width):
    return pl.BlockSpec((rows, width), lambda i: (0, i))


def sds(shape, dtype):
    return jax.ShapeDtypeStruct(shape, dtype)


def kernel_call(body, grid, in_specs, out_specs, out_shape, flops, scratch=()):
    return pl.pallas_call(
        body,
        grid=grid,
        in_specs=in_specs,
        out_specs=out_specs,
        out_shape=out_shape,
        scratch_shapes=list(scratch),
        compiler_params=pltpu.CompilerParams(vmem_limit_bytes=VMEM_LIMIT),
        cost_estimate=pl.CostEstimate(flops=flops, transcendentals=0, bytes_accessed=2**24),
    )


def add_up(ref, part, start=None):
    first = pl.program_id(0) == 0

    @pl.when(first)
    def _():
        ref[...] = part if start is None else start[...] + part

    @pl.when(jnp.logical_not(first))
    def _():
        ref[...] += part


def at_end(fn):
    pl.when(pl.program_id(0) == pl.num_programs(0) - 1)(fn)


def embed_kernel(code_ref, own_ref, peer_ref, turn_ref, hot_ref, mod_ref, tok_ref, na_ref, na_t_ref, acc):
    step, steps = pl.program_id(0), pl.num_programs(0)
    rows = own_ref.shape[0]
    lane = lax.broadcasted_iota(jnp.int32, (LEN, rows), 1) + step * rows
    hot_own = (lane == code_ref[...]).astype(bf16)
    hot_peer = (lane + steps * rows == code_ref[...]).astype(bf16)
    add_up(acc, matmul(hot_own, own_ref[...]) + matmul(hot_peer, peer_ref[...]))

    @at_end
    def _():
        tokens = matmul(acc[...].astype(bf16), turn_ref[...])
        tok_ref[...] = tokens.astype(bf16)
        hat, _ = normed(tokens)
        out = hat * (1.0 + spread(hot_ref[...], mod_ref[:, :D])) + spread(hot_ref[...], mod_ref[:, D:])
        na_ref[...] = out.astype(bf16)
        na_t_ref[...] = flip(out)


def embed(code_rows, own, peer, turn, hot, mod):
    rows = own.shape[0]
    block = rows // 4
    rows_spec = pl.BlockSpec((block, D), lambda i: (i, 0))
    return kernel_call(
        embed_kernel,
        (4,),
        [whole(LEN, 1), rows_spec, rows_spec, whole(D, D), whole(LEN, 24), whole(ITEMS, 2 * D)],
        [whole(LEN, D), whole(LEN, D), whole(D, LEN)],
        [sds((LEN, D), bf16), sds((LEN, D), bf16), sds((D, LEN), bf16)],
        4 * LEN * rows * D,
        [pltpu.VMEM((LEN, D), f32)],
    )(code_rows, own, peer, turn, hot, mod)


def attend_pair(na_ref, w_ref, bias_ref):
    raw = matmul(na_ref[...], w_ref[:, : 3 * PAIR])
    outs = []
    for head in range(2):
        cut = [slice(i * PAIR + head * HEAD_WIDTH, i * PAIR + (head + 1) * HEAD_WIDTH) for i in range(3)]
        _, query_n = unit_pair(raw[:, cut[0]])
        _, key_n = unit_pair(raw[:, cut[1]])
        raised = jnp.exp2(matmul_nt(query_n, key_n) * SCORE_POWER + bias_ref[...])
        share = 1.0 / jnp.sum(raised, axis=-1, keepdims=True)
        outs.append(matmul((raised * share).astype(bf16), raw[:, cut[2]].astype(bf16)).astype(bf16))
    return jnp.concatenate(outs, axis=1)


def attend_first_kernel(na_ref, w_ref, bias_ref, out_ref, acc_ref):
    out = attend_pair(na_ref, w_ref, bias_ref)
    out_ref[...] = out
    add_up(acc_ref, matmul_nt(out, w_ref[:, 3 * PAIR :]))


def attend_last_kernel(
    na_ref, w_ref, bias_ref, part_ref, tok_ref, hot_ref, mod_ref, out_ref, acc_ref, mid_ref, nm_ref, nm_t_ref
):
    out = attend_pair(na_ref, w_ref, bias_ref)
    out_ref[...] = out
    add_up(acc_ref, matmul_nt(out, w_ref[:, 3 * PAIR :]), part_ref)

    @at_end
    def _():
        middle = tok_ref[...].astype(f32) + spread(hot_ref[...], mod_ref[:, :D]) * acc_ref[...]
        mid_ref[...] = middle
        hat, _ = normed(middle)
        out = hat * (1.0 + spread(hot_ref[...], mod_ref[:, D : 2 * D])) + spread(
            hot_ref[...], mod_ref[:, 2 * D :]
        )
        nm_ref[...] = out.astype(bf16)
        nm_t_ref[...] = flip(out)


def attend_first(na, w, bias):
    steps = w.shape[1] // (4 * PAIR)
    return kernel_call(
        attend_first_kernel,
        (steps,),
        [whole(LEN, D), columns(D, 4 * PAIR), whole(LEN, LEN)],
        [columns(LEN, PAIR), whole(LEN, D)],
        [sds((LEN, steps * PAIR), bf16), sds((LEN, D), f32)],
        steps * ATTEND_FLOPS,
    )(na, w, bias)


def attend_last(na, w, bias, part, tokens, hot, mod):
    steps = w.shape[1] // (4 * PAIR)
    return kernel_call(
        attend_last_kernel,
        (steps,),
        [
            whole(LEN, D),
            columns(D, 4 * PAIR),
            whole(LEN, LEN),
            whole(LEN, D),
            whole(LEN, D),
            whole(LEN, 24),
            whole(ITEMS, 3 * D),
        ],
        [columns(LEN, PAIR), whole(LEN, D), whole(LEN, D), whole(LEN, D), whole(D, LEN)],
        [
            sds((LEN, steps * PAIR), bf16),
            sds((LEN, D), f32),
            sds((LEN, D), f32),
            sds((LEN, D), bf16),
            sds((D, LEN), bf16),
        ],
        steps * ATTEND_FLOPS,
    )(na, w, bias, part, tokens, hot, mod)


def attend_pair_back(na_ref, na_t_ref, go_ref, go_t_ref, o_ref, w_ref, bias_ref, dw_ref):
    raw = matmul(na_ref[...], w_ref[:, : 3 * PAIR])
    grad_att = matmul(go_ref[...], w_ref[:, 3 * PAIR :]).astype(bf16)
    results = [[], [], []]
    for head in range(2):
        cut = [slice(i * PAIR + head * HEAD_WIDTH, i * PAIR + (head + 1) * HEAD_WIDTH) for i in range(3)]
        query, key = raw[:, cut[0]], raw[:, cut[1]]
        query_f, query_n = unit_pair(query)
        key_f, key_n = unit_pair(key)
        value_b = raw[:, cut[2]].astype(bf16)
        grad_out = grad_att[:, head * HEAD_WIDTH : (head + 1) * HEAD_WIDTH]
        grad_q, grad_k, grad_v = [], 0.0, 0.0
        for low, high in ((0, 384), (384, LEN)):
            raised = jnp.exp2(matmul_nt(key_n, query_n[low:high]) * SCORE_POWER + bias_ref[:, low:high])
            attention = raised * (1.0 / jnp.sum(raised, axis=0, keepdims=True))
            grad_probs = matmul_nt(value_b, grad_out[low:high])
            row_dot = jnp.sum(attention * grad_probs, axis=0, keepdims=True)
            grad_scores = (attention * (grad_probs - row_dot)).astype(bf16)
            grad_v = grad_v + matmul(attention.astype(bf16), grad_out[low:high])
            grad_k = grad_k + matmul(grad_scores, query_n[low:high])
            grad_q.append(matmul_tn(key_n, grad_scores).T)
        grad_q = jnp.concatenate(grad_q, axis=0) * SCORE_SCALE
        results[0].append(unit_back(query, query_f, grad_q))
        results[1].append(unit_back(key, key_f, grad_k * SCORE_SCALE))
        results[2].append(grad_v.astype(bf16))
    grad_raw = jnp.concatenate([part for pair in results for part in pair], axis=1)
    dw_ref[:, : 3 * PAIR] = matmul(na_t_ref[...], grad_raw).astype(bf16)
    dw_ref[:, 3 * PAIR :] = matmul(go_t_ref[...], o_ref[...]).astype(bf16)
    return matmul_nt(grad_raw, w_ref[:, : 3 * PAIR])


def attend_back_first_kernel(na_ref, na_t_ref, go_ref, go_t_ref, o_ref, w_ref, bias_ref, dw_ref, acc_ref):
    add_up(acc_ref, attend_pair_back(na_ref, na_t_ref, go_ref, go_t_ref, o_ref, w_ref, bias_ref, dw_ref))


def attend_back_last_kernel(
    na_ref, na_t_ref, go_ref, go_t_ref, o_ref, w_ref, bias_ref,
    part_ref, tok_ref, gm_ref, hot_ref, hot_t_ref, mod_ref,
    dw_ref, gt_ref, items_ref, acc_ref,
):
    part = attend_pair_back(na_ref, na_t_ref, go_ref, go_t_ref, o_ref, w_ref, bias_ref, dw_ref)
    add_up(acc_ref, part, part_ref)

    @at_end
    def _():
        grad = acc_ref[...]
        hat, factor = normed(tok_ref[...].astype(f32))
        items_ref[:, :D] = item_sum(hot_t_ref[...], grad * hat)
        items_ref[:, D:] = item_sum(hot_t_ref[...], grad)
        inner = normed_back(hat, factor, grad * (1.0 + spread(hot_ref[...], mod_ref[...])))
        gt_ref[...] = (gm_ref[...] + inner).astype(bf16)


def attend_back_specs():
    return [
        whole(LEN, D),
        whole(D, LEN),
        whole(LEN, D),
        whole(D, LEN),
        columns(LEN, PAIR),
        columns(D, 4 * PAIR),
        whole(LEN, LEN),
    ]


def attend_back_first(na, na_t, go, go_t, out, w, bias_t):
    steps = w.shape[1] // (4 * PAIR)
    return kernel_call(
        attend_back_first_kernel,
        (steps,),
        attend_back_specs(),
        [columns(D, 4 * PAIR), whole(LEN, D)],
        [sds(w.shape, bf16), sds((LEN, D), f32)],
        3 * steps * ATTEND_FLOPS,
    )(na, na_t, go, go_t, out, w, bias_t)


def attend_back_last(na, na_t, go, go_t, out, w, bias_t, part, tokens, grad_middle, hot, hot_t, mod):
    steps = w.shape[1] // (4 * PAIR)
    return kernel_call(
        attend_back_last_kernel,
        (steps,),
        attend_back_specs()
        + [
            whole(LEN, D),
            whole(LEN, D),
            whole(LEN, D),
            whole(LEN, 24),
            whole(2 * ITEMS, LEN),
            whole(ITEMS, D),
        ],
        [columns(D, 4 * PAIR), whole(LEN, D), whole(2 * ITEMS, 2 * D)],
        [sds(w.shape, bf16), sds((LEN, D), bf16), sds((2 * ITEMS, 2 * D), f32)],
        3 * steps * ATTEND_FLOPS,
        [pltpu.VMEM((LEN, D), f32)],
    )(na, na_t, go, go_t, out, w, bias_t, part, tokens, grad_middle, hot, hot_t, mod)


def mlp_part(nm_ref, w_refs, h_refs):
    total = 0.0
    for w_ref, h_ref in zip(w_refs, h_refs):
        hidden = matmul(nm_ref[...], w_ref[:, :BLOCK])
        h_ref[...] = hidden
        _, active = gelu_parts(hidden)
        total = total + matmul_nt(active.astype(bf16), w_ref[:, BLOCK:])
    return total


def mlp_first_kernel(nm_ref, w0_ref, w1_ref, h0_ref, h1_ref, acc_ref):
    add_up(acc_ref, mlp_part(nm_ref, (w0_ref, w1_ref), (h0_ref, h1_ref)))


def mlp_last_kernel(
    nm_ref, w0_ref, w1_ref, part_ref, mid_ref, hot_ref, mod_ref, h0_ref, h1_ref, acc_ref, res_ref, nh_ref, nh_t_ref
):
    add_up(acc_ref, mlp_part(nm_ref, (w0_ref, w1_ref), (h0_ref, h1_ref)), part_ref)

    @at_end
    def _():
        residual = mid_ref[...] + spread(hot_ref[...], mod_ref[...]) * acc_ref[...]
        res_ref[...] = residual
        hat, _ = normed(residual)
        nh_ref[...] = hat.astype(bf16)
        nh_t_ref[...] = flip(hat)


def mlp_first(nm, ws):
    steps = ws[0].shape[1] // (2 * BLOCK)
    hidden = sds((LEN, steps * BLOCK), f32)
    *hiddens, acc = kernel_call(
        mlp_first_kernel,
        (steps,),
        [whole(LEN, D)] + [columns(D, 2 * BLOCK)] * 2,
        [columns(LEN, BLOCK)] * 2 + [whole(LEN, D)],
        [hidden, hidden, sds((LEN, D), f32)],
        8 * steps * LEN * D * BLOCK,
    )(nm, *ws)
    return hiddens, acc


def mlp_last(nm, ws, part, middle, hot, mod):
    steps = ws[0].shape[1] // (2 * BLOCK)
    hidden = sds((LEN, steps * BLOCK), f32)
    h0, h1, *rest = kernel_call(
        mlp_last_kernel,
        (steps,),
        [whole(LEN, D)]
        + [columns(D, 2 * BLOCK)] * 2
        + [whole(LEN, D), whole(LEN, D), whole(LEN, 24), whole(ITEMS, D)],
        [columns(LEN, BLOCK)] * 2 + [whole(LEN, D), whole(LEN, D), whole(LEN, D), whole(D, LEN)],
        [
            hidden,
            hidden,
            sds((LEN, D), f32),
            sds((LEN, D), f32),
            sds((LEN, D), bf16),
            sds((D, LEN), bf16),
        ],
        8 * steps * LEN * D * BLOCK,
    )(nm, *ws, part, middle, hot, mod)
    return [h0, h1], *rest


def mlp_part_back(nm_t_ref, g_ref, g_t_ref, h_refs, w_refs, dw_ref):
    total = 0.0
    for i, (h_ref, w_ref) in enumerate(zip(h_refs, w_refs)):
        hidden = h_ref[...]
        cdf, active = gelu_parts(hidden)
        at = 2 * i * BLOCK
        dw_ref[:, at + BLOCK : at + 2 * BLOCK] = matmul(g_t_ref[...], active.astype(bf16)).astype(bf16)
        grad_pre = (gelu_slope(hidden, cdf) * matmul(g_ref[...], w_ref[:, BLOCK:])).astype(bf16)
        dw_ref[:, at : at + BLOCK] = matmul(nm_t_ref[...], grad_pre).astype(bf16)
        total = total + matmul_nt(grad_pre, w_ref[:, :BLOCK])
    return total


def mlp_back_first_kernel(nm_t_ref, g_ref, g_t_ref, h0_ref, h1_ref, w0_ref, w1_ref, dw_ref, acc_ref):
    add_up(acc_ref, mlp_part_back(nm_t_ref, g_ref, g_t_ref, (h0_ref, h1_ref), (w0_ref, w1_ref), dw_ref))


def mlp_back_last_kernel(
    nm_t_ref, g_ref, g_t_ref, h0_ref, h1_ref, w0_ref, w1_ref,
    part_ref, mid_ref, gr_ref, out_ref, hot_ref, hot_t_ref, mod_ref,
    dw_ref, gm_ref, go_ref, go_t_ref, items_ref, acc_ref,
):
    part = mlp_part_back(nm_t_ref, g_ref, g_t_ref, (h0_ref, h1_ref), (w0_ref, w1_ref), dw_ref)
    add_up(acc_ref, part, part_ref)

    @at_end
    def _():
        grad = acc_ref[...]
        hat, factor = normed(mid_ref[...])
        items_ref[:, D : 2 * D] = item_sum(hot_t_ref[...], grad * hat)
        items_ref[:, 2 * D :] = item_sum(hot_t_ref[...], grad)
        grad_middle = gr_ref[...] + normed_back(
            hat, factor, grad * (1.0 + spread(hot_ref[...], mod_ref[:, D:]))
        )
        gm_ref[...] = grad_middle
        items_ref[:, :D] = item_sum(hot_t_ref[...], grad_middle * out_ref[...])
        grad_out = spread(hot_ref[...], mod_ref[:, :D]) * grad_middle
        go_ref[...] = grad_out.astype(bf16)
        go_t_ref[...] = flip(grad_out)


def mlp_back_specs():
    return (
        [whole(D, LEN), whole(LEN, D), whole(D, LEN)]
        + [columns(LEN, BLOCK)] * 2
        + [columns(D, 2 * BLOCK)] * 2
    )


def mlp_back_first(nm_t, g, g_t, hiddens, ws):
    steps = ws[0].shape[1] // (2 * BLOCK)
    return kernel_call(
        mlp_back_first_kernel,
        (steps,),
        mlp_back_specs(),
        [columns(D, 4 * BLOCK), whole(LEN, D)],
        [sds((D, 4 * steps * BLOCK), bf16), sds((LEN, D), f32)],
        16 * steps * LEN * D * BLOCK,
    )(nm_t, g, g_t, *hiddens, *ws)


def mlp_back_last(nm_t, g, g_t, hiddens, ws, part, middle, grad_res, attn_out, hot, hot_t, mod):
    steps = ws[0].shape[1] // (2 * BLOCK)
    return kernel_call(
        mlp_back_last_kernel,
        (steps,),
        mlp_back_specs()
        + [whole(LEN, D)] * 4
        + [whole(LEN, 24), whole(2 * ITEMS, LEN), whole(ITEMS, 2 * D)],
        [
            columns(D, 4 * BLOCK),
            whole(LEN, D),
            whole(LEN, D),
            whole(D, LEN),
            whole(2 * ITEMS, 3 * D),
        ],
        [
            sds((D, 4 * steps * BLOCK), bf16),
            sds((LEN, D), f32),
            sds((LEN, D), bf16),
            sds((D, LEN), bf16),
            sds((2 * ITEMS, 3 * D), f32),
        ],
        16 * steps * LEN * D * BLOCK,
        [pltpu.VMEM((LEN, D), f32)],
    )(nm_t, g, g_t, *hiddens, *ws, part, middle, grad_res, attn_out, hot, hot_t, mod)


def head_kernel(
    nh_ref, nh_t_ref, own_ref, peer_ref, target_ref, weight_ref, res_ref, mlp_ref, hot_ref, hot_t_ref, mod_ref,
    dw_own_ref, dw_peer_ref, loss_ref, gr_ref, gmo_ref, gmo_t_ref, items_ref,
    logits, most, total, chosen, acc,
):
    step = pl.program_id(0)
    half = pl.num_programs(0) // 2
    block = own_ref.shape[1]
    lane = lax.broadcasted_iota(jnp.int32, (LEN, block), 1)

    @pl.when(step == 0)
    def _():
        most[...] = jnp.full((LEN, 1), -1e30, f32)
        total[...] = jnp.zeros((LEN, 1), f32)
        chosen[...] = jnp.zeros((LEN, 1), f32)

    for which, w_ref, dw_ref in ((0, own_ref, dw_own_ref), (1, peer_ref, dw_peer_ref)):

        @pl.when(step < half)
        def _():
            place = step + which * half
            values = matmul(nh_ref[...], w_ref[...])
            logits[place] = values
            most_new = jnp.maximum(most[...], jnp.max(values, axis=1, keepdims=True))
            total[...] = total[...] * jnp.exp(most[...] - most_new) + jnp.sum(
                jnp.exp(values - most_new), axis=1, keepdims=True
            )
            most[...] = most_new
            is_target = lane + place * block == target_ref[...]
            chosen[...] += jnp.sum(jnp.where(is_target, values, 0.0), axis=1, keepdims=True)

    @pl.when(step == half - 1)
    def _():
        most[...] = most[...] + jnp.log(total[...])
        loss = jnp.sum(weight_ref[...] * (most[...] - chosen[...]), axis=0, keepdims=True)
        loss_ref[...] = jnp.broadcast_to(loss, (8, 128))

    for which, w_ref, dw_ref in ((0, own_ref, dw_own_ref), (1, peer_ref, dw_peer_ref)):

        @pl.when(step >= half)
        def _():
            place = step - half + which * half
            is_target = lane + place * block == target_ref[...]
            grad = (jnp.exp(logits[place] - most[...]) - is_target.astype(f32)) * weight_ref[...]
            grad = grad.astype(bf16)
            dw_ref[...] = matmul(nh_t_ref[...], grad).astype(bf16)
            part = matmul_nt(grad, w_ref[...])

            @pl.when(jnp.logical_and(step == half, which == 0))
            def _():
                acc[...] = part

            @pl.when(jnp.logical_not(jnp.logical_and(step == half, which == 0)))
            def _():
                acc[...] += part

    @at_end
    def _():
        hat, factor = normed(res_ref[...])
        grad_res = normed_back(hat, factor, acc[...])
        gr_ref[...] = grad_res
        items_ref[...] = item_sum(hot_t_ref[...], grad_res * mlp_ref[...])
        grad_mlp = spread(hot_ref[...], mod_ref[...]) * grad_res
        gmo_ref[...] = grad_mlp.astype(bf16)
        gmo_t_ref[...] = flip(grad_mlp)


def head(nh, nh_t, own, peer, target, weight, residual, mlp_out, hot, hot_t, mod):
    half = own.shape[1] // BLOCK
    w_spec = pl.BlockSpec((D, BLOCK), lambda i: (0, i % half))
    dw_spec = pl.BlockSpec((D, BLOCK), lambda i: (0, jnp.maximum(i - half, 0)))
    return kernel_call(
        head_kernel,
        (2 * half,),
        [
            whole(LEN, D),
            whole(D, LEN),
            w_spec,
            w_spec,
            whole(LEN, 1),
            whole(LEN, 1),
            whole(LEN, D),
            whole(LEN, D),
            whole(LEN, 24),
            whole(2 * ITEMS, LEN),
            whole(ITEMS, D),
        ],
        [
            dw_spec,
            dw_spec,
            whole(8, 128),
            whole(LEN, D),
            whole(LEN, D),
            whole(D, LEN),
            whole(2 * ITEMS, D),
        ],
        [
            sds(own.shape, bf16),
            sds(own.shape, bf16),
            sds((8, 128), f32),
            sds((LEN, D), f32),
            sds((LEN, D), bf16),
            sds((D, LEN), bf16),
            sds((2 * ITEMS, D), f32),
        ],
        12 * half * LEN * D * BLOCK,
        [
            pltpu.VMEM((2 * half, LEN, BLOCK), f32),
            pltpu.VMEM((LEN, 1), f32),
            pltpu.VMEM((LEN, 1), f32),
            pltpu.VMEM((LEN, 1), f32),
            pltpu.VMEM((LEN, D), f32),
        ],
    )(nh, nh_t, own, peer, target, weight, residual, mlp_out, hot, hot_t, mod)


def code_first_kernel(code_ref, gt_ref, turn_ref, out_ref, flat_ref):
    step, steps = pl.program_id(0), pl.num_programs(0)
    rows = out_ref.shape[0]

    @pl.when(step == 0)
    def _():
        flat_ref[...] = matmul_nt(gt_ref[...], turn_ref[...]).astype(bf16)

    row = lax.broadcasted_iota(jnp.int32, (rows, LEN), 0) + (step + steps) * rows
    out_ref[...] = matmul((row == code_ref[...]).astype(bf16), flat_ref[...]).astype(bf16)


def code_last_kernel(code_ref, flat_ref, out_ref):
    rows = out_ref.shape[0]
    row = lax.broadcasted_iota(jnp.int32, (rows, LEN), 0) + pl.program_id(0) * rows
    out_ref[...] = matmul((row == code_ref[...]).astype(bf16), flat_ref[...]).astype(bf16)


def code_back_first(code_rows, grad_tokens, turn, rows):
    spec = pl.BlockSpec((rows // 4, D), lambda i: (i, 0))
    out, flat = kernel_call(
        code_first_kernel,
        (4,),
        [whole(1, LEN), whole(LEN, D), whole(D, D)],
        [spec, whole(LEN, D)],
        [sds((rows, D), bf16), sds((LEN, D), bf16)],
        2 * LEN * rows * D,
    )(code_rows, grad_tokens, turn)
    return code_rows, flat, out


def code_back_last(code_rows, flat, rows):
    spec = pl.BlockSpec((rows // 4, D), lambda i: (i, 0))
    return kernel_call(
        code_last_kernel,
        (4,),
        [whole(1, LEN), whole(LEN, D)],
        spec,
        sds((rows, D), bf16),
        2 * LEN * rows * D,
    )(code_rows, flat)


def step_rates():
    return (
        2.5,
        2.5,
        2.5 / math.sqrt(D),
        2.5 / math.sqrt(D),
        2.5 / math.sqrt(D // 32),
        2.5 / math.sqrt(D),
        2.5 / math.sqrt(FF),
        5.0 / math.sqrt(D),
    )


def adamw_update(weight, grad, moment, square, rate):
    first = BETA_ONE * moment + (1.0 - BETA_ONE) * grad
    second = BETA_TWO * square + (1.0 - BETA_TWO) * grad * grad
    corrected = (
        first / (1.0 - BETA_ONE**STEP) / (jnp.sqrt(second / (1.0 - BETA_TWO**STEP)) + ADAM_EPSILON)
    )
    return (first, second, weight - rate * (corrected + DECAY * weight))


def on_device(
    input_codes,
    target_codes,
    item_lengths,
    item_labels,
    code_table,
    class_table,
    adaln_weight,
    qkv_weight,
    proj_weight,
    expand_weight,
    contract_weight,
    head_weight,
    code_moment,
    class_moment,
    adaln_moment,
    qkv_moment,
    proj_moment,
    expand_moment,
    contract_moment,
    head_moment,
    code_square,
    class_square,
    adaln_square,
    qkv_square,
    proj_square,
    expand_square,
    contract_square,
    head_square,
):
    masters = (
        code_table,
        class_table,
        adaln_weight,
        qkv_weight,
        proj_weight.T,
        expand_weight,
        contract_weight.T,
        head_weight,
    )
    moments = (
        code_moment,
        class_moment,
        adaln_moment,
        qkv_moment,
        proj_moment.T,
        expand_moment,
        contract_moment.T,
        head_moment,
    )
    squares = (
        code_square,
        class_square,
        adaln_square,
        qkv_square,
        proj_square.T,
        expand_square,
        contract_square.T,
        head_square,
    )
    n = lax.axis_size("dp")
    core = lax.axis_index("mp")
    rows = code_table.shape[0]
    half_rows = rows // 2
    width = proj_weight.shape[0]
    wide = expand_weight.shape[1]
    codes_local = head_weight.shape[1]

    def mine(values):
        return lax.dynamic_index_in_dim(values, core, 0, keepdims=False)

    pairs = width // PAIR
    code_block = lax.dynamic_slice_in_dim(code_table, core * half_rows, half_rows, 0).astype(bf16)
    attn_block = jnp.stack([qkv_weight[0], qkv_weight[1], qkv_weight[2], proj_weight.T], axis=1)
    attn_block = attn_block.reshape(-1, 4, pairs, PAIR).swapaxes(1, 2).reshape(-1, 4 * width)
    blocks = wide // BLOCK
    mlp_blocks = jnp.stack(
        [expand_weight.reshape(-1, blocks, BLOCK), contract_weight.T.reshape(-1, blocks, BLOCK)], axis=2
    ).astype(bf16)
    code_w, attn_w, mlp_a, mlp_b, head_w = [
        Gather(block, behind)
        for block, behind in (
            (code_block, False),
            (attn_block.astype(bf16), False),
            (mlp_blocks[:, 0::2].reshape(-1, wide), True),
            (mlp_blocks[:, 1::2].reshape(-1, wide), True),
            (head_weight.astype(bf16), True),
        )
    ]
    begin = Ticks()
    begin([code_w])
    numbers = small_gather(jnp.stack([item_lengths[:, 0], item_labels[:, 0]], axis=1))
    positions = jnp.arange(n, dtype=jnp.int32)
    block_at = ((lax.axis_index("dp") & 3) ^ (positions // quarter())) + 4 * (positions % quarter())
    block_place = place_of(positions)
    labels = numbers[:, :, 1]
    labels_own = jnp.where(core == 0, labels[:, 0], labels[:, 1])
    labels_peer = jnp.where(core == 0, labels[:, 1], labels[:, 0])
    class_low = class_table.astype(bf16)
    adaln_low = adaln_weight.astype(bf16)

    def class_part(item_labels):
        ids = jnp.arange(CLASSES, dtype=jnp.int32)
        picked = (item_labels.reshape(-1, 1) == ids[None, :]).astype(bf16)
        class_rows = matmul(picked, class_low)
        return picked, class_rows, jax.nn.silu(class_rows).astype(bf16)

    _, _, class_vec = class_part(labels_own[block_at])
    order = (2, 4, 0, 1, 3, 5)
    adaln_parts = jnp.concatenate([adaln_low[:, i * D : (i + 1) * D] for i in order], axis=1)

    mod_parts = matmul(class_vec, adaln_parts)

    mod_job = Scatter(None, mod_parts, dtype=f32)
    attn_w.block, mod_job.own = begin.wait((attn_w.block, mod_job.own))
    begin([code_w, attn_w, mod_job, mlp_a])
    begin.wait()
    begin([code_w, mod_job])
    mlp_a.group = begin.wait(mlp_a.group)
    begin([code_w, attn_w, mlp_b, mod_job])
    begin.wait()

    lengths = mine(item_lengths)[0]
    code_ids = mine(input_codes)[0]
    target_ids = mine(target_codes)[0]
    segment, scale_id, usable = layout(lengths)
    bounds = jnp.array((0,) + PYRAMID, dtype=jnp.int32)
    sizes = jnp.array(PYRAMID + (LEN,), dtype=jnp.int32) - bounds
    all_lengths = numbers[:, :, 0].reshape(-1)
    scale_counts = jnp.sum(
        jnp.clip(all_lengths[:, None] - bounds[None, :], 0, sizes[None, :]), axis=0
    ).astype(f32)
    inv_counts = 1.0 / (NSCALES * jnp.maximum(scale_counts, 1.0))
    scale_hot = scale_id[:, None] == jnp.arange(NSCALES, dtype=jnp.int32)[None, :]
    token_weight = jnp.where(
        usable, jnp.sum(jnp.where(scale_hot, inv_counts[None, :], 0.0), axis=1), 0.0
    )
    same = segment[:, None] == segment[None, :]
    bias = jnp.where(same & (scale_id[None, :] <= scale_id[:, None]), 0.0, -1e30)
    bias_t = jnp.where(same & (scale_id[:, None] <= scale_id[None, :]), 0.0, -1e30)
    hot = (segment[:, None] == jnp.arange(3 * ITEMS, dtype=jnp.int32)[None, :] % ITEMS).astype(bf16)
    item_rows = jnp.arange(2 * ITEMS, dtype=jnp.int32)
    hot_t = ((segment[None, :] == item_rows[:, None]) & (item_rows[:, None] < ITEMS)).astype(bf16)

    block_width = D // n
    feature_place = (block_place[:, None] * block_width + jnp.arange(block_width)[None, :]).reshape(-1)
    turn = (feature_place[:, None] == jnp.arange(D, dtype=jnp.int32)[None, :]).astype(bf16)
    within = code_ids % rows
    other = (within // half_rows != core).astype(jnp.int32)
    code_rows = other * (n * half_rows) + place_of(code_ids // rows) * half_rows + within % half_rows
    target = jnp.where(target_ids // codes_local == core, 0, codes_local) + target_ids % codes_local

    def placed(values):
        values = values.reshape(-1, n, block_width)
        return jnp.take(values, block_at, axis=1).reshape(ITEMS, -1)

    def beside(*parts):
        return jnp.concatenate(parts, axis=1)

    mods_embed = placed(mod_job.total[:, : 2 * D])
    scale_attn = mods_embed[:, :D]
    code_col = code_rows.reshape(LEN, 1)

    code_own, code_peer, code_col = begin(
        [attn_w, mlp_a, head_w], (code_w.own, code_w.peer, code_col)
    )
    tokens, na, na_t = begin.wait(embed(code_col, code_own, code_peer, turn, hot, mods_embed))
    na = begin([attn_w, mlp_a, mlp_b], na)
    att_own, part = begin.wait(attend_first(na, attn_w.own, bias))
    mods = placed(mod_job.total[:, 2 * D :])
    gate_attn, gate_mlp, scale_mlp, shift_mlp = jnp.split(mods, 4, axis=1)
    mods_attend = beside(gate_attn, scale_mlp, shift_mlp)
    mods_back = beside(gate_attn, scale_mlp)
    part = begin([mlp_a, mlp_b, head_w], part)
    att_peer, attn_out, middle, nm, nm_t = begin.wait(
        attend_last(na, attn_w.peer, bias, part, tokens, hot, mods_attend)
    )
    nm = begin([mlp_b, head_w], nm)
    mlp_own = (mlp_a.own, mlp_b.own)
    hidden_own, part = begin.wait(mlp_first(nm, mlp_own))
    mlp_peer = (mlp_a.peer, mlp_b.peer)
    part = begin([head_w], part)
    hidden_peer, mlp_out, residual, nh, nh_t = begin.wait(
        mlp_last(nm, mlp_peer, part, middle, hot, gate_mlp)
    )
    dhead_own, dhead_peer, loss_tile, grad_res, gmo, gmo_t, items_head = head(
        nh, nh_t, head_w.own, head_w.peer, target.reshape(LEN, 1), token_weight.reshape(LEN, 1),
        residual, mlp_out, hot, hot_t, gate_mlp,
    )
    loss_local = loss_tile[0, 0]

    def turned(parts):
        values = beside(*parts)
        values = jnp.take(values.reshape(-1, n, block_width), block_place, axis=1)
        return values.reshape(ITEMS, -1).astype(bf16)

    head_job = Scatter(dhead_peer, dhead_own, behind=True, wide=True)
    gmo = begin([head_job], gmo)
    dmlp_peer, part = begin.wait(mlp_back_first(nm_t, gmo, gmo_t, hidden_peer, mlp_peer))
    mlp_job = Scatter(dmlp_peer, behind=True)
    part = begin([head_job, mlp_job], part)
    mlp_job.own, grad_middle, gao, gao_t, items_mlp = begin.wait(
        mlp_back_last(
            nm_t, gmo, gmo_t, hidden_own, mlp_own, part, middle, grad_res, attn_out, hot, hot_t, mods_back
        )
    )
    item_job = Exchange(turned([items_mlp[:ITEMS, :D], items_head[:ITEMS], items_mlp[:ITEMS, D:]]), behind=True)
    gao = begin([head_job, mlp_job, item_job], gao)
    dattn_peer, part = begin.wait(attend_back_first(na, na_t, gao, gao_t, att_peer, attn_w.peer, bias_t))
    attn_job = Scatter(dattn_peer, behind=True)
    part = begin([head_job, mlp_job, attn_job], part)
    attn_job.own, grad_tokens, items_attn = begin.wait(
        attend_back_last(
            na, na_t, gao, gao_t, att_own, attn_w.own, bias_t, part, tokens, grad_middle, hot, hot_t, scale_attn
        )
    )
    late_job = Exchange(turned([items_attn[:ITEMS]]))
    grad_tokens = begin([attn_job, late_job, mlp_job], grad_tokens)
    code_row, flat, dcode_peer = begin.wait(
        code_back_first(code_rows.reshape(1, LEN), grad_tokens, turn, n * half_rows)
    )
    code_job = Scatter(dcode_peer)
    flat = begin([code_job, attn_job], flat)
    code_job.own = begin.wait(code_back_last(code_row, flat, n * half_rows))
    begin([code_job, item_job, late_job, attn_job])
    begin.wait()
    begin([code_job])
    begin.wait()
    head_job.total, mlp_job.total = begin([code_job], (head_job.total, mlp_job.total))
    begin.wait()

    def factor_part(item_labels, grads):
        picked, class_rows, class_vec = class_part(item_labels)
        grad_class_vec = matmul_nt(grads, adaln_low)
        _, silu_back = jax.vjp(jax.nn.silu, class_rows)
        return matmul_tn(class_vec, grads), exact_tn(picked.astype(f32), silu_back(grad_class_vec)[0])

    def grad_rows(which):
        early, late = getattr(item_job, which), getattr(late_job, which)
        order = [early[:, : 2 * D], late[:, :D], early[:, 2 * D : 3 * D], late[:, D:], early[:, 3 * D :]]
        return beside(*order)

    adaln_a, class_a = factor_part(labels_own, grad_rows("own"))
    adaln_b, class_b = factor_part(labels_peer, grad_rows("peer"))
    adaln_grad = adaln_a + adaln_b
    class_grad = class_a + class_b
    code_half = code_job.result()
    code_other = swap_core(code_half)
    code_grad = jnp.where(
        core == 0,
        jnp.concatenate([code_half, code_other]),
        jnp.concatenate([code_other, code_half]),
    )
    attn_grad = attn_job.result()
    kinds = attn_grad.reshape(-1, pairs, 4, PAIR).transpose(2, 0, 1, 3).reshape(4, -1, width)
    mlp_kinds = mlp_job.result().reshape(-1, blocks, 2, BLOCK)
    gradients = (
        code_grad,
        class_grad,
        adaln_grad,
        kinds[:3],
        kinds[3],
        mlp_kinds[:, :, 0].reshape(-1, wide),
        mlp_kinds[:, :, 1].reshape(-1, wide),
        head_job.result(),
    )
    shared_sq = jnp.sum(class_grad * class_grad) + jnp.sum(adaln_grad * adaln_grad)
    own_sq = jnp.sum(code_half * code_half) + jnp.sum(attn_grad * attn_grad)
    for grad in gradients[5:]:
        own_sq = own_sq + jnp.sum(grad * grad)
    totals = total_over_all(
        jnp.concatenate([(own_sq + 0.5 * shared_sq).reshape(1), loss_local.reshape(1)])
    )
    squared, loss = totals[0], totals[1]
    grad_norm = jnp.sqrt(squared)
    clip = jnp.minimum(1.0, CLIP_NORM / (grad_norm + 1e-06))
    firsts, seconds, updated = ([], [], [])
    for place, (weight, grad, moment, square, rate) in enumerate(
        zip(masters, gradients, moments, squares, step_rates())
    ):
        for kept, value in zip(
            (firsts, seconds, updated), adamw_update(weight, grad * clip, moment, square, rate)
        ):
            kept.append(value.T if place in (4, 6) else value)
    return (*firsts, *seconds, *updated, loss, scale_counts, grad_norm)


def solution(mesh):
    token_spec = P(None, "dp", None)
    weight_specs = (
        P("dp", None),
        P(None, "dp"),
        P("dp", None),
        P(None, "dp", "mp"),
        P("mp", "dp"),
        P("dp", "mp"),
        P("mp", "dp"),
        P("dp", "mp"),
    )
    return jax.shard_map(
        on_device,
        mesh=mesh,
        in_specs=(token_spec,) * 4 + weight_specs * 3,
        out_specs=weight_specs * 3 + (P(), P(), P()),
        check_vma=False,
    )
```

```python
import math

import jax
import jax.numpy as jnp
from jax import lax
from jax.experimental import pallas as pl
from jax.experimental.pallas import tpu as pltpu
from jax.sharding import PartitionSpec as P

D = 1024
HEAD_WIDTH = 64
FF = 4096
CLASSES = 1000
LEN = 800
ITEMS = 8
NSCALES = 10
MICRO = 2
STEP = 10


EPSILON = 1e-06
SOFTMAX_WARMTH = 12.0
CLIP_NORM = 0.001
BETA_ONE = 0.9
BETA_TWO = 0.95
DECAY = 0.05
ADAM_EPSILON = 1e-08
PYRAMID = (1, 5, 14, 30, 55, 91, 155, 255, 424)

SCORE_SCALE = SOFTMAX_WARMTH / HEAD_WIDTH
SCORE_POWER = SCORE_SCALE * math.log2(math.e)
GELU_C = math.sqrt(2.0 / math.pi)
PAIR = 2 * HEAD_WIDTH
BLOCK = 512
JOIN_BLOCK = 1024
ATTEND_FLOPS = LEN * PAIR * (8 * D + 4 * LEN)
VMEM_LIMIT = 60 * 2**20

bf16 = jnp.bfloat16
f32 = jnp.float32
barrier = lax.optimization_barrier


def swap(values, bits):
    n = lax.axis_size("dp")
    return lax.ppermute(values, "dp", [(i, i ^ bits) for i in range(n)])


def swap_core(values):
    return lax.ppermute(values, "mp", [(0, 1), (1, 0)])


def quarter():
    return lax.axis_size("dp") // 4


def columns_of_chips():
    n = lax.axis_size("dp")
    return [[xy + 4 * z for z in range(n // 4)] for xy in range(4)]


def over_z(values):
    return lax.all_to_all(values, "dp", 0, 0, tiled=True, axis_index_groups=columns_of_chips())


def sum_z(values):
    return lax.psum_scatter(values, "dp", scatter_dimension=0, axis_index_groups=columns_of_chips())


def join_kernel(*refs):
    parts, out = refs[:-1], refs[-1]
    at = 0
    for part in parts:
        rows = part.shape[0]
        out[at : at + rows, :] = part[...]
        at += rows


def join(parts):
    rows = sum(part.shape[0] for part in parts)
    total = parts[0].shape[1]
    return pl.pallas_call(
        join_kernel,
        grid=(total // JOIN_BLOCK,),
        in_specs=[pl.BlockSpec((part.shape[0], JOIN_BLOCK), lambda i: (0, i)) for part in parts],
        out_specs=pl.BlockSpec((rows, JOIN_BLOCK), lambda i: (0, i)),
        out_shape=jax.ShapeDtypeStruct((rows, total), parts[0].dtype),
    )(*parts)


class Gather:
    def __init__(self, block, behind=False):
        self.block = block
        self.behind = behind
        self.step = 0

    def request(self):
        if self.step == 0 and self.behind:
            return self.block
        if self.step == 0:
            return jnp.broadcast_to(self.block[None], (quarter(),) + self.block.shape)
        if self.step == 1:
            return self.group
        if self.step == 2:
            half = self.group.shape[0] // 2
            return (self.from_y[:half], self.from_x[half:])
        return self.own

    def send(self, values):
        self.step += 1
        if self.step == 1 and self.behind:
            self.group = lax.all_gather(values, "dp", axis=0, tiled=True, axis_index_groups=columns_of_chips())
            return None
        if self.step == 1:
            return over_z(values)
        if self.step == 2:
            return swap(values, 1), swap(values, 2)
        if self.step == 3:
            return swap(values[0], 1), swap(values[1], 2)
        return swap_core(values)

    def accept(self, out):
        if out is None:
            return
        if self.step == 1:
            self.group = out.reshape((-1,) + self.block.shape[1:])
        elif self.step == 2:
            self.from_x, self.from_y = out
        elif self.step == 3:
            self.own = join([self.group, self.from_x, self.from_y, *out])
        else:
            self.peer = out


class Exchange:
    def __init__(self, block, behind=False):
        self.block = block
        self.behind = behind
        self.step = 0

    def request(self):
        n = lax.axis_size("dp")
        if self.step == 1:
            return self.own
        return self.block if self.behind else jnp.broadcast_to(self.block[None], (n,) + self.block.shape)

    def send(self, values):
        self.step += 1
        if self.step == 2:
            return swap_core(values)
        if self.behind:
            self.own = lax.all_gather(values, "dp", axis=0, tiled=True)
            return None
        return lax.all_to_all(values, "dp", 0, 0, tiled=True)

    def accept(self, out):
        if self.step == 2:
            self.peer = out
        elif not self.behind:
            self.own = out.reshape(-1, out.shape[-1])


class Scatter:
    def __init__(self, peer, own=None, behind=False, wide=False, dtype=bf16):
        self.wide = wide
        self.dtype = dtype
        self.peer = peer
        self.own = own
        self.behind = behind
        self.step = 0 if peer is not None else 1

    def group(self, g, part=slice(None)):
        n = lax.axis_size("dp")
        shape = (4, n // 4, self.own.shape[0] // n) + self.own.shape[1:]
        total = self.own.reshape(shape)[g, part].astype(f32)
        if self.peer is not None:
            total = total + self.other.reshape(shape)[g, part].astype(f32)
        return total

    def request(self):
        if self.step == 0:
            return self.peer
        half = quarter() // 2
        low, high = slice(0, half), slice(half, None)
        if self.step == 1:
            values = (self.group(3, low), self.group(3, high))
        elif self.step == 2:
            values = (
                jnp.concatenate([self.group(1, low), self.group(1, high) + self.diagonal[1].astype(f32)]),
                jnp.concatenate([self.group(2, low) + self.diagonal[0].astype(f32), self.group(2, high)]),
            )
        else:
            values = self.group(0) + self.sides[0].astype(f32) + self.sides[1].astype(f32)
            if self.behind and self.wide:
                return values
        return jax.tree.map(lambda value: value.astype(self.dtype), values)

    def send(self, values):
        self.step += 1
        if self.step == 1:
            return swap_core(values)
        if self.step < 4:
            return swap(values[0], 1), swap(values[1], 2)
        if self.behind:
            self.total = sum_z(values).astype(f32)
            return None
        return over_z(values)

    def accept(self, out):
        if self.step == 1:
            self.other = out
        elif self.step == 2:
            self.diagonal = out
        elif self.step == 3:
            self.sides = out
        elif not self.behind:
            self.total = jnp.sum(out.astype(f32), axis=0)

    def result(self):
        return self.total


class Ticks:
    def __init__(self):
        self.last = []

    def wait(self, live=()):
        outs, live = barrier(([out for _, out in self.last], live))
        for (job, _), out in zip(self.last, outs):
            if out is not None:
                job.accept(out)
        self.last = []
        return live

    def __call__(self, jobs, live=()):
        values, live = barrier(([job.request() for job in jobs], live))
        self.last = [(job, job.send(value)) for job, value in zip(jobs, values)]
        return live


def small_gather(values):
    group = jnp.stack([values] + [swap(values, 4 * j) for j in range(1, quarter())])
    group = jnp.concatenate([group] + [swap(group, g) for g in (1, 2, 3)])
    apart = jnp.bitwise_xor(jnp.arange(4 * quarter(), dtype=jnp.int32), lax.axis_index("dp"))
    return jnp.take(group, (apart & 3) * quarter() + (apart >> 2), axis=0)


def total_over_all(values):
    count = lax.axis_size("dp") * lax.axis_size("mp")
    parts = jnp.broadcast_to(values[None], (count,) + values.shape)
    return jnp.sum(lax.all_to_all(parts, ("dp", "mp"), 0, 0, tiled=True), axis=0)


def place_of(index):
    apart = jnp.bitwise_xor(index, lax.axis_index("dp")) & 3
    return apart * quarter() + (index >> 2)


def layout(lengths):
    ends = jnp.cumsum(lengths)
    places = jnp.arange(LEN, dtype=jnp.int32)
    passed = places[:, None] >= ends[None, :]
    segment = jnp.sum(passed.astype(jnp.int32), axis=1)
    start = jnp.sum(jnp.where(passed, lengths[None, :], 0), axis=1)
    offset = places - start
    bounds = jnp.array(PYRAMID, dtype=jnp.int32)
    scale_id = jnp.sum((offset[:, None] >= bounds[None, :]).astype(jnp.int32), axis=1)
    usable = places < ends[-1]
    return (segment, scale_id, usable)


def matmul(left, right):
    return jnp.dot(left, right, preferred_element_type=f32)


def matmul_tn(left, right):
    return lax.dot_general(left, right, (((0,), (0,)), ((), ())), preferred_element_type=f32)


def matmul_nt(left, right):
    return lax.dot_general(left, right, (((1,), (1,)), ((), ())), preferred_element_type=f32)


def exact_tn(left, right):
    return lax.dot_general(
        left,
        right,
        (((0,), (0,)), ((), ())),
        precision=lax.Precision.HIGHEST,
        preferred_element_type=f32,
    )


def unit_pair(values):
    factor = lax.rsqrt(jnp.mean(values * values, axis=-1, keepdims=True) + EPSILON)
    return factor, (values * factor).astype(bf16)


def unit_back(values, factor, grad):
    inner = jnp.mean(grad * values, axis=-1, keepdims=True)
    return (factor * (grad - values * (factor * factor * inner))).astype(bf16)


def normed(values):
    centered = values - jnp.mean(values, axis=-1, keepdims=True)
    factor = lax.rsqrt(jnp.mean(centered * centered, axis=-1, keepdims=True) + EPSILON)
    return centered * factor, factor


def normed_back(hat, factor, grad):
    inner = jnp.mean(grad * hat, axis=-1, keepdims=True)
    return factor * (grad - jnp.mean(grad, axis=-1, keepdims=True) - hat * inner)


def spread(hot, part):
    high = part.astype(bf16).astype(f32)
    mid = (part - high).astype(bf16).astype(f32)
    low = part - high - mid
    return matmul(hot, jnp.concatenate([high, mid, low], axis=0).astype(bf16))


def item_sum(hot_t, values):
    high = values.astype(bf16)
    low = (values - high.astype(f32)).astype(bf16)
    return matmul(hot_t, high) + matmul(hot_t, low)


def flip(values):
    return values.astype(f32).T.astype(bf16)


def gelu_parts(values):
    inner = GELU_C * (values + 0.044715 * values * values * values)
    cdf = 0.5 * (1.0 + jnp.tanh(inner))
    return cdf, values * cdf


def gelu_slope(values, cdf):
    return cdf + values * (2.0 * cdf * (1.0 - cdf)) * (GELU_C * (1.0 + 0.134145 * values * values))


def whole(*shape):
    return pl.BlockSpec(shape, lambda *_: (0,) * len(shape), pipeline_mode=pl.Buffered(1))


def columns(rows, width):
    return pl.BlockSpec((rows, width), lambda i: (0, i))


def sds(shape, dtype):
    return jax.ShapeDtypeStruct(shape, dtype)


def kernel_call(body, grid, in_specs, out_specs, out_shape, flops, scratch=()):
    return pl.pallas_call(
        body,
        grid=grid,
        in_specs=in_specs,
        out_specs=out_specs,
        out_shape=out_shape,
        scratch_shapes=list(scratch),
        compiler_params=pltpu.CompilerParams(vmem_limit_bytes=VMEM_LIMIT),
        cost_estimate=pl.CostEstimate(flops=flops, transcendentals=0, bytes_accessed=2**24),
    )


def add_up(ref, part, start=None):
    first = pl.program_id(0) == 0

    @pl.when(first)
    def _():
        ref[...] = part if start is None else start[...] + part

    @pl.when(jnp.logical_not(first))
    def _():
        ref[...] += part


def held_back(refs, held, sems, into=()):
    def copies():
        places = [held.at[i] for i in range(len(refs) - len(into))] + list(into)
        return [pltpu.make_async_copy(ref, place, sems.at[i]) for i, (ref, place) in enumerate(zip(refs, places))]

    @pl.when(pl.program_id(0) == 0)
    def _():
        for copy in copies():
            copy.start()

    def arrive():
        for copy in copies():
            copy.wait()

    return arrive


ANYWHERE = pl.BlockSpec(memory_space=pl.ANY)


def held_scratch(count, copies=None):
    return [pltpu.VMEM((count, LEN, D), f32), pltpu.SemaphoreType.DMA((copies or count,))]


def at_end(fn):
    pl.when(pl.program_id(0) == pl.num_programs(0) - 1)(fn)


def embed_kernel(code_ref, own_ref, peer_ref, turn_ref, hot_ref, mod_ref, tok_ref, na_ref, na_t_ref, acc):
    step, steps = pl.program_id(0), pl.num_programs(0)
    rows = own_ref.shape[0]
    lane = lax.broadcasted_iota(jnp.int32, (LEN, rows), 1) + step * rows
    hot_own = (lane == code_ref[...]).astype(bf16)
    hot_peer = (lane + steps * rows == code_ref[...]).astype(bf16)
    add_up(acc, matmul(hot_own, own_ref[...]) + matmul(hot_peer, peer_ref[...]))

    @at_end
    def _():
        tokens = matmul(acc[...].astype(bf16), turn_ref[...])
        tok_ref[...] = tokens.astype(bf16)
        hat, _ = normed(tokens)
        out = hat * (1.0 + spread(hot_ref[...], mod_ref[:, :D])) + spread(hot_ref[...], mod_ref[:, D:])
        na_ref[...] = out.astype(bf16)
        na_t_ref[...] = flip(out)


def embed(code_rows, own, peer, turn, hot, mod):
    rows = own.shape[0]
    block = rows // 4
    rows_spec = pl.BlockSpec((block, D), lambda i: (i, 0))
    return kernel_call(
        embed_kernel,
        (4,),
        [whole(LEN, 1), rows_spec, rows_spec, whole(D, D), whole(LEN, 24), whole(ITEMS, 2 * D)],
        [whole(LEN, D), whole(LEN, D), whole(D, LEN)],
        [sds((LEN, D), bf16), sds((LEN, D), bf16), sds((D, LEN), bf16)],
        4 * LEN * rows * D,
        [pltpu.VMEM((LEN, D), f32)],
    )(code_rows, own, peer, turn, hot, mod)


def attend_pair(na_ref, w_ref, bias_ref):
    raw = matmul(na_ref[...], w_ref[:, : 3 * PAIR])
    outs = []
    for head in range(2):
        cut = [slice(i * PAIR + head * HEAD_WIDTH, i * PAIR + (head + 1) * HEAD_WIDTH) for i in range(3)]
        _, query_n = unit_pair(raw[:, cut[0]])
        _, key_n = unit_pair(raw[:, cut[1]])
        raised = jnp.exp2(matmul_nt(query_n, key_n) * SCORE_POWER + bias_ref[...])
        share = 1.0 / jnp.sum(raised, axis=-1, keepdims=True)
        outs.append(matmul((raised * share).astype(bf16), raw[:, cut[2]].astype(bf16)).astype(bf16))
    return jnp.concatenate(outs, axis=1)


def attend_first_kernel(na_ref, w_ref, bias_ref, out_ref, acc_ref):
    out = attend_pair(na_ref, w_ref, bias_ref)
    out_ref[...] = out
    add_up(acc_ref, matmul_nt(out, w_ref[:, 3 * PAIR :]))


def attend_last_kernel(
    na_ref, w_ref, bias_ref, part_ref, tok_ref, hot_ref, mod_ref, out_ref, acc_ref, mid_ref, nm_ref, nm_t_ref,
    held, sems,
):
    arrive = held_back([part_ref], held, sems)
    out = attend_pair(na_ref, w_ref, bias_ref)
    out_ref[...] = out
    add_up(acc_ref, matmul_nt(out, w_ref[:, 3 * PAIR :]))

    @at_end
    def _():
        arrive()
        acc_ref[...] += held[0]
        middle = tok_ref[...].astype(f32) + spread(hot_ref[...], mod_ref[:, :D]) * acc_ref[...]
        mid_ref[...] = middle
        hat, _ = normed(middle)
        out = hat * (1.0 + spread(hot_ref[...], mod_ref[:, D : 2 * D])) + spread(
            hot_ref[...], mod_ref[:, 2 * D :]
        )
        nm_ref[...] = out.astype(bf16)
        nm_t_ref[...] = flip(out)


def attend_first(na, w, bias):
    steps = w.shape[1] // (4 * PAIR)
    return kernel_call(
        attend_first_kernel,
        (steps,),
        [whole(LEN, D), columns(D, 4 * PAIR), whole(LEN, LEN)],
        [columns(LEN, PAIR), whole(LEN, D)],
        [sds((LEN, steps * PAIR), bf16), sds((LEN, D), f32)],
        steps * ATTEND_FLOPS,
    )(na, w, bias)


def attend_last(na, w, bias, part, tokens, hot, mod):
    steps = w.shape[1] // (4 * PAIR)
    return kernel_call(
        attend_last_kernel,
        (steps,),
        [
            whole(LEN, D),
            columns(D, 4 * PAIR),
            whole(LEN, LEN),
            ANYWHERE,
            whole(LEN, D),
            whole(LEN, 24),
            whole(ITEMS, 3 * D),
        ],
        [columns(LEN, PAIR), whole(LEN, D), whole(LEN, D), whole(LEN, D), whole(D, LEN)],
        [
            sds((LEN, steps * PAIR), bf16),
            sds((LEN, D), f32),
            sds((LEN, D), f32),
            sds((LEN, D), bf16),
            sds((D, LEN), bf16),
        ],
        steps * ATTEND_FLOPS,
        held_scratch(1),
    )(na, w, bias, part, tokens, hot, mod)


def attend_pair_back(na_ref, na_t_ref, go_ref, go_t_ref, o_ref, w_ref, bias_ref, dw_ref):
    raw = matmul(na_ref[...], w_ref[:, : 3 * PAIR])
    grad_att = matmul(go_ref[...], w_ref[:, 3 * PAIR :]).astype(bf16)
    results = [[], [], []]
    for head in range(2):
        cut = [slice(i * PAIR + head * HEAD_WIDTH, i * PAIR + (head + 1) * HEAD_WIDTH) for i in range(3)]
        query, key = raw[:, cut[0]], raw[:, cut[1]]
        query_f, query_n = unit_pair(query)
        key_f, key_n = unit_pair(key)
        value_b = raw[:, cut[2]].astype(bf16)
        grad_out = grad_att[:, head * HEAD_WIDTH : (head + 1) * HEAD_WIDTH]
        grad_q, grad_k, grad_v = [], 0.0, 0.0
        for low, high in ((0, 384), (384, LEN)):
            raised = jnp.exp2(matmul_nt(key_n, query_n[low:high]) * SCORE_POWER + bias_ref[:, low:high])
            attention = raised * (1.0 / jnp.sum(raised, axis=0, keepdims=True))
            grad_probs = matmul_nt(value_b, grad_out[low:high])
            row_dot = jnp.sum(attention * grad_probs, axis=0, keepdims=True)
            grad_scores = (attention * (grad_probs - row_dot)).astype(bf16)
            grad_v = grad_v + matmul(attention.astype(bf16), grad_out[low:high])
            grad_k = grad_k + matmul(grad_scores, query_n[low:high])
            grad_q.append(matmul_tn(key_n, grad_scores).T)
        grad_q = jnp.concatenate(grad_q, axis=0) * SCORE_SCALE
        results[0].append(unit_back(query, query_f, grad_q))
        results[1].append(unit_back(key, key_f, grad_k * SCORE_SCALE))
        results[2].append(grad_v.astype(bf16))
    grad_raw = jnp.concatenate([part for pair in results for part in pair], axis=1)
    dw_ref[:, : 3 * PAIR] = matmul(na_t_ref[...], grad_raw).astype(bf16)
    dw_ref[:, 3 * PAIR :] = matmul(go_t_ref[...], o_ref[...]).astype(bf16)
    return matmul_nt(grad_raw, w_ref[:, : 3 * PAIR])


def attend_back_first_kernel(na_ref, na_t_ref, go_ref, go_t_ref, o_ref, w_ref, bias_ref, dw_ref, acc_ref):
    add_up(acc_ref, attend_pair_back(na_ref, na_t_ref, go_ref, go_t_ref, o_ref, w_ref, bias_ref, dw_ref))


def attend_back_last_kernel(
    na_ref, na_t_ref, go_ref, go_t_ref, o_ref, w_ref, bias_ref,
    part_ref, tok_ref, gm_ref, hot_ref, hot_t_ref, mod_ref,
    dw_ref, gt_ref, items_ref, acc_ref, held, sems,
):
    arrive = held_back([part_ref, gm_ref], held, sems)
    add_up(acc_ref, attend_pair_back(na_ref, na_t_ref, go_ref, go_t_ref, o_ref, w_ref, bias_ref, dw_ref))

    @at_end
    def _():
        arrive()
        grad = acc_ref[...] + held[0]
        hat, factor = normed(tok_ref[...].astype(f32))
        items_ref[:, :D] = item_sum(hot_t_ref[...], grad * hat)
        items_ref[:, D:] = item_sum(hot_t_ref[...], grad)
        inner = normed_back(hat, factor, grad * (1.0 + spread(hot_ref[...], mod_ref[...])))
        gt_ref[...] = (held[1] + inner).astype(bf16)


def attend_back_specs():
    return [
        whole(LEN, D),
        whole(D, LEN),
        whole(LEN, D),
        whole(D, LEN),
        columns(LEN, PAIR),
        columns(D, 4 * PAIR),
        whole(LEN, LEN),
    ]


def attend_back_first(na, na_t, go, go_t, out, w, bias_t):
    steps = w.shape[1] // (4 * PAIR)
    return kernel_call(
        attend_back_first_kernel,
        (steps,),
        attend_back_specs(),
        [columns(D, 4 * PAIR), whole(LEN, D)],
        [sds(w.shape, bf16), sds((LEN, D), f32)],
        3 * steps * ATTEND_FLOPS,
    )(na, na_t, go, go_t, out, w, bias_t)


def attend_back_last(na, na_t, go, go_t, out, w, bias_t, part, tokens, grad_middle, hot, hot_t, mod):
    steps = w.shape[1] // (4 * PAIR)
    return kernel_call(
        attend_back_last_kernel,
        (steps,),
        attend_back_specs()
        + [
            ANYWHERE,
            whole(LEN, D),
            ANYWHERE,
            whole(LEN, 24),
            whole(2 * ITEMS, LEN),
            whole(ITEMS, D),
        ],
        [columns(D, 4 * PAIR), whole(LEN, D), whole(2 * ITEMS, 2 * D)],
        [sds(w.shape, bf16), sds((LEN, D), bf16), sds((2 * ITEMS, 2 * D), f32)],
        3 * steps * ATTEND_FLOPS,
        [pltpu.VMEM((LEN, D), f32)] + held_scratch(2),
    )(na, na_t, go, go_t, out, w, bias_t, part, tokens, grad_middle, hot, hot_t, mod)


def mlp_part(nm_ref, w_refs, h_refs):
    total = 0.0
    for w_ref, h_ref in zip(w_refs, h_refs):
        hidden = matmul(nm_ref[...], w_ref[:, :BLOCK])
        h_ref[...] = hidden
        _, active = gelu_parts(hidden)
        total = total + matmul_nt(active.astype(bf16), w_ref[:, BLOCK:])
    return total


def mlp_first_kernel(nm_ref, w0_ref, w1_ref, h0_ref, h1_ref, acc_ref):
    add_up(acc_ref, mlp_part(nm_ref, (w0_ref, w1_ref), (h0_ref, h1_ref)))


def mlp_last_kernel(
    nm_ref, w0_ref, w1_ref, part_ref, mid_ref, hot_ref, mod_ref, h0_ref, h1_ref, acc_ref, res_ref, nh_ref, nh_t_ref,
    held, sems,
):
    arrive = held_back([part_ref, mid_ref], held, sems)
    add_up(acc_ref, mlp_part(nm_ref, (w0_ref, w1_ref), (h0_ref, h1_ref)))

    @at_end
    def _():
        arrive()
        acc_ref[...] += held[0]
        residual = held[1] + spread(hot_ref[...], mod_ref[...]) * acc_ref[...]
        res_ref[...] = residual
        hat, _ = normed(residual)
        nh_ref[...] = hat.astype(bf16)
        nh_t_ref[...] = flip(hat)


def mlp_first(nm, ws):
    steps = ws[0].shape[1] // (2 * BLOCK)
    hidden = sds((LEN, steps * BLOCK), f32)
    *hiddens, acc = kernel_call(
        mlp_first_kernel,
        (steps,),
        [whole(LEN, D)] + [columns(D, 2 * BLOCK)] * 2,
        [columns(LEN, BLOCK)] * 2 + [whole(LEN, D)],
        [hidden, hidden, sds((LEN, D), f32)],
        8 * steps * LEN * D * BLOCK,
    )(nm, *ws)
    return hiddens, acc


def mlp_last(nm, ws, part, middle, hot, mod):
    steps = ws[0].shape[1] // (2 * BLOCK)
    hidden = sds((LEN, steps * BLOCK), f32)
    h0, h1, *rest = kernel_call(
        mlp_last_kernel,
        (steps,),
        [whole(LEN, D)]
        + [columns(D, 2 * BLOCK)] * 2
        + [ANYWHERE, ANYWHERE, whole(LEN, 24), whole(ITEMS, D)],
        [columns(LEN, BLOCK)] * 2 + [whole(LEN, D), whole(LEN, D), whole(LEN, D), whole(D, LEN)],
        [
            hidden,
            hidden,
            sds((LEN, D), f32),
            sds((LEN, D), f32),
            sds((LEN, D), bf16),
            sds((D, LEN), bf16),
        ],
        8 * steps * LEN * D * BLOCK,
        held_scratch(2),
    )(nm, *ws, part, middle, hot, mod)
    return [h0, h1], *rest


def mlp_part_back(nm_t_ref, g_ref, g_t_ref, h_refs, w_refs, dw_ref):
    total = 0.0
    for i, (h_ref, w_ref) in enumerate(zip(h_refs, w_refs)):
        hidden = h_ref[...]
        cdf, active = gelu_parts(hidden)
        at = 2 * i * BLOCK
        dw_ref[:, at + BLOCK : at + 2 * BLOCK] = matmul(g_t_ref[...], active.astype(bf16)).astype(bf16)
        grad_pre = (gelu_slope(hidden, cdf) * matmul(g_ref[...], w_ref[:, BLOCK:])).astype(bf16)
        dw_ref[:, at : at + BLOCK] = matmul(nm_t_ref[...], grad_pre).astype(bf16)
        total = total + matmul_nt(grad_pre, w_ref[:, :BLOCK])
    return total


def mlp_back_first_kernel(nm_t_ref, g_ref, g_t_ref, h0_ref, h1_ref, w0_ref, w1_ref, dw_ref, acc_ref):
    add_up(acc_ref, mlp_part_back(nm_t_ref, g_ref, g_t_ref, (h0_ref, h1_ref), (w0_ref, w1_ref), dw_ref))


def mlp_back_last_kernel(
    nm_t_ref, g_ref, g_t_ref, h0_ref, h1_ref, w0_ref, w1_ref,
    part_ref, mid_ref, gr_ref, out_ref, hot_ref, hot_t_ref, mod_ref,
    dw_ref, gm_ref, go_ref, go_t_ref, items_ref, acc_ref, held, sems,
):
    arrive = held_back([part_ref, mid_ref, out_ref, gr_ref], held, sems, [gm_ref])
    add_up(acc_ref, mlp_part_back(nm_t_ref, g_ref, g_t_ref, (h0_ref, h1_ref), (w0_ref, w1_ref), dw_ref))

    @at_end
    def _():
        arrive()
        grad = acc_ref[...] + held[0]
        hat, factor = normed(held[1])
        items_ref[:, D : 2 * D] = item_sum(hot_t_ref[...], grad * hat)
        items_ref[:, 2 * D :] = item_sum(hot_t_ref[...], grad)
        grad_middle = gm_ref[...] + normed_back(
            hat, factor, grad * (1.0 + spread(hot_ref[...], mod_ref[:, D:]))
        )
        gm_ref[...] = grad_middle
        items_ref[:, :D] = item_sum(hot_t_ref[...], grad_middle * held[2])
        grad_out = spread(hot_ref[...], mod_ref[:, :D]) * grad_middle
        go_ref[...] = grad_out.astype(bf16)
        go_t_ref[...] = flip(grad_out)


def mlp_back_specs():
    return (
        [whole(D, LEN), whole(LEN, D), whole(D, LEN)]
        + [columns(LEN, BLOCK)] * 2
        + [columns(D, 2 * BLOCK)] * 2
    )


def mlp_back_first(nm_t, g, g_t, hiddens, ws):
    steps = ws[0].shape[1] // (2 * BLOCK)
    return kernel_call(
        mlp_back_first_kernel,
        (steps,),
        mlp_back_specs(),
        [columns(D, 4 * BLOCK), whole(LEN, D)],
        [sds((D, 4 * steps * BLOCK), bf16), sds((LEN, D), f32)],
        16 * steps * LEN * D * BLOCK,
    )(nm_t, g, g_t, *hiddens, *ws)


def mlp_back_last(nm_t, g, g_t, hiddens, ws, part, middle, grad_res, attn_out, hot, hot_t, mod):
    steps = ws[0].shape[1] // (2 * BLOCK)
    return kernel_call(
        mlp_back_last_kernel,
        (steps,),
        mlp_back_specs()
        + [ANYWHERE] * 4
        + [whole(LEN, 24), whole(2 * ITEMS, LEN), whole(ITEMS, 2 * D)],
        [
            columns(D, 4 * BLOCK),
            whole(LEN, D),
            whole(LEN, D),
            whole(D, LEN),
            whole(2 * ITEMS, 3 * D),
        ],
        [
            sds((D, 4 * steps * BLOCK), bf16),
            sds((LEN, D), f32),
            sds((LEN, D), bf16),
            sds((D, LEN), bf16),
            sds((2 * ITEMS, 3 * D), f32),
        ],
        16 * steps * LEN * D * BLOCK,
        [pltpu.VMEM((LEN, D), f32)] + held_scratch(3, 4),
    )(nm_t, g, g_t, *hiddens, *ws, part, middle, grad_res, attn_out, hot, hot_t, mod)


def head_kernel(
    nh_ref, nh_t_ref, own_ref, peer_ref, target_ref, weight_ref, res_ref, mlp_ref, hot_ref, hot_t_ref, mod_ref,
    dw_own_ref, dw_peer_ref, loss_ref, gr_ref, gmo_ref, gmo_t_ref, items_ref,
    logits, most, total, chosen, acc, held, sems,
):
    arrive = held_back([res_ref, mlp_ref], held, sems)
    step = pl.program_id(0)
    half = pl.num_programs(0) // 2
    block = own_ref.shape[1]
    lane = lax.broadcasted_iota(jnp.int32, (LEN, block), 1)

    @pl.when(step == 0)
    def _():
        most[...] = jnp.full((LEN, 1), -1e30, f32)
        total[...] = jnp.zeros((LEN, 1), f32)
        chosen[...] = jnp.zeros((LEN, 1), f32)

    for which, w_ref, dw_ref in ((0, own_ref, dw_own_ref), (1, peer_ref, dw_peer_ref)):

        @pl.when(step < half)
        def _():
            place = step + which * half
            values = matmul(nh_ref[...], w_ref[...])
            logits[place] = values
            most_new = jnp.maximum(most[...], jnp.max(values, axis=1, keepdims=True))
            total[...] = total[...] * jnp.exp(most[...] - most_new) + jnp.sum(
                jnp.exp(values - most_new), axis=1, keepdims=True
            )
            most[...] = most_new
            is_target = lane + place * block == target_ref[...]
            chosen[...] += jnp.sum(jnp.where(is_target, values, 0.0), axis=1, keepdims=True)

    @pl.when(step == half - 1)
    def _():
        most[...] = most[...] + jnp.log(total[...])
        loss = jnp.sum(weight_ref[...] * (most[...] - chosen[...]), axis=0, keepdims=True)
        loss_ref[...] = jnp.broadcast_to(loss, (8, 128))

    for which, w_ref, dw_ref in ((0, own_ref, dw_own_ref), (1, peer_ref, dw_peer_ref)):

        @pl.when(step >= half)
        def _():
            place = step - half + which * half
            is_target = lane + place * block == target_ref[...]
            grad = (jnp.exp(logits[place] - most[...]) - is_target.astype(f32)) * weight_ref[...]
            grad = grad.astype(bf16)
            dw_ref[...] = matmul(nh_t_ref[...], grad).astype(bf16)
            part = matmul_nt(grad, w_ref[...])

            @pl.when(jnp.logical_and(step == half, which == 0))
            def _():
                acc[...] = part

            @pl.when(jnp.logical_not(jnp.logical_and(step == half, which == 0)))
            def _():
                acc[...] += part

    @at_end
    def _():
        arrive()
        hat, factor = normed(held[0])
        grad_res = normed_back(hat, factor, acc[...])
        gr_ref[...] = grad_res
        items_ref[...] = item_sum(hot_t_ref[...], grad_res * held[1])
        grad_mlp = spread(hot_ref[...], mod_ref[...]) * grad_res
        gmo_ref[...] = grad_mlp.astype(bf16)
        gmo_t_ref[...] = flip(grad_mlp)


def head(nh, nh_t, own, peer, target, weight, residual, mlp_out, hot, hot_t, mod):
    half = own.shape[1] // BLOCK
    w_spec = pl.BlockSpec((D, BLOCK), lambda i: (0, i % half))
    dw_spec = pl.BlockSpec((D, BLOCK), lambda i: (0, jnp.maximum(i - half, 0)))
    return kernel_call(
        head_kernel,
        (2 * half,),
        [
            whole(LEN, D),
            whole(D, LEN),
            w_spec,
            w_spec,
            whole(LEN, 1),
            whole(LEN, 1),
            ANYWHERE,
            ANYWHERE,
            whole(LEN, 24),
            whole(2 * ITEMS, LEN),
            whole(ITEMS, D),
        ],
        [
            dw_spec,
            dw_spec,
            whole(8, 128),
            whole(LEN, D),
            whole(LEN, D),
            whole(D, LEN),
            whole(2 * ITEMS, D),
        ],
        [
            sds(own.shape, bf16),
            sds(own.shape, bf16),
            sds((8, 128), f32),
            sds((LEN, D), f32),
            sds((LEN, D), bf16),
            sds((D, LEN), bf16),
            sds((2 * ITEMS, D), f32),
        ],
        12 * half * LEN * D * BLOCK,
        [
            pltpu.VMEM((2 * half, LEN, BLOCK), f32),
            pltpu.VMEM((LEN, 1), f32),
            pltpu.VMEM((LEN, 1), f32),
            pltpu.VMEM((LEN, 1), f32),
            pltpu.VMEM((LEN, D), f32),
            *held_scratch(2),
        ],
    )(nh, nh_t, own, peer, target, weight, residual, mlp_out, hot, hot_t, mod)


def code_first_kernel(code_ref, gt_ref, turn_ref, out_ref, flat_ref):
    step, steps = pl.program_id(0), pl.num_programs(0)
    rows = out_ref.shape[0]

    @pl.when(step == 0)
    def _():
        flat_ref[...] = matmul_nt(gt_ref[...], turn_ref[...]).astype(bf16)

    row = lax.broadcasted_iota(jnp.int32, (rows, LEN), 0) + (step + steps) * rows
    out_ref[...] = matmul((row == code_ref[...]).astype(bf16), flat_ref[...]).astype(bf16)


def code_last_kernel(code_ref, flat_ref, out_ref):
    rows = out_ref.shape[0]
    row = lax.broadcasted_iota(jnp.int32, (rows, LEN), 0) + pl.program_id(0) * rows
    out_ref[...] = matmul((row == code_ref[...]).astype(bf16), flat_ref[...]).astype(bf16)


def code_back_first(code_rows, grad_tokens, turn, rows):
    spec = pl.BlockSpec((rows // 4, D), lambda i: (i, 0))
    out, flat = kernel_call(
        code_first_kernel,
        (4,),
        [whole(1, LEN), whole(LEN, D), whole(D, D)],
        [spec, whole(LEN, D)],
        [sds((rows, D), bf16), sds((LEN, D), bf16)],
        2 * LEN * rows * D,
    )(code_rows, grad_tokens, turn)
    return code_rows, flat, out


def code_back_last(code_rows, flat, rows):
    spec = pl.BlockSpec((rows // 4, D), lambda i: (i, 0))
    return kernel_call(
        code_last_kernel,
        (4,),
        [whole(1, LEN), whole(LEN, D)],
        spec,
        sds((rows, D), bf16),
        2 * LEN * rows * D,
    )(code_rows, flat)


def step_rates():
    return (
        2.5,
        2.5,
        2.5 / math.sqrt(D),
        2.5 / math.sqrt(D),
        2.5 / math.sqrt(D // 32),
        2.5 / math.sqrt(D),
        2.5 / math.sqrt(FF),
        5.0 / math.sqrt(D),
    )


def adamw_update(weight, grad, moment, square, rate):
    first = BETA_ONE * moment + (1.0 - BETA_ONE) * grad
    second = BETA_TWO * square + (1.0 - BETA_TWO) * grad * grad
    corrected = (
        first / (1.0 - BETA_ONE**STEP) / (jnp.sqrt(second / (1.0 - BETA_TWO**STEP)) + ADAM_EPSILON)
    )
    return (first, second, weight - rate * (corrected + DECAY * weight))


def on_device(
    input_codes,
    target_codes,
    item_lengths,
    item_labels,
    code_table,
    class_table,
    adaln_weight,
    qkv_weight,
    proj_weight,
    expand_weight,
    contract_weight,
    head_weight,
    code_moment,
    class_moment,
    adaln_moment,
    qkv_moment,
    proj_moment,
    expand_moment,
    contract_moment,
    head_moment,
    code_square,
    class_square,
    adaln_square,
    qkv_square,
    proj_square,
    expand_square,
    contract_square,
    head_square,
):
    masters = (
        code_table,
        class_table,
        adaln_weight,
        qkv_weight,
        proj_weight.T,
        expand_weight,
        contract_weight.T,
        head_weight,
    )
    moments = (
        code_moment,
        class_moment,
        adaln_moment,
        qkv_moment,
        proj_moment.T,
        expand_moment,
        contract_moment.T,
        head_moment,
    )
    squares = (
        code_square,
        class_square,
        adaln_square,
        qkv_square,
        proj_square.T,
        expand_square,
        contract_square.T,
        head_square,
    )
    n = lax.axis_size("dp")
    core = lax.axis_index("mp")
    rows = code_table.shape[0]
    half_rows = rows // 2
    width = proj_weight.shape[0]
    wide = expand_weight.shape[1]
    codes_local = head_weight.shape[1]

    def mine(values):
        return lax.dynamic_index_in_dim(values, core, 0, keepdims=False)

    pairs = width // PAIR
    code_block = lax.dynamic_slice_in_dim(code_table, core * half_rows, half_rows, 0).astype(bf16)
    attn_block = jnp.stack([qkv_weight[0], qkv_weight[1], qkv_weight[2], proj_weight.T], axis=1)
    attn_block = attn_block.reshape(-1, 4, pairs, PAIR).swapaxes(1, 2).reshape(-1, 4 * width)
    blocks = wide // BLOCK
    mlp_blocks = jnp.stack(
        [expand_weight.reshape(-1, blocks, BLOCK), contract_weight.T.reshape(-1, blocks, BLOCK)], axis=2
    ).astype(bf16)
    code_w, attn_w, mlp_a, mlp_b, head_w = [
        Gather(block, behind)
        for block, behind in (
            (code_block, False),
            (attn_block.astype(bf16), False),
            (mlp_blocks[:, 0::2].reshape(-1, wide), True),
            (mlp_blocks[:, 1::2].reshape(-1, wide), True),
            (head_weight.astype(bf16), True),
        )
    ]
    begin = Ticks()
    begin([code_w])
    numbers = small_gather(jnp.stack([item_lengths[:, 0], item_labels[:, 0]], axis=1))
    positions = jnp.arange(n, dtype=jnp.int32)
    block_at = ((lax.axis_index("dp") & 3) ^ (positions // quarter())) + 4 * (positions % quarter())
    block_place = place_of(positions)
    labels = numbers[:, :, 1]
    labels_own = jnp.where(core == 0, labels[:, 0], labels[:, 1])
    labels_peer = jnp.where(core == 0, labels[:, 1], labels[:, 0])
    class_low = class_table.astype(bf16)
    adaln_low = adaln_weight.astype(bf16)

    def class_part(item_labels):
        ids = jnp.arange(CLASSES, dtype=jnp.int32)
        picked = (item_labels.reshape(-1, 1) == ids[None, :]).astype(bf16)
        class_rows = matmul(picked, class_low)
        return picked, class_rows, jax.nn.silu(class_rows).astype(bf16)

    _, _, class_vec = class_part(labels_own[block_at])
    order = (2, 4, 0, 1, 3, 5)
    adaln_parts = jnp.concatenate([adaln_low[:, i * D : (i + 1) * D] for i in order], axis=1)

    mod_parts = matmul(class_vec, adaln_parts)

    mod_job = Scatter(None, mod_parts, dtype=f32)
    attn_w.block, mod_job.own = begin.wait((attn_w.block, mod_job.own))
    begin([code_w, attn_w, mod_job, mlp_a])
    begin.wait()
    lengths = mine(item_lengths)[0]
    code_ids = mine(input_codes)[0]
    target_ids = mine(target_codes)[0]
    segment, scale_id, usable = layout(lengths)
    bounds = jnp.array((0,) + PYRAMID, dtype=jnp.int32)
    sizes = jnp.array(PYRAMID + (LEN,), dtype=jnp.int32) - bounds
    all_lengths = numbers[:, :, 0].reshape(-1)
    scale_counts = jnp.sum(
        jnp.clip(all_lengths[:, None] - bounds[None, :], 0, sizes[None, :]), axis=0
    ).astype(f32)
    inv_counts = 1.0 / (NSCALES * jnp.maximum(scale_counts, 1.0))
    scale_hot = scale_id[:, None] == jnp.arange(NSCALES, dtype=jnp.int32)[None, :]
    token_weight = jnp.where(
        usable, jnp.sum(jnp.where(scale_hot, inv_counts[None, :], 0.0), axis=1), 0.0
    )
    same = segment[:, None] == segment[None, :]
    bias = jnp.where(same & (scale_id[None, :] <= scale_id[:, None]), 0.0, -1e30)
    bias_t = jnp.where(same & (scale_id[:, None] <= scale_id[None, :]), 0.0, -1e30)
    hot = (segment[:, None] == jnp.arange(3 * ITEMS, dtype=jnp.int32)[None, :] % ITEMS).astype(bf16)
    item_rows = jnp.arange(2 * ITEMS, dtype=jnp.int32)
    hot_t = ((segment[None, :] == item_rows[:, None]) & (item_rows[:, None] < ITEMS)).astype(bf16)

    block_width = D // n
    feature_place = (block_place[:, None] * block_width + jnp.arange(block_width)[None, :]).reshape(-1)
    turn = (feature_place[:, None] == jnp.arange(D, dtype=jnp.int32)[None, :]).astype(bf16)
    within = code_ids % rows
    other = (within // half_rows != core).astype(jnp.int32)
    code_rows = other * (n * half_rows) + place_of(code_ids // rows) * half_rows + within % half_rows
    target = jnp.where(target_ids // codes_local == core, 0, codes_local) + target_ids % codes_local

    begin([code_w, mod_job])
    mlp_a.group, bias, bias_t, turn, hot, hot_t, code_rows, target, token_weight = begin.wait(
        (mlp_a.group, bias, bias_t, turn, hot, hot_t, code_rows, target, token_weight)
    )
    begin([code_w, attn_w, mlp_b, mod_job])
    begin.wait()

    def placed(values):
        values = values.reshape(-1, n, block_width)
        return jnp.take(values, block_at, axis=1).reshape(ITEMS, -1)

    def beside(*parts):
        return jnp.concatenate(parts, axis=1)

    mods_embed = placed(mod_job.total[:, : 2 * D])
    scale_attn = mods_embed[:, :D]
    code_col = code_rows.reshape(LEN, 1)

    code_own, code_peer, code_col = begin(
        [attn_w, mlp_a, head_w], (code_w.own, code_w.peer, code_col)
    )
    tokens, na, na_t = begin.wait(embed(code_col, code_own, code_peer, turn, hot, mods_embed))
    na = begin([attn_w, mlp_a, mlp_b], na)
    att_own, part = begin.wait(attend_first(na, attn_w.own, bias))
    mods = placed(mod_job.total[:, 2 * D :])
    gate_attn, gate_mlp, scale_mlp, shift_mlp = jnp.split(mods, 4, axis=1)
    mods_attend = beside(gate_attn, scale_mlp, shift_mlp)
    mods_back = beside(gate_attn, scale_mlp)
    part = begin([mlp_a, mlp_b, head_w], part)
    att_peer, attn_out, middle, nm, nm_t = begin.wait(
        attend_last(na, attn_w.peer, bias, part, tokens, hot, mods_attend)
    )
    nm = begin([mlp_b, head_w], nm)
    mlp_own = (mlp_a.own, mlp_b.own)
    hidden_own, part = begin.wait(mlp_first(nm, mlp_own))
    mlp_peer = (mlp_a.peer, mlp_b.peer)
    part = begin([head_w], part)
    hidden_peer, mlp_out, residual, nh, nh_t = begin.wait(
        mlp_last(nm, mlp_peer, part, middle, hot, gate_mlp)
    )
    dhead_own, dhead_peer, loss_tile, grad_res, gmo, gmo_t, items_head = head(
        nh, nh_t, head_w.own, head_w.peer, target.reshape(LEN, 1), token_weight.reshape(LEN, 1),
        residual, mlp_out, hot, hot_t, gate_mlp,
    )
    loss_local = loss_tile[0, 0]

    def turned(parts):
        values = beside(*parts)
        values = jnp.take(values.reshape(-1, n, block_width), block_place, axis=1)
        return values.reshape(ITEMS, -1).astype(bf16)

    head_job = Scatter(dhead_peer, dhead_own, behind=True, wide=True)
    gmo = begin([head_job], gmo)
    dmlp_peer, part = begin.wait(mlp_back_first(nm_t, gmo, gmo_t, hidden_peer, mlp_peer))
    mlp_job = Scatter(dmlp_peer, behind=True)
    part = begin([head_job, mlp_job], part)
    mlp_job.own, grad_middle, gao, gao_t, items_mlp = begin.wait(
        mlp_back_last(
            nm_t, gmo, gmo_t, hidden_own, mlp_own, part, middle, grad_res, attn_out, hot, hot_t, mods_back
        )
    )
    item_job = Exchange(turned([items_mlp[:ITEMS, :D], items_head[:ITEMS], items_mlp[:ITEMS, D:]]), behind=True)
    gao = begin([head_job, mlp_job, item_job], gao)
    dattn_peer, part = begin.wait(attend_back_first(na, na_t, gao, gao_t, att_peer, attn_w.peer, bias_t))
    attn_job = Scatter(dattn_peer, behind=True)
    part = begin([head_job, mlp_job, attn_job], part)
    attn_job.own, grad_tokens, items_attn = begin.wait(
        attend_back_last(
            na, na_t, gao, gao_t, att_own, attn_w.own, bias_t, part, tokens, grad_middle, hot, hot_t, scale_attn
        )
    )
    late_job = Exchange(turned([items_attn[:ITEMS]]))
    grad_tokens = begin([attn_job, late_job, mlp_job], grad_tokens)
    code_row, flat, dcode_peer = begin.wait(
        code_back_first(code_rows.reshape(1, LEN), grad_tokens, turn, n * half_rows)
    )
    code_job = Scatter(dcode_peer)
    flat = begin([code_job, attn_job], flat)
    code_job.own = begin.wait(code_back_last(code_row, flat, n * half_rows))
    begin([code_job, item_job, late_job, attn_job])
    begin.wait()
    begin([code_job])
    begin.wait()
    head_job.total, mlp_job.total = begin([code_job], (head_job.total, mlp_job.total))
    begin.wait()

    def factor_part(item_labels, grads):
        picked, class_rows, class_vec = class_part(item_labels)
        grad_class_vec = matmul_nt(grads, adaln_low)
        _, silu_back = jax.vjp(jax.nn.silu, class_rows)
        return matmul_tn(class_vec, grads), exact_tn(picked.astype(f32), silu_back(grad_class_vec)[0])

    def grad_rows(which):
        early, late = getattr(item_job, which), getattr(late_job, which)
        order = [early[:, : 2 * D], late[:, :D], early[:, 2 * D : 3 * D], late[:, D:], early[:, 3 * D :]]
        return beside(*order)

    adaln_a, class_a = factor_part(labels_own, grad_rows("own"))
    adaln_b, class_b = factor_part(labels_peer, grad_rows("peer"))
    adaln_grad = adaln_a + adaln_b
    class_grad = class_a + class_b
    code_half = code_job.result()
    code_other = swap_core(code_half)
    code_grad = jnp.where(
        core == 0,
        jnp.concatenate([code_half, code_other]),
        jnp.concatenate([code_other, code_half]),
    )
    attn_grad = attn_job.result()
    kinds = attn_grad.reshape(-1, pairs, 4, PAIR).transpose(2, 0, 1, 3).reshape(4, -1, width)
    mlp_kinds = mlp_job.result().reshape(-1, blocks, 2, BLOCK)
    gradients = (
        code_grad,
        class_grad,
        adaln_grad,
        kinds[:3],
        kinds[3],
        mlp_kinds[:, :, 0].reshape(-1, wide),
        mlp_kinds[:, :, 1].reshape(-1, wide),
        head_job.result(),
    )
    shared_sq = jnp.sum(class_grad * class_grad) + jnp.sum(adaln_grad * adaln_grad)
    own_sq = jnp.sum(code_half * code_half) + jnp.sum(attn_grad * attn_grad)
    for grad in gradients[5:]:
        own_sq = own_sq + jnp.sum(grad * grad)
    totals = total_over_all(
        jnp.concatenate([(own_sq + 0.5 * shared_sq).reshape(1), loss_local.reshape(1)])
    )
    squared, loss = totals[0], totals[1]
    grad_norm = jnp.sqrt(squared)
    clip = jnp.minimum(1.0, CLIP_NORM / (grad_norm + 1e-06))
    firsts, seconds, updated = ([], [], [])
    for place, (weight, grad, moment, square, rate) in enumerate(
        zip(masters, gradients, moments, squares, step_rates())
    ):
        for kept, value in zip(
            (firsts, seconds, updated), adamw_update(weight, grad * clip, moment, square, rate)
        ):
            kept.append(value.T if place in (4, 6) else value)
    return (*firsts, *seconds, *updated, loss, scale_counts, grad_norm)


def solution(mesh):
    token_spec = P(None, "dp", None)
    weight_specs = (
        P("dp", None),
        P(None, "dp"),
        P("dp", None),
        P(None, "dp", "mp"),
        P("mp", "dp"),
        P("dp", "mp"),
        P("mp", "dp"),
        P("dp", "mp"),
    )
    return jax.shard_map(
        on_device,
        mesh=mesh,
        in_specs=(token_spec,) * 4 + weight_specs * 3,
        out_specs=weight_specs * 3 + (P(), P(), P()),
        check_vma=False,
    )
```

```python
import math

import jax
import jax.numpy as jnp
from jax import lax
from jax.experimental import pallas as pl
from jax.experimental.pallas import tpu as pltpu
from jax.sharding import PartitionSpec as P

D = 1024
HEAD_WIDTH = 64
FF = 4096
CLASSES = 1000
LEN = 800
ITEMS = 8
NSCALES = 10
MICRO = 2
STEP = 10


EPSILON = 1e-06
SOFTMAX_WARMTH = 12.0
CLIP_NORM = 0.001
BETA_ONE = 0.9
BETA_TWO = 0.95
DECAY = 0.05
ADAM_EPSILON = 1e-08
PYRAMID = (1, 5, 14, 30, 55, 91, 155, 255, 424)

SCORE_SCALE = SOFTMAX_WARMTH / HEAD_WIDTH
SCORE_POWER = SCORE_SCALE * math.log2(math.e)
GELU_C = math.sqrt(2.0 / math.pi)
PAIR = 2 * HEAD_WIDTH
BLOCK = 512
JOIN_BLOCK = 1024
ATTEND_FLOPS = LEN * PAIR * (8 * D + 4 * LEN)
VMEM_LIMIT = 60 * 2**20

bf16 = jnp.bfloat16
f32 = jnp.float32
barrier = lax.optimization_barrier


def swap(values, bits):
    n = lax.axis_size("dp")
    return lax.ppermute(values, "dp", [(i, i ^ bits) for i in range(n)])


def swap_core(values):
    return lax.ppermute(values, "mp", [(0, 1), (1, 0)])


def quarter():
    return lax.axis_size("dp") // 4


def columns_of_chips():
    n = lax.axis_size("dp")
    return [[xy + 4 * z for z in range(n // 4)] for xy in range(4)]


def over_z(values):
    return lax.all_to_all(values, "dp", 0, 0, tiled=True, axis_index_groups=columns_of_chips())


def sum_z(values):
    return lax.psum_scatter(values, "dp", scatter_dimension=0, axis_index_groups=columns_of_chips())


def join_kernel(*refs):
    parts, out = refs[:-1], refs[-1]
    at = 0
    for part in parts:
        rows = part.shape[0]
        out[at : at + rows, :] = part[...]
        at += rows


def join(parts):
    rows = sum(part.shape[0] for part in parts)
    total = parts[0].shape[1]
    return pl.pallas_call(
        join_kernel,
        grid=(total // JOIN_BLOCK,),
        in_specs=[pl.BlockSpec((part.shape[0], JOIN_BLOCK), lambda i: (0, i)) for part in parts],
        out_specs=pl.BlockSpec((rows, JOIN_BLOCK), lambda i: (0, i)),
        out_shape=jax.ShapeDtypeStruct((rows, total), parts[0].dtype),
    )(*parts)


class Gather:
    def __init__(self, block, behind=False):
        self.block = block
        self.behind = behind
        self.step = 0

    def request(self):
        if self.step == 0 and self.behind:
            return self.block
        if self.step == 0:
            return jnp.broadcast_to(self.block[None], (quarter(),) + self.block.shape)
        if self.step == 1:
            return self.group
        if self.step == 2:
            half = self.group.shape[0] // 2
            return (self.from_y[:half], self.from_x[half:])
        return self.own

    def send(self, values):
        self.step += 1
        if self.step == 1 and self.behind:
            self.group = lax.all_gather(values, "dp", axis=0, tiled=True, axis_index_groups=columns_of_chips())
            return None
        if self.step == 1:
            return over_z(values)
        if self.step == 2:
            return swap(values, 1), swap(values, 2)
        if self.step == 3:
            return swap(values[0], 1), swap(values[1], 2)
        return swap_core(values)

    def accept(self, out):
        if out is None:
            return
        if self.step == 1:
            self.group = out.reshape((-1,) + self.block.shape[1:])
        elif self.step == 2:
            self.from_x, self.from_y = out
        elif self.step == 3:
            self.own = join([self.group, self.from_x, self.from_y, *out])
        else:
            self.peer = out


class Exchange:
    def __init__(self, block, behind=False):
        self.block = block
        self.behind = behind
        self.step = 0

    def request(self):
        n = lax.axis_size("dp")
        if self.step == 1:
            return self.own
        return self.block if self.behind else jnp.broadcast_to(self.block[None], (n,) + self.block.shape)

    def send(self, values):
        self.step += 1
        if self.step == 2:
            return swap_core(values)
        if self.behind:
            self.own = lax.all_gather(values, "dp", axis=0, tiled=True)
            return None
        return lax.all_to_all(values, "dp", 0, 0, tiled=True)

    def accept(self, out):
        if self.step == 2:
            self.peer = out
        elif not self.behind:
            self.own = out.reshape(-1, out.shape[-1])


class Scatter:
    def __init__(self, peer, own=None, behind=False, wide=False, dtype=bf16):
        self.wide = wide
        self.dtype = dtype
        self.peer = peer
        self.own = own
        self.behind = behind
        self.step = 0 if peer is not None else 1

    def group(self, g, part=slice(None)):
        n = lax.axis_size("dp")
        shape = (4, n // 4, self.own.shape[0] // n) + self.own.shape[1:]
        total = self.own.reshape(shape)[g, part].astype(f32)
        if self.peer is not None:
            total = total + self.other.reshape(shape)[g, part].astype(f32)
        return total

    def request(self):
        if self.step == 0:
            return self.peer
        half = quarter() // 2
        low, high = slice(0, half), slice(half, None)
        if self.step == 1:
            values = (self.group(3, low), self.group(3, high))
        elif self.step == 2:
            values = (
                jnp.concatenate([self.group(1, low), self.group(1, high) + self.diagonal[1].astype(f32)]),
                jnp.concatenate([self.group(2, low) + self.diagonal[0].astype(f32), self.group(2, high)]),
            )
        else:
            values = self.group(0) + self.sides[0].astype(f32) + self.sides[1].astype(f32)
            if self.behind and self.wide:
                return values
        return jax.tree.map(lambda value: value.astype(self.dtype), values)

    def send(self, values):
        self.step += 1
        if self.step == 1:
            return swap_core(values)
        if self.step < 4:
            return swap(values[0], 1), swap(values[1], 2)
        if self.behind:
            self.total = sum_z(values).astype(f32)
            return None
        return over_z(values)

    def accept(self, out):
        if self.step == 1:
            self.other = out
        elif self.step == 2:
            self.diagonal = out
        elif self.step == 3:
            self.sides = out
        elif not self.behind:
            self.total = jnp.sum(out.astype(f32), axis=0)

    def result(self):
        return self.total


class Ticks:
    def __init__(self):
        self.last = []

    def wait(self, live=()):
        outs, live = barrier(([out for _, out in self.last], live))
        for (job, _), out in zip(self.last, outs):
            if out is not None:
                job.accept(out)
        self.last = []
        return live

    def __call__(self, jobs, live=()):
        values, live = barrier(([job.request() for job in jobs], live))
        self.last = [(job, job.send(value)) for job, value in zip(jobs, values)]
        return live


def small_gather(values):
    group = jnp.stack([values] + [swap(values, 4 * j) for j in range(1, quarter())])
    group = jnp.concatenate([group] + [swap(group, g) for g in (1, 2, 3)])
    apart = jnp.bitwise_xor(jnp.arange(4 * quarter(), dtype=jnp.int32), lax.axis_index("dp"))
    return jnp.take(group, (apart & 3) * quarter() + (apart >> 2), axis=0)


def total_over_all(values):
    count = lax.axis_size("dp") * lax.axis_size("mp")
    parts = jnp.broadcast_to(values[None], (count,) + values.shape)
    return jnp.sum(lax.all_to_all(parts, ("dp", "mp"), 0, 0, tiled=True), axis=0)


def place_of(index):
    apart = jnp.bitwise_xor(index, lax.axis_index("dp")) & 3
    return apart * quarter() + (index >> 2)


def layout(lengths):
    ends = jnp.cumsum(lengths)
    places = jnp.arange(LEN, dtype=jnp.int32)
    passed = places[:, None] >= ends[None, :]
    segment = jnp.sum(passed.astype(jnp.int32), axis=1)
    start = jnp.sum(jnp.where(passed, lengths[None, :], 0), axis=1)
    offset = places - start
    bounds = jnp.array(PYRAMID, dtype=jnp.int32)
    scale_id = jnp.sum((offset[:, None] >= bounds[None, :]).astype(jnp.int32), axis=1)
    usable = places < ends[-1]
    return (segment, scale_id, usable)


def matmul(left, right):
    return jnp.dot(left, right, preferred_element_type=f32)


def matmul_tn(left, right):
    return lax.dot_general(left, right, (((0,), (0,)), ((), ())), preferred_element_type=f32)


def matmul_nt(left, right):
    return lax.dot_general(left, right, (((1,), (1,)), ((), ())), preferred_element_type=f32)


def exact_tn(left, right):
    return lax.dot_general(
        left,
        right,
        (((0,), (0,)), ((), ())),
        precision=lax.Precision.HIGHEST,
        preferred_element_type=f32,
    )


def unit_pair(values):
    factor = lax.rsqrt(jnp.mean(values * values, axis=-1, keepdims=True) + EPSILON)
    return factor, (values * factor).astype(bf16)


def unit_back(values, factor, grad):
    inner = jnp.mean(grad * values, axis=-1, keepdims=True)
    return (factor * (grad - values * (factor * factor * inner))).astype(bf16)


def normed(values):
    centered = values - jnp.mean(values, axis=-1, keepdims=True)
    factor = lax.rsqrt(jnp.mean(centered * centered, axis=-1, keepdims=True) + EPSILON)
    return centered * factor, factor


def normed_back(hat, factor, grad):
    inner = jnp.mean(grad * hat, axis=-1, keepdims=True)
    return factor * (grad - jnp.mean(grad, axis=-1, keepdims=True) - hat * inner)


def spread(hot, part):
    high = part.astype(bf16).astype(f32)
    mid = (part - high).astype(bf16).astype(f32)
    low = part - high - mid
    return matmul(hot, jnp.concatenate([high, mid, low], axis=0).astype(bf16))


def item_sum(hot_t, values):
    high = values.astype(bf16)
    low = (values - high.astype(f32)).astype(bf16)
    return matmul(hot_t, high) + matmul(hot_t, low)


def flip(values):
    return values.astype(f32).T.astype(bf16)


def gelu_parts(values):
    inner = GELU_C * (values + 0.044715 * values * values * values)
    cdf = 0.5 * (1.0 + jnp.tanh(inner))
    return cdf, values * cdf


def gelu_slope(values, cdf):
    return cdf + values * (2.0 * cdf * (1.0 - cdf)) * (GELU_C * (1.0 + 0.134145 * values * values))


def whole(*shape):
    return pl.BlockSpec(shape, lambda *_: (0,) * len(shape), pipeline_mode=pl.Buffered(1))


def columns(rows, width):
    return pl.BlockSpec((rows, width), lambda i: (0, i))


def sds(shape, dtype):
    return jax.ShapeDtypeStruct(shape, dtype)


def kernel_call(body, grid, in_specs, out_specs, out_shape, flops, scratch=()):
    return pl.pallas_call(
        body,
        grid=grid,
        in_specs=in_specs,
        out_specs=out_specs,
        out_shape=out_shape,
        scratch_shapes=list(scratch),
        compiler_params=pltpu.CompilerParams(vmem_limit_bytes=VMEM_LIMIT),
        cost_estimate=pl.CostEstimate(flops=flops, transcendentals=0, bytes_accessed=2**24),
    )


def add_up(ref, part, start=None):
    first = pl.program_id(0) == 0

    @pl.when(first)
    def _():
        ref[...] = part if start is None else start[...] + part

    @pl.when(jnp.logical_not(first))
    def _():
        ref[...] += part


def held_back(refs, held, sems, into=()):
    def copies():
        places = [held.at[i] for i in range(len(refs) - len(into))] + list(into)
        return [pltpu.make_async_copy(ref, place, sems.at[i]) for i, (ref, place) in enumerate(zip(refs, places))]

    @pl.when(pl.program_id(0) == 0)
    def _():
        for copy in copies():
            copy.start()

    def arrive():
        for copy in copies():
            copy.wait()

    return arrive


ANYWHERE = pl.BlockSpec(memory_space=pl.ANY)


def held_scratch(count, copies=None):
    return [pltpu.VMEM((count, LEN, D), f32), pltpu.SemaphoreType.DMA((copies or count,))]


def at_end(fn):
    pl.when(pl.program_id(0) == pl.num_programs(0) - 1)(fn)


def embed_kernel(code_ref, own_ref, peer_ref, turn_ref, hot_ref, mod_ref, tok_ref, na_ref, na_t_ref, acc):
    step, steps = pl.program_id(0), pl.num_programs(0)
    rows = own_ref.shape[0]
    lane = lax.broadcasted_iota(jnp.int32, (LEN, rows), 1) + step * rows
    hot_own = (lane == code_ref[...]).astype(bf16)
    hot_peer = (lane + steps * rows == code_ref[...]).astype(bf16)
    add_up(acc, matmul(hot_own, own_ref[...]) + matmul(hot_peer, peer_ref[...]))

    @at_end
    def _():
        tokens = matmul(acc[...].astype(bf16), turn_ref[...])
        tok_ref[...] = tokens.astype(bf16)
        hat, _ = normed(tokens)
        out = hat * (1.0 + spread(hot_ref[...], mod_ref[:, :D])) + spread(hot_ref[...], mod_ref[:, D:])
        na_ref[...] = out.astype(bf16)
        na_t_ref[...] = flip(out)


def embed(code_rows, own, peer, turn, hot, mod):
    rows = own.shape[0]
    block = rows // 4
    rows_spec = pl.BlockSpec((block, D), lambda i: (i, 0))
    return kernel_call(
        embed_kernel,
        (4,),
        [whole(LEN, 1), rows_spec, rows_spec, whole(D, D), whole(LEN, 24), whole(ITEMS, 2 * D)],
        [whole(LEN, D), whole(LEN, D), whole(D, LEN)],
        [sds((LEN, D), bf16), sds((LEN, D), bf16), sds((D, LEN), bf16)],
        4 * LEN * rows * D,
        [pltpu.VMEM((LEN, D), f32)],
    )(code_rows, own, peer, turn, hot, mod)


def attend_pair(na_ref, w_ref, bias_ref):
    raw = matmul(na_ref[...], w_ref[:, : 3 * PAIR])
    outs = []
    for head in range(2):
        cut = [slice(i * PAIR + head * HEAD_WIDTH, i * PAIR + (head + 1) * HEAD_WIDTH) for i in range(3)]
        _, query_n = unit_pair(raw[:, cut[0]])
        _, key_n = unit_pair(raw[:, cut[1]])
        raised = jnp.exp2(matmul_nt(query_n, key_n) * SCORE_POWER + bias_ref[...])
        share = 1.0 / jnp.sum(raised, axis=-1, keepdims=True)
        outs.append(matmul((raised * share).astype(bf16), raw[:, cut[2]].astype(bf16)).astype(bf16))
    return jnp.concatenate(outs, axis=1)


def attend_first_kernel(na_ref, w_ref, bias_ref, out_ref, acc_ref):
    out = attend_pair(na_ref, w_ref, bias_ref)
    out_ref[...] = out
    add_up(acc_ref, matmul_nt(out, w_ref[:, 3 * PAIR :]))


def attend_last_kernel(
    na_ref, w_ref, bias_ref, part_ref, tok_ref, hot_ref, mod_ref, out_ref, acc_ref, mid_ref, nm_ref, nm_t_ref,
    held, sems,
):
    arrive = held_back([part_ref], held, sems)
    out = attend_pair(na_ref, w_ref, bias_ref)
    out_ref[...] = out
    add_up(acc_ref, matmul_nt(out, w_ref[:, 3 * PAIR :]))

    @at_end
    def _():
        arrive()
        acc_ref[...] += held[0]
        middle = tok_ref[...].astype(f32) + spread(hot_ref[...], mod_ref[:, :D]) * acc_ref[...]
        mid_ref[...] = middle
        hat, _ = normed(middle)
        out = hat * (1.0 + spread(hot_ref[...], mod_ref[:, D : 2 * D])) + spread(
            hot_ref[...], mod_ref[:, 2 * D :]
        )
        nm_ref[...] = out.astype(bf16)
        nm_t_ref[...] = flip(out)


def attend_first(na, w, bias):
    steps = w.shape[1] // (4 * PAIR)
    return kernel_call(
        attend_first_kernel,
        (steps,),
        [whole(LEN, D), columns(D, 4 * PAIR), whole(LEN, LEN)],
        [columns(LEN, PAIR), whole(LEN, D)],
        [sds((LEN, steps * PAIR), bf16), sds((LEN, D), f32)],
        steps * ATTEND_FLOPS,
    )(na, w, bias)


def attend_last(na, w, bias, part, tokens, hot, mod):
    steps = w.shape[1] // (4 * PAIR)
    return kernel_call(
        attend_last_kernel,
        (steps,),
        [
            whole(LEN, D),
            columns(D, 4 * PAIR),
            whole(LEN, LEN),
            ANYWHERE,
            whole(LEN, D),
            whole(LEN, 24),
            whole(ITEMS, 3 * D),
        ],
        [columns(LEN, PAIR), whole(LEN, D), whole(LEN, D), whole(LEN, D), whole(D, LEN)],
        [
            sds((LEN, steps * PAIR), bf16),
            sds((LEN, D), f32),
            sds((LEN, D), f32),
            sds((LEN, D), bf16),
            sds((D, LEN), bf16),
        ],
        steps * ATTEND_FLOPS,
        held_scratch(1),
    )(na, w, bias, part, tokens, hot, mod)


def attend_pair_back(na_ref, na_t_ref, go_ref, go_t_ref, o_ref, w_ref, bias_ref, dw_ref):
    raw = matmul(na_ref[...], w_ref[:, : 3 * PAIR])
    grad_att = matmul(go_ref[...], w_ref[:, 3 * PAIR :]).astype(bf16)
    results = [[], [], []]
    for head in range(2):
        cut = [slice(i * PAIR + head * HEAD_WIDTH, i * PAIR + (head + 1) * HEAD_WIDTH) for i in range(3)]
        query, key = raw[:, cut[0]], raw[:, cut[1]]
        query_f, query_n = unit_pair(query)
        key_f, key_n = unit_pair(key)
        value_b = raw[:, cut[2]].astype(bf16)
        grad_out = grad_att[:, head * HEAD_WIDTH : (head + 1) * HEAD_WIDTH]
        grad_q, grad_k, grad_v = [], 0.0, 0.0
        for low, high in ((0, 384), (384, LEN)):
            raised = jnp.exp2(matmul_nt(key_n, query_n[low:high]) * SCORE_POWER + bias_ref[:, low:high])
            attention = raised * (1.0 / jnp.sum(raised, axis=0, keepdims=True))
            grad_probs = matmul_nt(value_b, grad_out[low:high])
            row_dot = jnp.sum(attention * grad_probs, axis=0, keepdims=True)
            grad_scores = (attention * (grad_probs - row_dot)).astype(bf16)
            grad_v = grad_v + matmul(attention.astype(bf16), grad_out[low:high])
            grad_k = grad_k + matmul(grad_scores, query_n[low:high])
            grad_q.append(matmul_tn(key_n, grad_scores).T)
        grad_q = jnp.concatenate(grad_q, axis=0) * SCORE_SCALE
        results[0].append(unit_back(query, query_f, grad_q))
        results[1].append(unit_back(key, key_f, grad_k * SCORE_SCALE))
        results[2].append(grad_v.astype(bf16))
    grad_raw = jnp.concatenate([part for pair in results for part in pair], axis=1)
    dw_ref[:, : 3 * PAIR] = matmul(na_t_ref[...], grad_raw).astype(bf16)
    dw_ref[:, 3 * PAIR :] = matmul(go_t_ref[...], o_ref[...]).astype(bf16)
    return matmul_nt(grad_raw, w_ref[:, : 3 * PAIR])


def attend_back_first_kernel(na_ref, na_t_ref, go_ref, go_t_ref, o_ref, w_ref, bias_ref, dw_ref, acc_ref):
    add_up(acc_ref, attend_pair_back(na_ref, na_t_ref, go_ref, go_t_ref, o_ref, w_ref, bias_ref, dw_ref))


def attend_back_last_kernel(
    na_ref, na_t_ref, go_ref, go_t_ref, o_ref, w_ref, bias_ref,
    part_ref, tok_ref, gm_ref, hot_ref, hot_t_ref, mod_ref,
    dw_ref, gt_ref, items_ref, acc_ref, held, sems,
):
    arrive = held_back([part_ref, gm_ref], held, sems)
    add_up(acc_ref, attend_pair_back(na_ref, na_t_ref, go_ref, go_t_ref, o_ref, w_ref, bias_ref, dw_ref))

    @at_end
    def _():
        arrive()
        grad = acc_ref[...] + held[0]
        hat, factor = normed(tok_ref[...].astype(f32))
        items_ref[:, :D] = item_sum(hot_t_ref[...], grad * hat)
        items_ref[:, D:] = item_sum(hot_t_ref[...], grad)
        inner = normed_back(hat, factor, grad * (1.0 + spread(hot_ref[...], mod_ref[...])))
        gt_ref[...] = (held[1] + inner).astype(bf16)


def attend_back_specs():
    return [
        whole(LEN, D),
        whole(D, LEN),
        whole(LEN, D),
        whole(D, LEN),
        columns(LEN, PAIR),
        columns(D, 4 * PAIR),
        whole(LEN, LEN),
    ]


def attend_back_first(na, na_t, go, go_t, out, w, bias_t):
    steps = w.shape[1] // (4 * PAIR)
    return kernel_call(
        attend_back_first_kernel,
        (steps,),
        attend_back_specs(),
        [columns(D, 4 * PAIR), whole(LEN, D)],
        [sds(w.shape, bf16), sds((LEN, D), f32)],
        3 * steps * ATTEND_FLOPS,
    )(na, na_t, go, go_t, out, w, bias_t)


def attend_back_last(na, na_t, go, go_t, out, w, bias_t, part, tokens, grad_middle, hot, hot_t, mod):
    steps = w.shape[1] // (4 * PAIR)
    return kernel_call(
        attend_back_last_kernel,
        (steps,),
        attend_back_specs()
        + [
            ANYWHERE,
            whole(LEN, D),
            ANYWHERE,
            whole(LEN, 24),
            whole(2 * ITEMS, LEN),
            whole(ITEMS, D),
        ],
        [columns(D, 4 * PAIR), whole(LEN, D), whole(2 * ITEMS, 2 * D)],
        [sds(w.shape, bf16), sds((LEN, D), bf16), sds((2 * ITEMS, 2 * D), f32)],
        3 * steps * ATTEND_FLOPS,
        [pltpu.VMEM((LEN, D), f32)] + held_scratch(2),
    )(na, na_t, go, go_t, out, w, bias_t, part, tokens, grad_middle, hot, hot_t, mod)


def mlp_part(nm_ref, w_refs, h_refs):
    total = 0.0
    for w_ref, h_ref in zip(w_refs, h_refs):
        hidden = matmul(nm_ref[...], w_ref[:, :BLOCK])
        h_ref[...] = hidden
        _, active = gelu_parts(hidden)
        total = total + matmul_nt(active.astype(bf16), w_ref[:, BLOCK:])
    return total


def mlp_first_kernel(nm_ref, w0_ref, w1_ref, h0_ref, h1_ref, acc_ref):
    add_up(acc_ref, mlp_part(nm_ref, (w0_ref, w1_ref), (h0_ref, h1_ref)))


def mlp_last_kernel(
    nm_ref, w0_ref, w1_ref, part_ref, mid_ref, hot_ref, mod_ref, h0_ref, h1_ref, acc_ref, res_ref, nh_ref, nh_t_ref,
    held, sems,
):
    arrive = held_back([part_ref, mid_ref], held, sems)
    add_up(acc_ref, mlp_part(nm_ref, (w0_ref, w1_ref), (h0_ref, h1_ref)))

    @at_end
    def _():
        arrive()
        acc_ref[...] += held[0]
        residual = held[1] + spread(hot_ref[...], mod_ref[...]) * acc_ref[...]
        res_ref[...] = residual
        hat, _ = normed(residual)
        nh_ref[...] = hat.astype(bf16)
        nh_t_ref[...] = flip(hat)


def mlp_first(nm, ws):
    steps = ws[0].shape[1] // (2 * BLOCK)
    hidden = sds((LEN, steps * BLOCK), f32)
    *hiddens, acc = kernel_call(
        mlp_first_kernel,
        (steps,),
        [whole(LEN, D)] + [columns(D, 2 * BLOCK)] * 2,
        [columns(LEN, BLOCK)] * 2 + [whole(LEN, D)],
        [hidden, hidden, sds((LEN, D), f32)],
        8 * steps * LEN * D * BLOCK,
    )(nm, *ws)
    return hiddens, acc


def mlp_last(nm, ws, part, middle, hot, mod):
    steps = ws[0].shape[1] // (2 * BLOCK)
    hidden = sds((LEN, steps * BLOCK), f32)
    h0, h1, *rest = kernel_call(
        mlp_last_kernel,
        (steps,),
        [whole(LEN, D)]
        + [columns(D, 2 * BLOCK)] * 2
        + [ANYWHERE, ANYWHERE, whole(LEN, 24), whole(ITEMS, D)],
        [columns(LEN, BLOCK)] * 2 + [whole(LEN, D), whole(LEN, D), whole(LEN, D), whole(D, LEN)],
        [
            hidden,
            hidden,
            sds((LEN, D), f32),
            sds((LEN, D), f32),
            sds((LEN, D), bf16),
            sds((D, LEN), bf16),
        ],
        8 * steps * LEN * D * BLOCK,
        held_scratch(2),
    )(nm, *ws, part, middle, hot, mod)
    return [h0, h1], *rest


def mlp_part_back(nm_t_ref, g_ref, g_t_ref, h_refs, w_refs, dw_ref):
    total = 0.0
    for i, (h_ref, w_ref) in enumerate(zip(h_refs, w_refs)):
        hidden = h_ref[...]
        cdf, active = gelu_parts(hidden)
        at = 2 * i * BLOCK
        dw_ref[:, at + BLOCK : at + 2 * BLOCK] = matmul(g_t_ref[...], active.astype(bf16)).astype(bf16)
        grad_pre = (gelu_slope(hidden, cdf) * matmul(g_ref[...], w_ref[:, BLOCK:])).astype(bf16)
        dw_ref[:, at : at + BLOCK] = matmul(nm_t_ref[...], grad_pre).astype(bf16)
        total = total + matmul_nt(grad_pre, w_ref[:, :BLOCK])
    return total


def mlp_back_first_kernel(nm_t_ref, g_ref, g_t_ref, h0_ref, h1_ref, w0_ref, w1_ref, dw_ref, acc_ref):
    add_up(acc_ref, mlp_part_back(nm_t_ref, g_ref, g_t_ref, (h0_ref, h1_ref), (w0_ref, w1_ref), dw_ref))


def mlp_back_last_kernel(
    nm_t_ref, g_ref, g_t_ref, h0_ref, h1_ref, w0_ref, w1_ref,
    part_ref, mid_ref, gr_ref, out_ref, hot_ref, hot_t_ref, mod_ref,
    dw_ref, gm_ref, go_ref, go_t_ref, items_ref, acc_ref, held, sems,
):
    arrive = held_back([part_ref, mid_ref, out_ref, gr_ref], held, sems, [gm_ref])
    add_up(acc_ref, mlp_part_back(nm_t_ref, g_ref, g_t_ref, (h0_ref, h1_ref), (w0_ref, w1_ref), dw_ref))

    @at_end
    def _():
        arrive()
        grad = acc_ref[...] + held[0]
        hat, factor = normed(held[1])
        items_ref[:, D : 2 * D] = item_sum(hot_t_ref[...], grad * hat)
        items_ref[:, 2 * D :] = item_sum(hot_t_ref[...], grad)
        grad_middle = gm_ref[...] + normed_back(
            hat, factor, grad * (1.0 + spread(hot_ref[...], mod_ref[:, D:]))
        )
        gm_ref[...] = grad_middle
        items_ref[:, :D] = item_sum(hot_t_ref[...], grad_middle * held[2])
        grad_out = spread(hot_ref[...], mod_ref[:, :D]) * grad_middle
        go_ref[...] = grad_out.astype(bf16)
        go_t_ref[...] = flip(grad_out)


def mlp_back_specs():
    return (
        [whole(D, LEN), whole(LEN, D), whole(D, LEN)]
        + [columns(LEN, BLOCK)] * 2
        + [columns(D, 2 * BLOCK)] * 2
    )


def mlp_back_first(nm_t, g, g_t, hiddens, ws):
    steps = ws[0].shape[1] // (2 * BLOCK)
    return kernel_call(
        mlp_back_first_kernel,
        (steps,),
        mlp_back_specs(),
        [columns(D, 4 * BLOCK), whole(LEN, D)],
        [sds((D, 4 * steps * BLOCK), bf16), sds((LEN, D), f32)],
        16 * steps * LEN * D * BLOCK,
    )(nm_t, g, g_t, *hiddens, *ws)


def mlp_back_last(nm_t, g, g_t, hiddens, ws, part, middle, grad_res, attn_out, hot, hot_t, mod):
    steps = ws[0].shape[1] // (2 * BLOCK)
    return kernel_call(
        mlp_back_last_kernel,
        (steps,),
        mlp_back_specs()
        + [ANYWHERE] * 4
        + [whole(LEN, 24), whole(2 * ITEMS, LEN), whole(ITEMS, 2 * D)],
        [
            columns(D, 4 * BLOCK),
            whole(LEN, D),
            whole(LEN, D),
            whole(D, LEN),
            whole(2 * ITEMS, 3 * D),
        ],
        [
            sds((D, 4 * steps * BLOCK), bf16),
            sds((LEN, D), f32),
            sds((LEN, D), bf16),
            sds((D, LEN), bf16),
            sds((2 * ITEMS, 3 * D), f32),
        ],
        16 * steps * LEN * D * BLOCK,
        [pltpu.VMEM((LEN, D), f32)] + held_scratch(3, 4),
    )(nm_t, g, g_t, *hiddens, *ws, part, middle, grad_res, attn_out, hot, hot_t, mod)


def head_kernel(
    nh_ref, nh_t_ref, own_ref, peer_ref, target_ref, weight_ref, res_ref, mlp_ref, hot_ref, hot_t_ref, mod_ref,
    dw_own_ref, dw_peer_ref, loss_ref, gr_ref, gmo_ref, gmo_t_ref, items_ref,
    logits, most, total, chosen, acc, held, sems,
):
    arrive = held_back([res_ref, mlp_ref], held, sems)
    step = pl.program_id(0)
    half = pl.num_programs(0) // 2
    block = own_ref.shape[1]
    lane = lax.broadcasted_iota(jnp.int32, (LEN, block), 1)

    @pl.when(step == 0)
    def _():
        most[...] = jnp.full((LEN, 1), -1e30, f32)
        total[...] = jnp.zeros((LEN, 1), f32)
        chosen[...] = jnp.zeros((LEN, 1), f32)

    for which, w_ref, dw_ref in ((0, own_ref, dw_own_ref), (1, peer_ref, dw_peer_ref)):

        @pl.when(step < half)
        def _():
            place = step + which * half
            values = matmul(nh_ref[...], w_ref[...])
            logits[place] = values
            most_new = jnp.maximum(most[...], jnp.max(values, axis=1, keepdims=True))
            total[...] = total[...] * jnp.exp(most[...] - most_new) + jnp.sum(
                jnp.exp(values - most_new), axis=1, keepdims=True
            )
            most[...] = most_new
            is_target = lane + place * block == target_ref[...]
            chosen[...] += jnp.sum(jnp.where(is_target, values, 0.0), axis=1, keepdims=True)

    @pl.when(step == half - 1)
    def _():
        most[...] = most[...] + jnp.log(total[...])
        loss = jnp.sum(weight_ref[...] * (most[...] - chosen[...]), axis=0, keepdims=True)
        loss_ref[...] = jnp.broadcast_to(loss, (8, 128))

    for which, w_ref, dw_ref in ((0, own_ref, dw_own_ref), (1, peer_ref, dw_peer_ref)):

        @pl.when(step >= half)
        def _():
            place = step - half + which * half
            is_target = lane + place * block == target_ref[...]
            grad = (jnp.exp(logits[place] - most[...]) - is_target.astype(f32)) * weight_ref[...]
            grad = grad.astype(bf16)
            dw_ref[...] = matmul(nh_t_ref[...], grad).astype(bf16)
            part = matmul_nt(grad, w_ref[...])

            @pl.when(jnp.logical_and(step == half, which == 0))
            def _():
                acc[...] = part

            @pl.when(jnp.logical_not(jnp.logical_and(step == half, which == 0)))
            def _():
                acc[...] += part

    @at_end
    def _():
        arrive()
        hat, factor = normed(held[0])
        grad_res = normed_back(hat, factor, acc[...])
        gr_ref[...] = grad_res
        items_ref[...] = item_sum(hot_t_ref[...], grad_res * held[1])
        grad_mlp = spread(hot_ref[...], mod_ref[...]) * grad_res
        gmo_ref[...] = grad_mlp.astype(bf16)
        gmo_t_ref[...] = flip(grad_mlp)


def head(nh, nh_t, own, peer, target, weight, residual, mlp_out, hot, hot_t, mod):
    half = own.shape[1] // BLOCK
    w_spec = pl.BlockSpec((D, BLOCK), lambda i: (0, i % half))
    dw_spec = pl.BlockSpec((D, BLOCK), lambda i: (0, jnp.maximum(i - half, 0)))
    return kernel_call(
        head_kernel,
        (2 * half,),
        [
            whole(LEN, D),
            whole(D, LEN),
            w_spec,
            w_spec,
            whole(LEN, 1),
            whole(LEN, 1),
            ANYWHERE,
            ANYWHERE,
            whole(LEN, 24),
            whole(2 * ITEMS, LEN),
            whole(ITEMS, D),
        ],
        [
            dw_spec,
            dw_spec,
            whole(8, 128),
            whole(LEN, D),
            whole(LEN, D),
            whole(D, LEN),
            whole(2 * ITEMS, D),
        ],
        [
            sds(own.shape, bf16),
            sds(own.shape, bf16),
            sds((8, 128), f32),
            sds((LEN, D), f32),
            sds((LEN, D), bf16),
            sds((D, LEN), bf16),
            sds((2 * ITEMS, D), f32),
        ],
        12 * half * LEN * D * BLOCK,
        [
            pltpu.VMEM((2 * half, LEN, BLOCK), f32),
            pltpu.VMEM((LEN, 1), f32),
            pltpu.VMEM((LEN, 1), f32),
            pltpu.VMEM((LEN, 1), f32),
            pltpu.VMEM((LEN, D), f32),
            *held_scratch(2),
        ],
    )(nh, nh_t, own, peer, target, weight, residual, mlp_out, hot, hot_t, mod)


def code_first_kernel(code_ref, gt_ref, turn_ref, out_ref, flat_ref):
    step, steps = pl.program_id(0), pl.num_programs(0)
    rows = out_ref.shape[0]

    @pl.when(step == 0)
    def _():
        flat_ref[...] = matmul_nt(gt_ref[...], turn_ref[...]).astype(bf16)

    row = lax.broadcasted_iota(jnp.int32, (rows, LEN), 0) + (step + steps) * rows
    out_ref[...] = matmul((row == code_ref[...]).astype(bf16), flat_ref[...]).astype(bf16)


def code_last_kernel(code_ref, flat_ref, out_ref):
    rows = out_ref.shape[0]
    row = lax.broadcasted_iota(jnp.int32, (rows, LEN), 0) + pl.program_id(0) * rows
    out_ref[...] = matmul((row == code_ref[...]).astype(bf16), flat_ref[...]).astype(bf16)


def code_back_first(code_rows, grad_tokens, turn, rows):
    spec = pl.BlockSpec((rows // 4, D), lambda i: (i, 0))
    out, flat = kernel_call(
        code_first_kernel,
        (4,),
        [whole(1, LEN), whole(LEN, D), whole(D, D)],
        [spec, whole(LEN, D)],
        [sds((rows, D), bf16), sds((LEN, D), bf16)],
        2 * LEN * rows * D,
    )(code_rows, grad_tokens, turn)
    return code_rows, flat, out


def code_back_last(code_rows, flat, rows):
    spec = pl.BlockSpec((rows // 4, D), lambda i: (i, 0))
    return kernel_call(
        code_last_kernel,
        (4,),
        [whole(1, LEN), whole(LEN, D)],
        spec,
        sds((rows, D), bf16),
        2 * LEN * rows * D,
    )(code_rows, flat)


def step_rates():
    return (
        2.5,
        2.5,
        2.5 / math.sqrt(D),
        2.5 / math.sqrt(D),
        2.5 / math.sqrt(D // 32),
        2.5 / math.sqrt(D),
        2.5 / math.sqrt(FF),
        5.0 / math.sqrt(D),
    )


def adamw_update(weight, grad, moment, square, rate):
    first = BETA_ONE * moment + (1.0 - BETA_ONE) * grad
    second = BETA_TWO * square + (1.0 - BETA_TWO) * grad * grad
    corrected = (
        first / (1.0 - BETA_ONE**STEP) / (jnp.sqrt(second / (1.0 - BETA_TWO**STEP)) + ADAM_EPSILON)
    )
    return (first, second, weight - rate * (corrected + DECAY * weight))


def on_device(
    input_codes,
    target_codes,
    item_lengths,
    item_labels,
    code_table,
    class_table,
    adaln_weight,
    qkv_weight,
    proj_weight,
    expand_weight,
    contract_weight,
    head_weight,
    code_moment,
    class_moment,
    adaln_moment,
    qkv_moment,
    proj_moment,
    expand_moment,
    contract_moment,
    head_moment,
    code_square,
    class_square,
    adaln_square,
    qkv_square,
    proj_square,
    expand_square,
    contract_square,
    head_square,
):
    masters = (
        code_table,
        class_table,
        adaln_weight,
        qkv_weight,
        proj_weight.T,
        expand_weight,
        contract_weight.T,
        head_weight,
    )
    moments = (
        code_moment,
        class_moment,
        adaln_moment,
        qkv_moment,
        proj_moment.T,
        expand_moment,
        contract_moment.T,
        head_moment,
    )
    squares = (
        code_square,
        class_square,
        adaln_square,
        qkv_square,
        proj_square.T,
        expand_square,
        contract_square.T,
        head_square,
    )
    n = lax.axis_size("dp")
    core = lax.axis_index("mp")
    rows = code_table.shape[0]
    half_rows = rows // 2
    width = proj_weight.shape[0]
    wide = expand_weight.shape[1]
    codes_local = head_weight.shape[1]

    def mine(values):
        return lax.dynamic_index_in_dim(values, core, 0, keepdims=False)

    pairs = width // PAIR
    code_block = lax.dynamic_slice_in_dim(code_table, core * half_rows, half_rows, 0).astype(bf16)
    attn_block = jnp.stack([qkv_weight[0], qkv_weight[1], qkv_weight[2], proj_weight.T], axis=1)
    attn_block = attn_block.reshape(-1, 4, pairs, PAIR).swapaxes(1, 2).reshape(-1, 4 * width)
    blocks = wide // BLOCK
    mlp_blocks = jnp.stack(
        [expand_weight.reshape(-1, blocks, BLOCK), contract_weight.T.reshape(-1, blocks, BLOCK)], axis=2
    ).astype(bf16)
    code_w, attn_w, mlp_a, mlp_b, head_w = [
        Gather(block, behind)
        for block, behind in (
            (code_block, False),
            (attn_block.astype(bf16), False),
            (mlp_blocks[:, 0::2].reshape(-1, wide), True),
            (mlp_blocks[:, 1::2].reshape(-1, wide), True),
            (head_weight.astype(bf16), True),
        )
    ]
    begin = Ticks()
    begin([code_w])
    numbers = small_gather(jnp.stack([item_lengths[:, 0], item_labels[:, 0]], axis=1))
    positions = jnp.arange(n, dtype=jnp.int32)
    block_at = ((lax.axis_index("dp") & 3) ^ (positions // quarter())) + 4 * (positions % quarter())
    block_place = place_of(positions)
    labels = numbers[:, :, 1]
    labels_own = jnp.where(core == 0, labels[:, 0], labels[:, 1])
    labels_peer = jnp.where(core == 0, labels[:, 1], labels[:, 0])
    class_low = class_table.astype(bf16)
    adaln_low = adaln_weight.astype(bf16)

    def class_part(item_labels):
        ids = jnp.arange(CLASSES, dtype=jnp.int32)
        picked = (item_labels.reshape(-1, 1) == ids[None, :]).astype(bf16)
        class_rows = matmul(picked, class_low)
        return picked, class_rows, jax.nn.silu(class_rows).astype(bf16)

    _, _, class_vec = class_part(labels_own[block_at])
    order = (2, 4, 0, 1, 3, 5)
    adaln_parts = jnp.concatenate([adaln_low[:, i * D : (i + 1) * D] for i in order], axis=1)

    mod_parts = matmul(class_vec, adaln_parts)

    mod_job = Scatter(None, mod_parts, dtype=f32)
    attn_w.block, mod_job.own = begin.wait((attn_w.block, mod_job.own))
    begin([code_w, attn_w, mod_job, mlp_a])
    begin.wait()
    lengths = mine(item_lengths)[0]
    code_ids = mine(input_codes)[0]
    target_ids = mine(target_codes)[0]
    segment, scale_id, usable = layout(lengths)
    bounds = jnp.array((0,) + PYRAMID, dtype=jnp.int32)
    sizes = jnp.array(PYRAMID + (LEN,), dtype=jnp.int32) - bounds
    all_lengths = numbers[:, :, 0].reshape(-1)
    scale_counts = jnp.sum(
        jnp.clip(all_lengths[:, None] - bounds[None, :], 0, sizes[None, :]), axis=0
    ).astype(f32)
    inv_counts = 1.0 / (NSCALES * jnp.maximum(scale_counts, 1.0))
    scale_hot = scale_id[:, None] == jnp.arange(NSCALES, dtype=jnp.int32)[None, :]
    token_weight = jnp.where(
        usable, jnp.sum(jnp.where(scale_hot, inv_counts[None, :], 0.0), axis=1), 0.0
    )
    same = segment[:, None] == segment[None, :]
    bias = jnp.where(same & (scale_id[None, :] <= scale_id[:, None]), 0.0, -1e30)
    bias_t = jnp.where(same & (scale_id[:, None] <= scale_id[None, :]), 0.0, -1e30)
    hot = (segment[:, None] == jnp.arange(3 * ITEMS, dtype=jnp.int32)[None, :] % ITEMS).astype(bf16)
    item_rows = jnp.arange(2 * ITEMS, dtype=jnp.int32)
    hot_t = ((segment[None, :] == item_rows[:, None]) & (item_rows[:, None] < ITEMS)).astype(bf16)

    block_width = D // n
    feature_place = (block_place[:, None] * block_width + jnp.arange(block_width)[None, :]).reshape(-1)
    turn = (feature_place[:, None] == jnp.arange(D, dtype=jnp.int32)[None, :]).astype(bf16)
    within = code_ids % rows
    other = (within // half_rows != core).astype(jnp.int32)
    code_rows = other * (n * half_rows) + place_of(code_ids // rows) * half_rows + within % half_rows
    target = jnp.where(target_ids // codes_local == core, 0, codes_local) + target_ids % codes_local

    begin([code_w, mod_job])
    mlp_a.group, bias, bias_t, turn, hot, hot_t, code_rows, target, token_weight = begin.wait(
        (mlp_a.group, bias, bias_t, turn, hot, hot_t, code_rows, target, token_weight)
    )
    begin([code_w, attn_w, mlp_b, mod_job])
    begin.wait()

    def placed(values):
        values = values.reshape(-1, n, block_width)
        return jnp.take(values, block_at, axis=1).reshape(ITEMS, -1)

    def beside(*parts):
        return jnp.concatenate(parts, axis=1)

    mods_embed = placed(mod_job.total[:, : 2 * D])
    scale_attn = mods_embed[:, :D]
    code_col = code_rows.reshape(LEN, 1)

    code_own, code_peer, code_col = begin(
        [attn_w, mlp_a, head_w], (code_w.own, code_w.peer, code_col)
    )
    tokens, na, na_t = begin.wait(embed(code_col, code_own, code_peer, turn, hot, mods_embed))
    na = begin([attn_w, mlp_a, mlp_b], na)
    att_own, part = begin.wait(attend_first(na, attn_w.own, bias))
    mods = placed(mod_job.total[:, 2 * D :])
    gate_attn, gate_mlp, scale_mlp, shift_mlp = jnp.split(mods, 4, axis=1)
    mods_attend = beside(gate_attn, scale_mlp, shift_mlp)
    mods_back = beside(gate_attn, scale_mlp)
    part = begin([mlp_a, mlp_b, head_w], part)
    att_peer, attn_out, middle, nm, nm_t = begin.wait(
        attend_last(na, attn_w.peer, bias, part, tokens, hot, mods_attend)
    )
    nm = begin([mlp_b, head_w], nm)
    mlp_own = (mlp_a.own, mlp_b.own)
    hidden_own, part = begin.wait(mlp_first(nm, mlp_own))
    mlp_peer = (mlp_a.peer, mlp_b.peer)
    part = begin([head_w], part)
    hidden_peer, mlp_out, residual, nh, nh_t = begin.wait(
        mlp_last(nm, mlp_peer, part, middle, hot, gate_mlp)
    )
    dhead_own, dhead_peer, loss_tile, grad_res, gmo, gmo_t, items_head = head(
        nh, nh_t, head_w.own, head_w.peer, target.reshape(LEN, 1), token_weight.reshape(LEN, 1),
        residual, mlp_out, hot, hot_t, gate_mlp,
    )
    loss_local = loss_tile[0, 0]

    def turned(parts):
        values = beside(*parts)
        values = jnp.take(values.reshape(-1, n, block_width), block_place, axis=1)
        return values.reshape(ITEMS, -1).astype(bf16)

    head_job = Scatter(dhead_peer, dhead_own, behind=True, wide=True)
    gmo = begin([head_job], gmo)
    dmlp_peer, part = begin.wait(mlp_back_first(nm_t, gmo, gmo_t, hidden_peer, mlp_peer))
    mlp_job = Scatter(dmlp_peer, behind=True)
    part = begin([head_job, mlp_job], part)
    mlp_job.own, grad_middle, gao, gao_t, items_mlp = begin.wait(
        mlp_back_last(
            nm_t, gmo, gmo_t, hidden_own, mlp_own, part, middle, grad_res, attn_out, hot, hot_t, mods_back
        )
    )
    item_job = Exchange(turned([items_mlp[:ITEMS, :D], items_head[:ITEMS], items_mlp[:ITEMS, D:]]), behind=True)
    gao = begin([head_job, mlp_job, item_job], gao)
    dattn_peer, part = begin.wait(attend_back_first(na, na_t, gao, gao_t, att_peer, attn_w.peer, bias_t))
    attn_job = Scatter(dattn_peer, behind=True)
    part = begin([head_job, mlp_job, attn_job], part)
    attn_job.own, grad_tokens, items_attn = begin.wait(
        attend_back_last(
            na, na_t, gao, gao_t, att_own, attn_w.own, bias_t, part, tokens, grad_middle, hot, hot_t, scale_attn
        )
    )
    late_job = Exchange(turned([items_attn[:ITEMS]]))
    grad_tokens = begin([attn_job, late_job], grad_tokens)
    code_row, flat, dcode_peer = begin.wait(
        code_back_first(code_rows.reshape(1, LEN), grad_tokens, turn, n * half_rows)
    )
    code_job = Scatter(dcode_peer)
    flat = begin([code_job, attn_job], flat)
    mlp_job.send(mlp_job.request())
    code_job.own = begin.wait(code_back_last(code_row, flat, n * half_rows))
    begin([code_job, item_job, late_job, attn_job])
    begin.wait()
    begin([code_job])
    begin.wait()
    head_job.total, mlp_job.total = begin([code_job], (head_job.total, mlp_job.total))
    begin.wait()

    def factor_part(item_labels, grads):
        picked, class_rows, class_vec = class_part(item_labels)
        grad_class_vec = matmul_nt(grads, adaln_low)
        _, silu_back = jax.vjp(jax.nn.silu, class_rows)
        return matmul_tn(class_vec, grads), exact_tn(picked.astype(f32), silu_back(grad_class_vec)[0])

    def grad_rows(which):
        early, late = getattr(item_job, which), getattr(late_job, which)
        order = [early[:, : 2 * D], late[:, :D], early[:, 2 * D : 3 * D], late[:, D:], early[:, 3 * D :]]
        return beside(*order)

    adaln_a, class_a = factor_part(labels_own, grad_rows("own"))
    adaln_b, class_b = factor_part(labels_peer, grad_rows("peer"))
    adaln_grad = adaln_a + adaln_b
    class_grad = class_a + class_b
    code_half = code_job.result()
    code_other = swap_core(code_half)
    code_grad = jnp.where(
        core == 0,
        jnp.concatenate([code_half, code_other]),
        jnp.concatenate([code_other, code_half]),
    )
    attn_grad = attn_job.result()
    kinds = attn_grad.reshape(-1, pairs, 4, PAIR).transpose(2, 0, 1, 3).reshape(4, -1, width)
    mlp_kinds = mlp_job.result().reshape(-1, blocks, 2, BLOCK)
    gradients = (
        code_grad,
        class_grad,
        adaln_grad,
        kinds[:3],
        kinds[3],
        mlp_kinds[:, :, 0].reshape(-1, wide),
        mlp_kinds[:, :, 1].reshape(-1, wide),
        head_job.result(),
    )
    shared_sq = jnp.sum(class_grad * class_grad) + jnp.sum(adaln_grad * adaln_grad)
    own_sq = jnp.sum(code_half * code_half) + jnp.sum(attn_grad * attn_grad)
    for grad in gradients[5:]:
        own_sq = own_sq + jnp.sum(grad * grad)
    totals = total_over_all(
        jnp.concatenate([(own_sq + 0.5 * shared_sq).reshape(1), loss_local.reshape(1)])
    )
    squared, loss = totals[0], totals[1]
    grad_norm = jnp.sqrt(squared)
    clip = jnp.minimum(1.0, CLIP_NORM / (grad_norm + 1e-06))
    firsts, seconds, updated = ([], [], [])
    for place, (weight, grad, moment, square, rate) in enumerate(
        zip(masters, gradients, moments, squares, step_rates())
    ):
        for kept, value in zip(
            (firsts, seconds, updated), adamw_update(weight, grad * clip, moment, square, rate)
        ):
            kept.append(value.T if place in (4, 6) else value)
    return (*firsts, *seconds, *updated, loss, scale_counts, grad_norm)


def solution(mesh):
    token_spec = P(None, "dp", None)
    weight_specs = (
        P("dp", None),
        P(None, "dp"),
        P("dp", None),
        P(None, "dp", "mp"),
        P("mp", "dp"),
        P("dp", "mp"),
        P("mp", "dp"),
        P("dp", "mp"),
    )
    return jax.shard_map(
        on_device,
        mesh=mesh,
        in_specs=(token_spec,) * 4 + weight_specs * 3,
        out_specs=weight_specs * 3 + (P(), P(), P()),
        check_vma=False,
    )
```
